32 devices in a mesh: seq: 4 (over y, x), batch: 8 (over z, core).
Axes of the slice: x: 2, y: 2, z: 4, core: 2. Of those that a mesh axis runs over, the one named last changes fastest.
Arguments:
- inputs: bfloat16 [8, 2048, 768], P('batch', 'seq'), may hold values from -6 to 6
- doc_ids: int32 [8, 2048], P('batch'), may hold values from 0 to 6, as said below
- w_qkv: bfloat16 [768, 896], replicated, may hold values from -0.3125 to 0.3125
- b_qkv: float32 [896], replicated, may hold values from -3 to 3
- w_o: bfloat16 [768, 768], replicated, may hold values from -0.875 to 0.875
- w_fc: bfloat16 [768, 3072], replicated, may hold values from -0.21875 to 0.21875
- b_fc: float32 [3072], replicated, may hold values from -3 to 3
- w_proj: bfloat16 [3072, 768], replicated, may hold values from -0.109375 to 0.109375
- b_proj: float32 [768], replicated, may hold values from -3 to 3
- gain_one: float32 [768], replicated, may hold values from 0.1 to 1.9
- shift_one: float32 [768], replicated, may hold values from -1.75 to 1.75
- gain_two: float32 [768], replicated, may hold values from 0.1 to 1.9
- shift_two: float32 [768], replicated, may hold values from -1.75 to 1.75
- cotangent: bfloat16 [8, 2048, 768], P('batch', 'seq'), may hold values from -6 to 6
Outputs:
- outputs: bfloat16 [8, 2048, 768], P('batch', 'seq')
- input_grads: bfloat16 [8, 2048, 768], P('batch', 'seq')
- grad_w_qkv: float32 [768, 896], P('batch')
- grad_b_qkv: float32 [896], P('batch')
- grad_w_o: float32 [768, 768], P('batch')
- grad_w_fc: float32 [768, 3072], P('batch')
- grad_b_fc: float32 [3072], P('batch')
- grad_w_proj: float32 [3072, 768], P('batch')
- grad_b_proj: float32 [768], P('batch')
- grad_gain_one: float32 [768], P('batch')
- grad_shift_one: float32 [768], P('batch')
- grad_gain_two: float32 [768], P('batch')
- grad_shift_two: float32 [768], P('batch')
The draws below stay inside these ranges and needn't reach their ends.
Inputs may be any that keep to these rules, and one draw needn't show every extreme that they name: `doc_ids`: along each row the ids never fall; in every row one document begins within the first 512 positions and ends within the last 512.
All inputs are finite; a program needn't handle non-finite values.
Results may differ from the reference program's by a relative error of at most 0.017.
Values may be sent and summed in bfloat16 or wider, within the bound.
A program may use at most 320 MiB of HBM per device.

```python
import math
import jax
import jax.numpy as jnp
from jax import lax

D = 768
HEAD = 64
ROT = 16
FF = 3072
SPAN = 512
CUTS = 6
QKV = 896
ROWS = 8
SEQ_LEN = 2048


def draw_doc_ids(key, part):
    key = jax.random.fold_in(key, 11)
    keys = jax.random.split(key, 4)
    start = jax.random.randint(keys[0], (ROWS, 1), 1, SPAN)
    finish = jax.random.randint(keys[1], (ROWS, 1), SEQ_LEN - SPAN + 1, SEQ_LEN)
    cuts = jax.random.randint(keys[2], (ROWS, CUTS), 1, SEQ_LEN)
    sides = jax.random.randint(keys[3], (ROWS, CUTS), 0, 2)
    inside = (cuts > start) & (cuts < finish)
    moved = jnp.where(sides == 1, start, finish)
    cuts = jnp.where(inside, moved, cuts)
    places = jnp.arange(SEQ_LEN, dtype=jnp.int32)
    return jnp.sum((places[None, :, None] >= cuts[:, None, :]).astype(jnp.int32), axis=-1)


def level_of(rng, shape, cuts, low, top_value):
    def one(axis_at, shards_of):
        draws = jax.random.uniform(jax.random.fold_in(jax.random.fold_in(rng, 6), axis_at), (shards_of,), jnp.float32, low / len(cuts), top_value / len(cuts))
        return jnp.repeat(jnp.exp(draws), shape[axis_at] // shards_of).reshape((-1,) + (1,) * (len(shape) - axis_at - 1))

    factor_of = one(*cuts[0])
    for cut in cuts[1:]:
        factor_of = factor_of * one(*cut)
    return factor_of


def scatter_about(own_key, shape, scale, limit, shards=(), kind=jnp.bfloat16):
    factor_of = level_of(own_key, shape, shards, -0.22, 0.18) if shards else 1.0
    entries = jax.random.normal(own_key, shape, jnp.float32) * scale * factor_of
    return jnp.minimum(jnp.maximum(entries, -limit), limit).astype(kind)


def setup_inputs(seed: int = 0) -> dict:
    streams_of = jax.random.split(jax.random.key(seed), 15)
    return {
        "inputs": scatter_about(streams_of[0], (ROWS, SEQ_LEN, D), 1.0, 6.0, ((0, 8), (1, 4))),
        "doc_ids": draw_doc_ids(jax.random.fold_in(streams_of[14], 71), 0),
        "w_qkv": scatter_about(streams_of[2], (D, QKV), (D // 2) ** -0.5, 0.3125),
        "b_qkv": scatter_about(streams_of[3], (QKV,), 0.5, 3.0, (), jnp.float32),
        "w_o": scatter_about(streams_of[4], (D, D), (D // 16) ** -0.5, 0.875),
        "w_fc": scatter_about(streams_of[5], (D, FF), D ** -0.5, 0.21875),
        "b_fc": scatter_about(streams_of[6], (FF,), 0.5, 3.0, (), jnp.float32),
        "w_proj": scatter_about(streams_of[7], (FF, D), FF ** -0.5, 0.109375),
        "b_proj": scatter_about(streams_of[8], (D,), 0.5, 3.0, (), jnp.float32),
        "gain_one": jnp.clip(1.0 + 0.18 * jax.random.normal(streams_of[9], (D,), jnp.float32), 0.1, 1.9),
        "shift_one": scatter_about(streams_of[10], (D,), 0.3, 1.75, (), jnp.float32),
        "gain_two": jnp.clip(1.0 + 0.18 * jax.random.normal(streams_of[11], (D,), jnp.float32), 0.1, 1.9),
        "shift_two": scatter_about(streams_of[12], (D,), 0.3, 1.75, (), jnp.float32),
        "cotangent": scatter_about(streams_of[13], (ROWS, SEQ_LEN, D), 1.0, 6.0, ((0, 8), (1, 4))),
    }


@jax.custom_vjp
def low(v):
    return lax.optimization_barrier(v.astype(jnp.bfloat16)).astype(jnp.float32)

@jax.custom_vjp
def low_back(v):
    return v

def low_keep(v):
    return (low(v), None)

def low_pass(kept, grad):
    return (grad,)

def back_keep(v):
    return (v, None)

def back_low(kept, grad):
    return (low(grad),)
low.defvjp(low_keep, low_pass)
low_back.defvjp(back_keep, back_low)

def matmul(left, right):
    return jnp.dot(left, right, precision=lax.Precision.HIGHEST)

def layer_norm(tokens, gain, shift):
    average = lax.optimization_barrier(jnp.mean(tokens, axis=-1, keepdims=True))
    centered = tokens - average
    variance = lax.optimization_barrier(jnp.mean(centered * centered, axis=-1, keepdims=True))
    return centered * lax.rsqrt(variance + 1e-05) * gain + shift

def rotate(values, cosine, sine):
    half = ROT // 2
    first = values[..., :half]
    second = values[..., half:ROT]
    return jnp.concatenate([first * cosine - second * sine, second * cosine + first * sine, values[..., ROT:]], axis=-1)

def row_forward(tokens, doc_row, w_qkv, b_qkv, w_o, w_fc, b_fc, w_proj, b_proj, gain_one, shift_one, gain_two, shift_two):
    length = tokens.shape[0]
    heads = D // HEAD
    normed_one = layer_norm(tokens, gain_one, shift_one)
    normed_two = layer_norm(tokens, gain_two, shift_two)
    project = low_back(matmul(low(normed_one), w_qkv) + b_qkv)
    queries = project[:, :heads * HEAD].reshape(length, heads, HEAD)
    keys = project[:, heads * HEAD:(heads + 1) * HEAD]
    values = project[:, (heads + 1) * HEAD:]
    places = jnp.arange(length, dtype=jnp.float32)
    frequency = 10000.0 ** (-jnp.arange(ROT // 2, dtype=jnp.float32) * 2.0 / ROT)
    angles = places[:, None] * frequency[None, :]
    cosine = jnp.cos(angles)
    sine = jnp.sin(angles)
    queries = low(rotate(queries, cosine[:, None, :], sine[:, None, :]))
    keys = low(rotate(keys, cosine, sine))
    values = low(values)
    scale = 1.0 / math.sqrt(HEAD)
    scores = low_back(jnp.einsum('qhd,kd->hqk', queries, keys, precision=lax.Precision.HIGHEST) * scale)
    positions = jnp.arange(length, dtype=jnp.int32)
    allowed = (positions[None, :] <= positions[:, None]) & (doc_row[None, :] == doc_row[:, None])
    scores = jnp.where(allowed[None], scores, -jnp.inf)
    probs = jax.nn.softmax(scores, axis=-1)
    attended = jnp.einsum('hqk,kd->qhd', low(probs), values, precision=lax.Precision.HIGHEST).reshape(length, D)
    attended = low(low_back(attended))
    hidden = low_back(matmul(low(normed_two), w_fc) + b_fc)
    act = low(jax.nn.gelu(hidden, approximate=False))
    return tokens + matmul(attended, w_o) + matmul(act, w_proj) + b_proj

def reference(inputs, doc_ids, w_qkv, b_qkv, w_o, w_fc, b_fc, w_proj, b_proj, gain_one, shift_one, gain_two, shift_two, cotangent):
    params = tuple((item.astype(jnp.float32) for item in (w_qkv, b_qkv, w_o, w_fc, b_fc, w_proj, b_proj, gain_one, shift_one, gain_two, shift_two)))

    def one_row(totals, row):
        tokens, doc_row, grad_out = row

        def forward(token_values, *weights):
            return row_forward(token_values, doc_row, *weights)
        result, pullback = jax.vjp(forward, tokens.astype(jnp.float32), *params)
        grads = pullback(grad_out.astype(jnp.float32))
        totals = tuple((total + grad for total, grad in zip(totals, grads[1:])))
        return (totals, (result.astype(jnp.bfloat16), grads[0].astype(jnp.bfloat16)))
    zeros = tuple((jnp.zeros_like(item) for item in params))
    totals, (outputs, input_grads) = lax.scan(one_row, zeros, (inputs, doc_ids, cotangent))
    return (outputs, input_grads, totals[0], totals[1], totals[2], totals[3], totals[4], totals[5], totals[6], totals[7], totals[8], totals[9], totals[10])
```

```python
import functools
import math
import types

import jax
import jax.numpy as jnp
import numpy as np
from jax import lax
from jax.experimental import pallas as pl
from jax.experimental.pallas import tpu as pltpu
from jax.sharding import PartitionSpec as P

HEAD = 64
ROT = 16
EPSILON = 1e-05
LANES = 128
BLOCK = 256
FAR = -1e30
LOG2E = math.log2(math.e)
MESH = pl.DeviceIdType.MESH
F32 = jnp.float32
BF16 = jnp.bfloat16

CHUNKS = 8


def mm(a, b, ca=1, cb=0):
    return lax.dot_general(a, b, (((ca,), (cb,)), ((), ())), preferred_element_type=F32)


def flip(value):
    return value.astype(F32).T


def lanes_of(shape):
    return lax.broadcasted_iota(jnp.int32, shape, 1)


def rows_of(shape):
    return lax.broadcasted_iota(jnp.int32, shape, 0)


def gelu_parts(hidden):
    size = jnp.abs(hidden)
    t = pl.reciprocal(1.0 + (0.3275911 / math.sqrt(2.0)) * size)
    bell = jnp.exp2(hidden * hidden * (-0.5 * LOG2E))
    poly = 0.5 * 1.061405429
    for term in (-1.453152027, 1.421413741, -0.284496736, 0.254829592):
        poly = poly * t + 0.5 * term
    tail = poly * t * bell
    below = jnp.where(hidden >= 0, 1.0 - tail, tail)
    return below, hidden * bell * (1.0 / math.sqrt(2.0 * math.pi))


def layer_kernel(names, parts, inside, *refs):
    r = types.SimpleNamespace(**dict(zip(names, refs, strict=True)))
    span, width = r.x.shape
    hidden_units = r.wfc.shape[1]
    heads = width // HEAD
    mine = lax.axis_index("seq")
    batch = lax.axis_index("batch")
    core = lax.rem(batch, 2)

    loads = [
        pltpu.make_async_copy(src, dst, r.load_sem.at[i])
        for i, (src, dst) in enumerate(
            [(r.x_h, r.x), (r.wq_h, r.wq), (r.cot_h, r.cot), (r.wo_h, r.wo), (r.wfc_h, r.wfc), (r.wp_h, r.wp)]
        )
    ]
    for load in loads:
        load.start()

    barrier = pltpu.get_barrier_semaphore()
    for distance in range(1, parts):
        pl.semaphore_signal(
            barrier, inc=1, device_id=(lax.rem(mine + distance, parts), batch), device_id_type=MESH
        )
    pl.semaphore_wait(barrier, parts - 1)

    loads[0].wait()

    def norm_tile(i):
        tokens = r.x[pl.ds(i * LANES, LANES), :].astype(F32)
        average = jnp.mean(tokens, axis=-1, keepdims=True)
        centered = tokens - average
        variance = jnp.mean(centered * centered, axis=-1, keepdims=True)
        inverse_std = lax.rsqrt(variance + EPSILON)
        return centered * inverse_std, inverse_std

    for i in range(span // LANES):
        normed, _ = norm_tile(i)
        rows = pl.ds(i * LANES, LANES)
        first = normed * r.g1[...] + r.s1[...]
        second = normed * r.g2[...] + r.s2[...]
        r.fi[rows, :] = first.astype(BF16)
        r.si[rows, :] = second.astype(BF16)
        r.fit[:, rows] = first.T.astype(BF16)
        r.sit[:, rows] = second.T.astype(BF16)

    half = ROT // 2
    index = rows_of((half, span))
    frequency = jnp.zeros((half, span), F32)
    for i in range(half):
        frequency = jnp.where(index == i, np.float32(10000.0 ** (-2.0 * i / ROT)), frequency)
    angle = (mine * span + lanes_of((half, span))).astype(F32) * frequency
    cosine, sine = jnp.cos(angle), jnp.sin(angle)
    r.cos[...] = cosine
    r.sin[...] = sine
    ones = jnp.ones((HEAD - ROT, span), F32)
    zeros = jnp.zeros((HEAD - ROT, span), F32)
    table_cos = jnp.concatenate([cosine, cosine, ones] * 2, axis=0).T
    table_sin = jnp.concatenate([-sine, sine, zeros] * 2, axis=0).T
    lane = lanes_of((span, LANES))

    def rotate(tile, cos_of, sin_of):
        partner = jnp.where(
            lax.rem(lane, HEAD) < half, pltpu.roll(tile, LANES - half, 1), pltpu.roll(tile, half, 1)
        )
        return tile * cos_of + partner * sin_of

    def docs_row(distance):
        part = jnp.maximum(mine - distance, 0)
        return r.docs[0:1, pl.ds(pl.multiple_of(part * span, LANES), span)]

    loads[1].wait()
    key_value = mm(r.fi[...], r.wq[:, width:]) + r.bq[:, width:]
    low = lane < HEAD
    key_value = rotate(key_value, jnp.where(low, table_cos, 1.0), jnp.where(low, table_sin, 0.0))
    r.kv[0] = key_value.astype(BF16)
    for distance in range(1, parts):

        @pl.when(mine + distance < parts)
        def _():
            kv_copy(r, mine, batch, parts, distance).start()

    feature_row = rows_of((LANES, span)) - HEAD
    query_feature = jnp.where(feature_row == docs_row(0), 1.0, 0.0).T
    for i in range(heads // 2):
        columns = slice(i * LANES, (i + 1) * LANES)
        tile = mm(r.fi[...], r.wq[:, columns]) + r.bq[:, columns]
        tile = rotate(tile, table_cos, table_sin) * (LOG2E / math.sqrt(HEAD))
        r.q[2 * i] = jnp.where(low, tile, query_feature).astype(BF16)
        r.q[2 * i + 1] = jnp.where(low, pltpu.roll(tile, HEAD, 1), query_feature).astype(BF16)

    loads[2].wait()
    loads[3].wait()
    for i in range(width // BLOCK):
        rows = slice(i * BLOCK, (i + 1) * BLOCK)
        r.dot[rows, :] = mm(r.wo[rows, :], r.cot[...], 1, 1).astype(BF16)

    loads[4].wait()
    loads[5].wait()
    r.result[...] = jnp.zeros_like(r.result)
    r.second[...] = jnp.zeros_like(r.second)
    ones_rows = jnp.ones((8, span), BF16)
    group = 2 * 4 * 96

    def feed_forward(g, _):
        columns = pl.ds(pl.multiple_of(g * group, LANES), group)
        hidden = mm(r.si[...], r.wfc[:, columns]) + r.bfc[:, columns]
        grad_act = mm(r.cot[...], r.wp[columns, :], 1, 1)
        below, slope = gelu_parts(hidden)
        r.act[...] = (hidden * below).astype(BF16)
        r.gh[...] = (grad_act * (below + slope)).astype(BF16)
        grad_w = mm(r.sit[...], r.gh[...])
        for k in range(group // BLOCK):
            place = g * (group // BLOCK) + k
            for b in range(8):
                r.grads[place // 4, b % 2, lax.rem(place, 4) // 2, lax.rem(place, 2), b // 2] = grad_w[
                    b * 96 : (b + 1) * 96, k * BLOCK : (k + 1) * BLOCK
                ].astype(BF16)
        grad_w = mm(r.act[...], r.cot[...], 0, 0)
        for k in range(3):
            for c in range(2):
                for q in range(4):
                    row = (c * 4 + q) * 96
                    r.grads[3 + k, c, q // 2, q % 2, g] = grad_w[
                        row : row + 96, k * BLOCK : (k + 1) * BLOCK
                    ].astype(BF16)
        r.sum_fc[:, columns] = mm(ones_rows, r.gh[...])
        r.result[...] += mm(r.act[...], r.wp[columns, :])
        r.second[...] += mm(r.gh[...], r.wfc[:, columns], 1, 1)
        return 0

    lax.fori_loop(0, hidden_units // group, feed_forward, 0)

    for distance in range(parts):

        @pl.when(mine >= distance)
        def _():
            if distance:
                kv_copy(r, mine, batch, parts, distance).wait_recv()
            docs = docs_row(distance)
            apart = (feature_row >= 0) & (feature_row < 8) & (feature_row != docs)
            key_feature = jnp.where(apart, FAR, 0.0).T
            pair = r.kv[distance].astype(F32)
            keys = jnp.where(low, pair, key_feature)
            values = jnp.where(low, pltpu.roll(pair, HEAD, 1), jnp.where(lane < HEAD + 2, 1.0, 0.0))
            r.kx[distance] = keys.astype(BF16)
            r.kxt[distance] = keys.T.astype(BF16)
            r.vx[distance] = values.astype(BF16)
            r.vxt[distance] = values.T.astype(BF16)

    r.dk[...] = jnp.zeros_like(r.dk)
    r.dv[...] = jnp.zeros_like(r.dv)

    def one_head(h, _):
        rows = pl.ds(pl.multiple_of(h * HEAD, HEAD), HEAD)

        def scores(distance, causal):
            raw = mm(r.kx[distance], r.q[h], 1, 1)
            if causal:
                raw = jnp.where(rows_of(raw.shape) <= lanes_of(raw.shape), raw, FAR)
            r.scores[distance] = raw
            return jnp.max(raw, axis=0, keepdims=True)

        top = scores(0, True)
        top = lax.fori_loop(1, mine + 1, lambda d, m: jnp.maximum(m, scores(d, False)), top)
        r.att[...] = jnp.zeros_like(r.att)

        def weigh(distance, _):
            raised = jnp.exp2(r.scores[distance] - top).astype(BF16)
            r.raised[distance] = raised
            r.att[...] += mm(r.vxt[distance], raised)
            return 0

        lax.fori_loop(0, mine + 1, weigh, 0)
        inverse = 1.0 / r.att[HEAD : HEAD + 1, :]
        attended = r.att[:HEAD, :] * inverse
        r.attt[rows, :] = attended.astype(BF16)
        grad_att = r.dot[rows, :].astype(F32)
        delta = jnp.sum(grad_att * attended, axis=0, keepdims=True) * -inverse
        delta_high = delta.astype(BF16).astype(F32)
        row = rows_of((HEAD, span))
        extra = jnp.where(row == 0, delta_high, jnp.where(row == 1, delta - delta_high, 0.0))
        grad_att = jnp.concatenate([grad_att * inverse, extra], axis=0)
        r.ga[...] = grad_att.astype(BF16)
        r.gat[...] = grad_att.T.astype(BF16)
        r.dq[...] = jnp.zeros_like(r.dq)

        def back(distance, _):
            grad_probs = mm(r.vx[distance], r.ga[...])
            raised = r.raised[distance]
            grad_scores = (raised.astype(F32) * grad_probs).astype(BF16)
            r.dv[distance] += mm(raised, r.gat[...])
            r.dk[distance] += mm(grad_scores, r.q[h])
            r.dq[...] += mm(r.kxt[distance], grad_scores)
            return 0

        lax.fori_loop(0, mine + 1, back, 0)
        r.gpt[rows, :] = rotate_back(r, r.dq[:HEAD, :] * (1.0 / math.sqrt(HEAD))).astype(BF16)
        return 0

    lax.fori_loop(0, heads, one_head, 0)

    def packed(distance):
        return jnp.where(low, r.dk[distance] * (1.0 / LOG2E), pltpu.roll(r.dv[distance], HEAD, 1))

    for distance in range(1, parts):

        @pl.when(mine >= distance)
        def _():
            r.dkv_out[distance] = packed(distance).astype(BF16)
            dkv_copy(r, mine, batch, parts, distance).start()

    grad_w = mm(r.attt[...], r.cot[...])
    for b in range(8):
        for q in range(4):
            piece = grad_w[b * 96 : (b + 1) * 96, q * 192 : (q + 1) * 192]
            piece = jnp.concatenate([piece, jnp.zeros((96, 64), F32)], axis=1)
            r.grads[6, b % 2, q // 2, q % 2, b // 2] = piece.astype(BF16)

    r.total[...] = packed(0)
    for distance in range(1, parts):

        @pl.when(mine + distance < parts)
        def _():
            dkv_copy(r, mine, batch, parts, distance).wait_recv()
            r.total[...] += r.dkv_in[distance].astype(F32)

    pair = r.total[...].T
    r.gpt[width : width + HEAD, :] = rotate_back(r, pair[:HEAD]).astype(BF16)
    r.gpt[width + HEAD :, :] = pair[HEAD:].astype(BF16)

    grad_w = mm(r.fit[...], r.gpt[...], 1, 1)
    for b in range(8):
        for q in range(4):
            piece = grad_w[b * 96 : (b + 1) * 96, q * BLOCK : min((q + 1) * BLOCK, width + 2 * HEAD)]
            if q == 3:
                piece = jnp.concatenate([piece, jnp.zeros((96, LANES), F32)], axis=1)
            r.grads[7, b % 2, q // 2, q % 2, b // 2] = piece.astype(BF16)
    for i in range((width + 2 * HEAD) // LANES):
        columns = slice(i * LANES, (i + 1) * LANES)
        r.gp[:, columns] = flip(r.gpt[columns, :]).astype(BF16)

    r.first[...] = mm(r.gp[...], r.wq[...], 1, 1)
    sums = [jnp.zeros((1, width), F32) for _ in range(4)]
    for i in range(span // LANES):
        rows = pl.ds(i * LANES, LANES)
        normed, inverse_std = norm_tile(i)
        first, second = r.first[rows, :], r.second[rows, :]
        for j, term in enumerate((normed * first, first, normed * second, second)):
            sums[j] = sums[j] + jnp.sum(term, axis=0, keepdims=True)
        scaled = first * r.g1[...] + second * r.g2[...]
        mean_one = jnp.mean(scaled, axis=-1, keepdims=True)
        mean_two = jnp.mean(scaled * normed, axis=-1, keepdims=True)
        back = inverse_std * (scaled - mean_one - normed * mean_two)
        r.input_grads[rows, :] = (r.cot[rows, :].astype(F32) + back).astype(BF16)

    sum_qkv = mm(ones_rows, r.gpt[...], 1, 1)[0:1]
    sum_proj = mm(ones_rows, r.cot[...])[0:1]
    for b in range(8):
        lines = [cut(sum_qkv, b * 112, 112)]
        lines += [r.sum_fc[0:1, b * 384 + i * LANES : b * 384 + (i + 1) * LANES] for i in range(3)]
        lines += [cut(line, b * 96, 96) for line in (sum_proj, *sums)]
        lines.append(jnp.zeros((16 - len(lines), LANES), F32))
        r.grads[7, b % 2, 1, 1, b // 2, 0:16, LANES:] = jnp.concatenate(lines, axis=0).astype(BF16)

    for i in range(width // LANES):
        columns = slice(i * LANES, (i + 1) * LANES)
        r.fi[:, columns] = flip(r.attt[columns, :]).astype(BF16)
    r.outputs[...] = (r.result[...] + r.x[...].astype(F32) + r.bp[...] + mm(r.fi[...], r.wo[...])).astype(BF16)

    copy = pltpu.make_async_copy(r.grads, r.grads_out, r.load_sem.at[0])
    copy.start()
    copy.wait()
    for distance in range(1, parts):

        @pl.when(mine + distance < parts)
        def _():
            kv_copy(r, mine, batch, parts, distance).wait_send()

        @pl.when(mine >= distance)
        def _():
            dkv_copy(r, mine, batch, parts, distance).wait_send()


def cut(line, start, size):
    line = jnp.concatenate([line, jnp.zeros((1, LANES), F32)], axis=1)
    base = start // LANES * LANES
    line = line[:, base : base + 2 * LANES]
    shift = start - base
    if shift:
        line = pltpu.roll(line, 2 * LANES - shift, 1)
    return jnp.where(lanes_of((1, LANES)) < size, line[:, :LANES], 0.0)


def rotate_back(r, grads):
    half = ROT // 2
    one, two = grads[:half], grads[half:ROT]
    cosine, sine = r.cos[...], r.sin[...]
    return jnp.concatenate([one * cosine + two * sine, two * cosine - one * sine, grads[ROT:]], axis=0)


def kv_copy(r, mine, batch, parts, distance):
    return pltpu.make_async_remote_copy(
        src_ref=r.kv.at[0],
        dst_ref=r.kv.at[distance],
        send_sem=r.kv_sem.at[0, distance],
        recv_sem=r.kv_sem.at[1, distance],
        device_id=(lax.rem(mine + distance, parts), batch),
        device_id_type=MESH,
    )


def dkv_copy(r, mine, batch, parts, distance):
    return pltpu.make_async_remote_copy(
        src_ref=r.dkv_out.at[distance],
        dst_ref=r.dkv_in.at[distance],
        send_sem=r.dkv_sem.at[0, distance],
        recv_sem=r.dkv_sem.at[1, distance],
        device_id=(lax.rem(mine - distance + parts, parts), batch),
        device_id_type=MESH,
    )


def per_device(inputs, doc_ids, w_qkv, b_qkv, w_o, w_fc, b_fc, w_proj, b_proj, gain_one, shift_one, gain_two, shift_two, cotangent):
    rows_here, span, width = inputs.shape
    assert rows_here == 1
    parts = lax.axis_size("seq")
    heads = width // HEAD
    hidden_units = w_fc.shape[1]
    merged = width + 2 * HEAD
    inside = False
    vmem = pl.BlockSpec(memory_space=pltpu.VMEM)
    anywhere = pl.BlockSpec(memory_space=pl.ANY)

    small = dict(docs=doc_ids, bq=b_qkv, bfc=b_fc, bp=b_proj, g1=gain_one, s1=shift_one, g2=gain_two, s2=shift_two)
    small = {name: value.reshape(1, -1) for name, value in small.items()}
    large = dict(x_h=inputs[0], cot_h=cotangent[0], wq_h=w_qkv, wo_h=w_o, wfc_h=w_fc, wp_h=w_proj)
    grads_shape = (CHUNKS, 2, 2, 2, 4, 96, BLOCK)
    outs = dict(
        outputs=(jax.ShapeDtypeStruct((span, width), BF16), vmem),
        input_grads=(jax.ShapeDtypeStruct((span, width), BF16), vmem),
        grads_out=(jax.ShapeDtypeStruct(grads_shape, BF16), anywhere),
    )
    scratch = dict(
        x=pltpu.VMEM((span, width), BF16),
        cot=pltpu.VMEM((span, width), BF16),
        wq=pltpu.VMEM((width, merged), BF16),
        wo=pltpu.VMEM((width, width), BF16),
        wfc=pltpu.VMEM((width, hidden_units), BF16),
        wp=pltpu.VMEM((hidden_units, width), BF16),
        fi=pltpu.VMEM((span, width), BF16),
        si=pltpu.VMEM((span, width), BF16),
        fit=pltpu.VMEM((width, span), BF16),
        sit=pltpu.VMEM((width, span), BF16),
        cos=pltpu.VMEM((ROT // 2, span), F32),
        sin=pltpu.VMEM((ROT // 2, span), F32),
        kv=pltpu.VMEM((parts, span, LANES), BF16),
        q=pltpu.VMEM((heads, span, LANES), BF16),
        dot=pltpu.VMEM((width, span), BF16),
        act=pltpu.VMEM((span, width), BF16),
        gh=pltpu.VMEM((span, width), BF16),
        result=pltpu.VMEM((span, width), F32),
        second=pltpu.VMEM((span, width), F32),
        first=pltpu.VMEM((span, width), F32),
        sum_fc=pltpu.VMEM((8, hidden_units), F32),
        kx=pltpu.VMEM((parts, span, LANES), BF16),
        kxt=pltpu.VMEM((parts, LANES, span), BF16),
        vx=pltpu.VMEM((parts, span, LANES), BF16),
        vxt=pltpu.VMEM((parts, LANES, span), BF16),
        dk=pltpu.VMEM((parts, span, LANES), F32),
        dv=pltpu.VMEM((parts, span, LANES), F32),
        scores=pltpu.VMEM((parts, span, span), F32),
        raised=pltpu.VMEM((parts, span, span), BF16),
        att=pltpu.VMEM((LANES, span), F32),
        dq=pltpu.VMEM((LANES, span), F32),
        ga=pltpu.VMEM((LANES, span), BF16),
        gat=pltpu.VMEM((span, LANES), BF16),
        attt=pltpu.VMEM((width, span), BF16),
        gpt=pltpu.VMEM((merged, span), BF16),
        gp=pltpu.VMEM((span, merged), BF16),
        dkv_out=pltpu.VMEM((parts, span, LANES), BF16),
        dkv_in=pltpu.VMEM((parts, span, LANES), BF16),
        total=pltpu.VMEM((span, LANES), F32),
        grads=pltpu.VMEM(grads_shape, BF16),
        load_sem=pltpu.SemaphoreType.DMA((6,)),
        kv_sem=pltpu.SemaphoreType.DMA((2, parts)),
        dkv_sem=pltpu.SemaphoreType.DMA((2, parts)),
    )
    names = [*small, *large, *outs, *scratch]
    results = pl.pallas_call(
        functools.partial(layer_kernel, names, parts, inside),
        out_shape=[shape for shape, _ in outs.values()],
        in_specs=[vmem] * len(small) + [anywhere] * len(large),
        out_specs=[spec for _, spec in outs.values()],
        scratch_shapes=list(scratch.values()),
        compiler_params=pltpu.CompilerParams(
            collective_id=0, has_side_effects=True, vmem_limit_bytes=63 * 2**20
        ),
        name="layer",
    )(*small.values(), *large.values())
    outputs, input_grads, grads = results

    blocks = 8
    fc = grads[0:3].transpose(4, 1, 5, 0, 2, 3, 6).reshape(width, hidden_units)
    proj = grads[3:6].transpose(4, 1, 2, 3, 5, 0, 6).reshape(hidden_units, width)
    o = grads[6].transpose(3, 0, 4, 1, 2, 5).reshape(width, 4, BLOCK)[:, :, :192].reshape(width, width)
    qkv = grads[7].transpose(3, 0, 4, 1, 2, 5).reshape(width, 4 * BLOCK)
    lines = qkv[:, merged:].reshape(blocks, 96, LANES)
    vectors = [lines[:, 0, : merged // blocks], lines[:, 1:4]] + [lines[:, i, : width // blocks] for i in range(4, 9)]
    vectors = [vector.reshape(-1) for vector in vectors]
    every = [qkv[:, :merged], vectors[0], o, fc, vectors[1], proj, *vectors[2:]]
    shards = [lax.psum_scatter(item, "batch", scatter_dimension=0, tiled=True) for item in every]
    shards = [lax.psum(item, "seq").astype(F32) for item in shards]
    return (outputs[None], input_grads[None], *shards)


def solution(mesh):
    whole, part = P(), P("batch", "seq", None)
    in_specs = (part, P("batch", None), *[whole] * 11, part)
    matrix, vector = P("batch", None), P("batch")
    out_specs = (part, part, matrix, vector, matrix, matrix, vector, matrix, *[vector] * 5)
    return jax.shard_map(per_device, mesh=mesh, in_specs=in_specs, out_specs=out_specs, check_vma=False)
```

```python
import functools
import math
import types

import jax
import jax.numpy as jnp
import numpy as np
from jax import lax
from jax.experimental import pallas as pl
from jax.experimental.pallas import tpu as pltpu
from jax.sharding import PartitionSpec as P

HEAD = 64
ROT = 16
EPSILON = 1e-05
LANES = 128
BLOCK = 256
FAR = -1e30
LOG2E = math.log2(math.e)
MESH = pl.DeviceIdType.MESH
F32 = jnp.float32
BF16 = jnp.bfloat16

CHUNKS = 8
PIECE = 96
SLOTS = 4


def x_first(chunk):
    return chunk % 2 == 0


def place(chunk, b, quarter, inside):
    y, x = quarter // 2, quarter % 2
    p, s = (x, y) if inside and x_first(chunk) else (y, x)
    return (((b % 2 * 2 + p) * 2 + s) * 4 + b // 2) * PIECE


def chunk_ref(r, chunk):
    if chunk < 6:
        return r.grads.at[chunk]
    return r.wp.at[:, (chunk - 6) * BLOCK : (chunk - 5) * BLOCK]


def mm(a, b, ca=1, cb=0):
    return lax.dot_general(a, b, (((ca,), (cb,)), ((), ())), preferred_element_type=F32)


def flip(value):
    return value.astype(F32).T


def lanes_of(shape):
    return lax.broadcasted_iota(jnp.int32, shape, 1)


def rows_of(shape):
    return lax.broadcasted_iota(jnp.int32, shape, 0)


SCHEDULE = {
    3: [("send_b", 0), ("send_a", 2)],
    4: [("send_b", 1), ("send_a", 3)],
    6: [("send_c", 0), ("send_c", 1)],
    8: [("send_b", 2), ("send_a", 4)],
    9: [("send_b", 3), ("send_a", 5)],
    10: [("send_d", 0)],
    11: [("send_d", 1), ("send_c", 2)],
    12: [("send_c", 3)],
    13: [("send_b", 4)],
    14: [("send_b", 5)],
    15: [("send_d", 2)],
    16: [("send_d", 3), ("send_c", 4)],
    17: [("send_c", 5)],
    20: [("send_d", 4)],
    21: [("send_d", 5)],
}


def gelu_parts(hidden):
    size = jnp.abs(hidden)
    t = pl.reciprocal(1.0 + (0.3275911 / math.sqrt(2.0)) * size)
    bell = jnp.exp2(hidden * hidden * (-0.5 * LOG2E))
    poly = 0.5 * 1.061405429
    for term in (-1.453152027, 1.421413741, -0.284496736, 0.254829592):
        poly = poly * t + 0.5 * term
    tail = poly * t * bell
    below = jnp.where(hidden >= 0, 1.0 - tail, tail)
    return below, hidden * bell * (1.0 / math.sqrt(2.0 * math.pi))


def layer_kernel(names, parts, inside, *refs):
    r = types.SimpleNamespace(**dict(zip(names, refs, strict=True)))
    span, width = r.x.shape
    hidden_units = r.wfc.shape[1]
    heads = width // HEAD
    mine = lax.axis_index("seq")
    batch = lax.axis_index("batch")
    core = lax.rem(batch, 2)

    loads = [
        pltpu.make_async_copy(src, dst, r.load_sem.at[i])
        for i, (src, dst) in enumerate(
            [(r.x_h, r.x), (r.wq_h, r.wq), (r.cot_h, r.cot), (r.wo_h, r.wo), (r.wfc_h, r.wfc), (r.wp_h, r.wp)]
        )
    ]
    for load in loads:
        load.start()

    barrier = pltpu.get_barrier_semaphore()
    peers = [(lax.rem(mine + distance, parts), batch) for distance in range(1, parts)]
    summing = Summing(r, mine, batch, parts) if inside else None
    if inside:
        peers += [summing.core_peer, *summing.z_peers]
    for peer in peers:
        pl.semaphore_signal(barrier, inc=1, device_id=peer, device_id_type=MESH)
    pl.semaphore_wait(barrier, len(peers))

    def keep(chunk, b, quarter, value):
        row = place(chunk, b, quarter, inside)
        chunk_ref(r, chunk)[row : row + PIECE, :] = value.astype(BF16)

    def step(*steps):
        for kind, chunk in steps if inside else ():
            getattr(summing, kind)(chunk)

    loads[0].wait()

    def norm_tile(i):
        tokens = r.x[pl.ds(i * LANES, LANES), :].astype(F32)
        average = jnp.mean(tokens, axis=-1, keepdims=True)
        centered = tokens - average
        variance = jnp.mean(centered * centered, axis=-1, keepdims=True)
        inverse_std = lax.rsqrt(variance + EPSILON)
        return centered * inverse_std, inverse_std

    for i in range(span // LANES):
        normed, _ = norm_tile(i)
        rows = pl.ds(i * LANES, LANES)
        first = normed * r.g1[...][None] + r.s1[...][None]
        second = normed * r.g2[...][None] + r.s2[...][None]
        r.fi[rows, :] = first.astype(BF16)
        r.si[rows, :] = second.astype(BF16)
        r.fit[:, rows] = first.T.astype(BF16)
        r.sit[:, rows] = second.T.astype(BF16)

    half = ROT // 2
    index = rows_of((half, span))
    frequency = jnp.zeros((half, span), F32)
    for i in range(half):
        frequency = jnp.where(index == i, np.float32(10000.0 ** (-2.0 * i / ROT)), frequency)
    angle = (mine * span + lanes_of((half, span))).astype(F32) * frequency
    cosine, sine = jnp.cos(angle), jnp.sin(angle)
    r.cos[...] = cosine
    r.sin[...] = sine
    ones = jnp.ones((HEAD - ROT, span), F32)
    zeros = jnp.zeros((HEAD - ROT, span), F32)
    table_cos = jnp.concatenate([cosine, cosine, ones] * 2, axis=0).T
    table_sin = jnp.concatenate([-sine, sine, zeros] * 2, axis=0).T
    lane = lanes_of((span, LANES))

    def rotate(tile, cos_of, sin_of):
        partner = jnp.where(
            lax.rem(lane, HEAD) < half, pltpu.roll(tile, LANES - half, 1), pltpu.roll(tile, half, 1)
        )
        return tile * cos_of + partner * sin_of

    def docs_row(distance):
        part = jnp.maximum(mine - distance, 0)
        return r.docs[0:1, pl.ds(pl.multiple_of(part * span, LANES), span)]

    loads[1].wait()
    key_value = mm(r.fi[...], r.wq[:, width:]) + r.bq[width:][None]
    low = lane < HEAD
    key_value = rotate(key_value, jnp.where(low, table_cos, 1.0), jnp.where(low, table_sin, 0.0))
    r.kv[0] = key_value.astype(BF16)
    for distance in range(1, parts):

        @pl.when(mine + distance < parts)
        def _():
            kv_copy(r, mine, batch, parts, distance).start()

    feature_row = rows_of((LANES, span)) - HEAD
    query_feature = jnp.where(feature_row == docs_row(0), 1.0, 0.0).T
    for i in range(heads // 2):
        columns = slice(i * LANES, (i + 1) * LANES)
        tile = mm(r.fi[...], r.wq[:, columns]) + r.bq[columns][None]
        tile = rotate(tile, table_cos, table_sin) * (LOG2E / math.sqrt(HEAD))
        r.q[2 * i] = jnp.where(low, tile, query_feature).astype(BF16)
        r.q[2 * i + 1] = jnp.where(low, pltpu.roll(tile, HEAD, 1), query_feature).astype(BF16)

    loads[2].wait()
    loads[3].wait()
    for i in range(width // BLOCK):
        rows = slice(i * BLOCK, (i + 1) * BLOCK)
        r.dot[rows, :] = mm(r.wo[rows, :], r.cot[...], 1, 1).astype(BF16)

    loads[4].wait()
    loads[5].wait()
    r.result[...] = jnp.zeros_like(r.result)
    r.second[...] = jnp.zeros_like(r.second)
    ones_rows = jnp.ones((8, span), BF16)
    group = 2 * 4 * 96

    for g in range(hidden_units // group):
        columns = slice(g * group, (g + 1) * group)
        hidden = mm(r.si[...], r.wfc[:, columns]) + r.bfc[columns][None]
        grad_act = mm(r.cot[...], r.wp[columns, :], 1, 1)
        below, slope = gelu_parts(hidden)
        r.act[...] = (hidden * below).astype(BF16)
        r.gh[...] = (grad_act * (below + slope)).astype(BF16)
        grad_w = mm(r.sit[...], r.gh[...])
        for k in range(group // BLOCK):
            chunk, quarter = divmod(g * (group // BLOCK) + k, 4)
            for b in range(8):
                keep(chunk, b, quarter, grad_w[b * PIECE : (b + 1) * PIECE, k * BLOCK : (k + 1) * BLOCK])
        step(*[("send", g - 1)] * (g > 0))
        grad_w = mm(r.act[...], r.cot[...], 0, 0)
        for k in range(3):
            for c in range(2):
                for q in range(4):
                    row = (c * 4 + q) * PIECE
                    keep(3 + k, 2 * g + c, q, grad_w[row : row + PIECE, k * BLOCK : (k + 1) * BLOCK])
        if g == 3:
            step(("send", 3), ("send_a", 0), ("send_a", 1))
        r.sum_fc[:, columns] = mm(ones_rows, r.gh[...])
        r.result[...] += mm(r.act[...], r.wp[columns, :])
        r.second[...] += mm(r.gh[...], r.wfc[:, columns], 1, 1)
    step(("send", 4), ("send", 5))

    for distance in range(parts):

        @pl.when(mine >= distance)
        def _():
            if distance:
                kv_copy(r, mine, batch, parts, distance).wait_recv()
            docs = docs_row(distance)
            apart = (feature_row >= 0) & (feature_row < 8) & (feature_row != docs)
            key_feature = jnp.where(apart, FAR, 0.0).T
            pair = r.kv[distance].astype(F32)
            keys = jnp.where(low, pair, key_feature)
            values = jnp.where(low, pltpu.roll(pair, HEAD, 1), jnp.where(lane < HEAD + 2, 1.0, 0.0))
            r.kx[distance] = keys.astype(BF16)
            r.kxt[distance] = keys.T.astype(BF16)
            r.vx[distance] = values.astype(BF16)
            r.vxt[distance] = values.T.astype(BF16)

    r.dk[...] = jnp.zeros_like(r.dk)
    r.dv[...] = jnp.zeros_like(r.dv)

    def scheduled(now):
        for when, steps in SCHEDULE.items():

            @pl.when(now == when)
            def _():
                step(*steps)

    def one_head(h, _):
        rows = pl.ds(pl.multiple_of(h * HEAD, HEAD), HEAD)

        def columns_of(distance):
            return pl.ds(pl.multiple_of(distance * span, LANES), span)

        def scores(distance, causal):
            raw = mm(r.kx[distance], r.q[h], 1, 1)
            if causal:
                raw = jnp.where(rows_of(raw.shape) <= lanes_of(raw.shape), raw, FAR)
            r.scores[:, columns_of(distance)] = raw
            return jnp.max(raw, axis=0, keepdims=True)

        top = scores(0, True)
        top = lax.fori_loop(1, mine + 1, lambda d, m: jnp.maximum(m, scores(d, False)), top)
        r.att[...] = jnp.zeros_like(r.att)

        def weigh(distance, _):
            raised = jnp.exp2(r.scores[:, columns_of(distance)] - top).astype(BF16)
            r.wfc[:span, columns_of(distance)] = raised
            r.att[...] += mm(r.vxt[distance], raised)
            return 0

        lax.fori_loop(0, mine + 1, weigh, 0)
        scheduled(2 * h)
        inverse = 1.0 / r.att[HEAD : HEAD + 1, :]
        attended = r.att[:HEAD, :] * inverse
        r.attt[rows, :] = attended.astype(BF16)
        grad_att = r.dot[rows, :].astype(F32)
        delta = jnp.sum(grad_att * attended, axis=0, keepdims=True) * -inverse
        delta_high = delta.astype(BF16).astype(F32)
        row = rows_of((HEAD, span))
        extra = jnp.where(row == 0, delta_high, jnp.where(row == 1, delta - delta_high, 0.0))
        grad_att = jnp.concatenate([grad_att * inverse, extra], axis=0)
        r.ga[...] = grad_att.astype(BF16)
        r.gat[...] = grad_att.T.astype(BF16)
        r.dq[...] = jnp.zeros_like(r.dq)

        def back(distance, _):
            grad_probs = mm(r.vx[distance], r.ga[...])
            raised = r.wfc[:span, columns_of(distance)]
            grad_scores = (raised.astype(F32) * grad_probs).astype(BF16)
            r.dv[distance] += mm(raised, r.gat[...])
            r.dk[distance] += mm(grad_scores, r.q[h])
            r.dq[...] += mm(r.kxt[distance], grad_scores)
            return 0

        lax.fori_loop(0, mine + 1, back, 0)
        r.gpt[rows, :] = rotate_back(r, r.dq[:HEAD, :] * (1.0 / math.sqrt(HEAD))).astype(BF16)
        scheduled(2 * h + 1)
        return 0

    lax.fori_loop(0, heads, one_head, 0)

    def packed(distance):
        return jnp.where(low, r.dk[distance] * (1.0 / LOG2E), pltpu.roll(r.dv[distance], HEAD, 1))

    for distance in range(1, parts):

        @pl.when(mine >= distance)
        def _():
            r.dkv_out[distance] = packed(distance).astype(BF16)
            dkv_copy(r, mine, batch, parts, distance).start()

    grad_w = mm(r.attt[...], r.cot[...])
    for b in range(8):
        for q in range(4):
            piece = grad_w[b * 96 : (b + 1) * 96, q * 192 : (q + 1) * 192]
            piece = jnp.concatenate([piece, jnp.zeros((96, 64), F32)], axis=1)
            keep(6, b, q, piece)
    step(("send", 6))

    r.total[...] = packed(0)
    for distance in range(1, parts):

        @pl.when(mine + distance < parts)
        def _():
            dkv_copy(r, mine, batch, parts, distance).wait_recv()
            r.total[...] += r.dkv_in[distance].astype(F32)

    pair = r.total[...].T
    r.gpt[width : width + HEAD, :] = rotate_back(r, pair[:HEAD]).astype(BF16)
    r.gpt[width + HEAD :, :] = pair[HEAD:].astype(BF16)

    grad_w = mm(r.fit[...], r.gpt[...], 1, 1)
    for b in range(8):
        for q in range(4):
            piece = grad_w[b * 96 : (b + 1) * 96, q * BLOCK : min((q + 1) * BLOCK, width + 2 * HEAD)]
            if q == 3:
                piece = jnp.concatenate([piece, jnp.zeros((96, LANES), F32)], axis=1)
            keep(7, b, q, piece)
    for i in range(width // LANES):
        columns = slice(i * LANES, (i + 1) * LANES)
        r.act[:, columns] = flip(r.gpt[columns, :]).astype(BF16)
    r.gh[:, :LANES] = flip(r.gpt[width:, :]).astype(BF16)

    first = mm(r.act[...], r.wq[:, :width], 1, 1) + mm(r.gh[:, :LANES], r.wq[:, width:], 1, 1)
    for i in range(width // LANES):
        (r.dk if i < parts else r.dv)[i % parts] = first[:, i * LANES : (i + 1) * LANES]
    sums = [jnp.zeros((1, width), F32) for _ in range(4)]
    for i in range(span // LANES):
        rows = pl.ds(i * LANES, LANES)
        normed, inverse_std = norm_tile(i)
        first = [(r.dk if j < parts else r.dv)[j % parts, rows, :] for j in range(width // LANES)]
        first, second = jnp.concatenate(first, axis=1), r.second[rows, :]
        for j, term in enumerate((normed * first, first, normed * second, second)):
            sums[j] = sums[j] + jnp.sum(term, axis=0, keepdims=True)
        scaled = first * r.g1[...][None] + second * r.g2[...][None]
        mean_one = jnp.mean(scaled, axis=-1, keepdims=True)
        mean_two = jnp.mean(scaled * normed, axis=-1, keepdims=True)
        back = inverse_std * (scaled - mean_one - normed * mean_two)
        r.si[rows, :] = (r.cot[rows, :].astype(F32) + back).astype(BF16)

    sum_qkv = mm(ones_rows, r.gpt[...], 1, 1)[0:1]
    sum_proj = mm(ones_rows, r.cot[...])[0:1]
    for b in range(8):
        lines = [cut(sum_qkv, b * 112, 112)]
        lines += [r.sum_fc[0:1, b * 384 + i * LANES : b * 384 + (i + 1) * LANES] for i in range(3)]
        lines += [cut(line, b * 96, 96) for line in (sum_proj, *sums)]
        lines.append(jnp.zeros((16 - len(lines), LANES), F32))
        row = place(7, b, 3, inside)
        chunk_ref(r, 7)[row : row + 16, LANES:] = jnp.concatenate(lines, axis=0).astype(BF16)
    step(("send", 7))
    copies = [pltpu.make_async_copy(r.si, r.input_grads, r.load_sem.at[0])]
    copies[0].start()

    for i in range(width // LANES):
        columns = slice(i * LANES, (i + 1) * LANES)
        r.fi[:, columns] = flip(r.attt[columns, :]).astype(BF16)
    r.x[...] = (r.result[...] + r.x[...].astype(F32) + r.bp[...][None] + mm(r.fi[...], r.wo[...])).astype(BF16)
    copies.append(pltpu.make_async_copy(r.x, r.outputs, r.load_sem.at[1]))
    copies[1].start()

    if inside:
        step(("send_a", 6), ("send_a", 7))
        step(*[("finish", k) for k in range(6)])
        step(("send_b", 6), ("send_b", 7), ("send_c", 6), ("send_c", 7), ("send_d", 6), ("send_d", 7))
        step(("finish", 6), ("finish", 7))
        summing.close()
    else:
        copies.append(pltpu.make_async_copy(r.grads, r.grads_out.at[:6], r.load_sem.at[2]))
        copies += [pltpu.make_async_copy(chunk_ref(r, k), r.grads_out.at[k], r.load_sem.at[k - 3]) for k in (6, 7)]
        for copy in copies[2:]:
            copy.start()
    for copy in copies:
        copy.wait()
    for distance in range(1, parts):

        @pl.when(mine + distance < parts)
        def _():
            kv_copy(r, mine, batch, parts, distance).wait_send()

        @pl.when(mine >= distance)
        def _():
            dkv_copy(r, mine, batch, parts, distance).wait_send()


def cut(line, start, size):
    line = jnp.concatenate([line, jnp.zeros((1, LANES), F32)], axis=1)
    base = start // LANES * LANES
    line = line[:, base : base + 2 * LANES]
    shift = start - base
    if shift:
        line = pltpu.roll(line, 2 * LANES - shift, 1)
    return jnp.where(lanes_of((1, LANES)) < size, line[:, :LANES], 0.0)


def rotate_back(r, grads):
    half = ROT // 2
    one, two = grads[:half], grads[half:ROT]
    cosine, sine = r.cos[...], r.sin[...]
    return jnp.concatenate([one * cosine + two * sine, two * cosine - one * sine, grads[ROT:]], axis=0)


class Summing:
    def __init__(self, r, mine, batch, parts):
        self.r, self.mine, self.batch, self.parts = r, mine, batch, parts
        y, x = mine // 2, lax.rem(mine, 2)
        self.z, self.core = batch // 2, lax.rem(batch, 2)
        self.axes = {"x": (x, (y * 2 + 1 - x, batch)), "y": (y, ((1 - y) * 2 + x, batch))}
        self.core_peer = (mine, self.z * 2 + 1 - self.core)
        self.z_peers = [(mine, lax.rem(self.z + i, 4) * 2 + self.core) for i in (1, 2, 3)]
        self.seq_peers = [(lax.rem(mine + i, parts), batch) for i in range(1, parts)]
        self.out_copies = []

    def of(self, chunk):
        first, then = ("x", "y") if x_first(chunk) else ("y", "x")
        return *self.axes[first], *self.axes[then]

    def copy(self, name, index, src, dst, peer):
        sem = getattr(self.r, name + "_sem")
        return pltpu.make_async_remote_copy(
            src_ref=src,
            dst_ref=dst,
            send_sem=sem.at[0, index],
            recv_sem=sem.at[1, index],
            device_id=peer,
            device_id_type=MESH,
        )

    def rows(self, chunk, start, count):
        return chunk_ref(self.r, chunk).at[pl.ds(pl.multiple_of(start, PIECE), count)]

    def pair(self, chunk):
        src = self.rows(chunk, (1 - self.core) * 16 * PIECE, 16 * PIECE)
        return self.copy("pair", chunk, src, self.r.pair.at[chunk % SLOTS], self.core_peer)

    def half(self, chunk):
        p, peer, _, _ = self.of(chunk)
        src = self.rows(chunk, (self.core * 2 + 1 - p) * 8 * PIECE, 8 * PIECE)
        return self.copy("half", chunk, src, self.r.half.at[chunk], peer)

    def quarter(self, chunk):
        p, _, s, peer = self.of(chunk)
        src = self.rows(chunk, ((self.core * 2 + p) * 2 + 1 - s) * 4 * PIECE, 4 * PIECE)
        return self.copy("quarter", chunk, src, self.r.quarter.at[chunk], peer)

    def start_of_mine(self, chunk):
        p, _, s, _ = self.of(chunk)
        return ((self.core * 2 + p) * 2 + s) * 4 * PIECE

    def line(self, chunk, i):
        src = self.rows(chunk, self.start_of_mine(chunk) + lax.rem(self.z + i, 4) * PIECE, PIECE)
        return self.copy("line", chunk * 3 + i - 1, src, self.r.line.at[chunk * 3 + i - 1], self.z_peers[i - 1])

    def share(self, chunk, i):
        here = self.r.share.at[chunk, self.mine]
        return self.copy("share", chunk * 3 + i - 1, here, here, self.seq_peers[i - 1])

    def add(self, chunk, start, other, other_start, pieces):
        ref = chunk_ref(self.r, chunk)

        def one(i, _):
            to = pl.ds(pl.multiple_of(start + i * PIECE, PIECE), PIECE)
            ref[to, :] += other[pl.ds(pl.multiple_of(other_start + i * PIECE, PIECE), PIECE), :]
            return 0

        lax.fori_loop(0, pieces, one, 0)

    def send(self, chunk):
        if chunk >= SLOTS:
            pl.semaphore_wait(self.r.free_sem, 1)
        self.pair(chunk).start()

    def send_a(self, chunk):
        self.pair(chunk).wait_recv()
        p = self.of(chunk)[0]
        got = self.r.pair.at[chunk % SLOTS]
        for side in (1 - p, p):
            self.add(chunk, (self.core * 2 + side) * 8 * PIECE, got, side * 8 * PIECE, 8)
            if side is not p:
                self.half(chunk).start()
        if chunk + SLOTS < CHUNKS:
            pl.semaphore_signal(self.r.free_sem, inc=1, device_id=self.core_peer, device_id_type=MESH)

    def send_b(self, chunk):
        self.half(chunk).wait_recv()
        p, _, s, _ = self.of(chunk)
        for side in (1 - s, s):
            start = ((self.core * 2 + p) * 2 + side) * 4 * PIECE
            self.add(chunk, start, self.r.half.at[chunk], side * 4 * PIECE, 4)
            if side is not s:
                self.quarter(chunk).start()

    def send_c(self, chunk):
        self.quarter(chunk).wait_recv()
        start = self.start_of_mine(chunk)
        for i in (1, 2, 3, 0):
            z = lax.rem(self.z + i, 4) * PIECE
            self.add(chunk, start + z, self.r.quarter.at[chunk], z, 1)
            if i:
                self.line(chunk, i).start()

    def send_d(self, chunk):
        total = self.rows(chunk, self.start_of_mine(chunk) + self.z * PIECE, PIECE)[...].astype(F32)
        for i in (1, 2, 3):
            self.line(chunk, i).wait_recv()
            total = total + self.r.line[chunk * 3 + i - 1].astype(F32)
        self.r.share[chunk, self.mine] = total.astype(BF16)
        for i in (1, 2, 3):
            self.share(chunk, i).start()

    def finish(self, chunk):
        r = self.r
        for i in (1, 2, 3):
            self.share(chunk, i).wait_recv()
        quarters = [r.share[chunk, q].astype(F32) for q in range(4)]
        top = chunk % 4 * LANES
        left = chunk // 4 * 4 * BLOCK
        if chunk == 6:
            whole = jnp.concatenate([quarter[:, :192] for quarter in quarters], axis=1)
        else:
            whole = jnp.concatenate(quarters, axis=1)
        r.scores[top : top + PIECE, left : left + whole.shape[1]] = whole
        stage = lambda a, b: r.scores.at[top : top + PIECE, left + a : left + b]
        if chunk < 3:
            moves = [(stage(0, 1024), r.grad_fc.at[:, chunk * 1024 : (chunk + 1) * 1024])]
        elif chunk < 6:
            columns = slice((chunk - 3) * BLOCK, (chunk - 2) * BLOCK)
            moves = [
                (stage(q * BLOCK, (q + 1) * BLOCK), r.grad_proj.at[q * PIECE : (q + 1) * PIECE, columns])
                for q in range(4)
            ]
        elif chunk == 6:
            moves = [(stage(0, r.grad_o.shape[1]), r.grad_o)]
        else:
            moves = [(stage(0, r.grad_qkv.shape[1]), r.grad_qkv)]
            lines = quarters[3][:16, LANES:]
            r.grad_bq[...] = lines[0, : r.grad_bq.shape[0]]
            for i in range(3):
                r.grad_bfc[i * LANES : (i + 1) * LANES] = lines[1 + i]
            for i, out in enumerate((r.grad_bp, r.grad_g1, r.grad_s1, r.grad_g2, r.grad_s2)):
                out[...] = lines[4 + i, : out.shape[0]]
        for src, dst in moves:
            copy = pltpu.make_async_copy(src, dst, r.out_sem.at[len(self.out_copies)])
            copy.start()
            self.out_copies.append(copy)

    def close(self):
        for copy in self.out_copies:
            copy.wait()
        for chunk in range(CHUNKS):
            for copy in (self.pair(chunk), self.half(chunk), self.quarter(chunk)):
                copy.wait_send()
            for i in (1, 2, 3):
                self.line(chunk, i).wait_send()
                self.share(chunk, i).wait_send()


def kv_copy(r, mine, batch, parts, distance):
    return pltpu.make_async_remote_copy(
        src_ref=r.kv.at[0],
        dst_ref=r.kv.at[distance],
        send_sem=r.kv_sem.at[0, distance],
        recv_sem=r.kv_sem.at[1, distance],
        device_id=(lax.rem(mine + distance, parts), batch),
        device_id_type=MESH,
    )


def dkv_copy(r, mine, batch, parts, distance):
    return pltpu.make_async_remote_copy(
        src_ref=r.dkv_out.at[distance],
        dst_ref=r.dkv_in.at[distance],
        send_sem=r.dkv_sem.at[0, distance],
        recv_sem=r.dkv_sem.at[1, distance],
        device_id=(lax.rem(mine - distance + parts, parts), batch),
        device_id_type=MESH,
    )


def per_device(inputs, doc_ids, w_qkv, b_qkv, w_o, w_fc, b_fc, w_proj, b_proj, gain_one, shift_one, gain_two, shift_two, cotangent):
    rows_here, span, width = inputs.shape
    assert rows_here == 1
    parts = lax.axis_size("seq")
    heads = width // HEAD
    hidden_units = w_fc.shape[1]
    merged = width + 2 * HEAD
    inside = parts == 4 and lax.axis_size("batch") == 8
    vmem = pl.BlockSpec(memory_space=pltpu.VMEM)
    anywhere = pl.BlockSpec(memory_space=pl.ANY)

    small = dict(docs=doc_ids, bq=b_qkv, bfc=b_fc, bp=b_proj, g1=gain_one, s1=shift_one, g2=gain_two, s2=shift_two)
    large = dict(x_h=inputs[0], cot_h=cotangent[0], wq_h=w_qkv, wo_h=w_o, wfc_h=w_fc, wp_h=w_proj)
    outs = dict(outputs=((span, width), BF16, anywhere), input_grads=((span, width), BF16, anywhere))
    if inside:
        outs |= dict(
            grad_qkv=((width // 8, merged), F32, anywhere),
            grad_bq=((merged // 8,), F32, vmem),
            grad_o=((width // 8, width), F32, anywhere),
            grad_fc=((width // 8, hidden_units), F32, anywhere),
            grad_bfc=((hidden_units // 8,), F32, vmem),
            grad_proj=((hidden_units // 8, width), F32, anywhere),
            grad_bp=((width // 8,), F32, vmem),
            grad_g1=((width // 8,), F32, vmem),
            grad_s1=((width // 8,), F32, vmem),
            grad_g2=((width // 8,), F32, vmem),
            grad_s2=((width // 8,), F32, vmem),
        )
    else:
        outs |= dict(grads_out=((CHUNKS, 32 * PIECE, BLOCK), BF16, anywhere))
    scratch = dict(
        x=pltpu.VMEM((span, width), BF16),
        cot=pltpu.VMEM((span, width), BF16),
        wq=pltpu.VMEM((width, merged), BF16),
        wo=pltpu.VMEM((width, width), BF16),
        wfc=pltpu.VMEM((width, hidden_units), BF16),
        wp=pltpu.VMEM((hidden_units, width), BF16),
        fi=pltpu.VMEM((span, width), BF16),
        si=pltpu.VMEM((span, width), BF16),
        fit=pltpu.VMEM((width, span), BF16),
        sit=pltpu.VMEM((width, span), BF16),
        cos=pltpu.VMEM((ROT // 2, span), F32),
        sin=pltpu.VMEM((ROT // 2, span), F32),
        kv=pltpu.VMEM((parts, span, LANES), BF16),
        q=pltpu.VMEM((heads, span, LANES), BF16),
        dot=pltpu.VMEM((width, span), BF16),
        act=pltpu.VMEM((span, width), BF16),
        gh=pltpu.VMEM((span, width), BF16),
        result=pltpu.VMEM((span, width), F32),
        second=pltpu.VMEM((span, width), F32),
        sum_fc=pltpu.VMEM((8, hidden_units), F32),
        kx=pltpu.VMEM((parts, span, LANES), BF16),
        kxt=pltpu.VMEM((parts, LANES, span), BF16),
        vx=pltpu.VMEM((parts, span, LANES), BF16),
        vxt=pltpu.VMEM((parts, LANES, span), BF16),
        dk=pltpu.VMEM((parts, span, LANES), F32),
        dv=pltpu.VMEM((parts, span, LANES), F32),
        scores=pltpu.VMEM((span, parts * span), F32),
        att=pltpu.VMEM((LANES, span), F32),
        dq=pltpu.VMEM((LANES, span), F32),
        ga=pltpu.VMEM((LANES, span), BF16),
        gat=pltpu.VMEM((span, LANES), BF16),
        attt=pltpu.VMEM((width, span), BF16),
        gpt=pltpu.VMEM((merged, span), BF16),
        dkv_out=pltpu.VMEM((parts, span, LANES), BF16),
        dkv_in=pltpu.VMEM((parts, span, LANES), BF16),
        total=pltpu.VMEM((span, LANES), F32),
        grads=pltpu.VMEM((6, 32 * PIECE, BLOCK), BF16),
        load_sem=pltpu.SemaphoreType.DMA((6,)),
        kv_sem=pltpu.SemaphoreType.DMA((2, parts)),
        dkv_sem=pltpu.SemaphoreType.DMA((2, parts)),
    )
    if inside:
        scratch |= dict(
            pair=pltpu.VMEM((SLOTS, 16 * PIECE, BLOCK), BF16),
            half=pltpu.VMEM((CHUNKS, 8 * PIECE, BLOCK), BF16),
            quarter=pltpu.VMEM((CHUNKS, 4 * PIECE, BLOCK), BF16),
            line=pltpu.VMEM((CHUNKS * 3, PIECE, BLOCK), BF16),
            share=pltpu.VMEM((CHUNKS, 4, PIECE, BLOCK), BF16),
            pair_sem=pltpu.SemaphoreType.DMA((2, CHUNKS)),
            half_sem=pltpu.SemaphoreType.DMA((2, CHUNKS)),
            quarter_sem=pltpu.SemaphoreType.DMA((2, CHUNKS)),
            line_sem=pltpu.SemaphoreType.DMA((2, CHUNKS * 3)),
            share_sem=pltpu.SemaphoreType.DMA((2, CHUNKS * 3)),
            out_sem=pltpu.SemaphoreType.DMA((17,)),
            free_sem=pltpu.SemaphoreType.REGULAR,
        )
    names = [*small, *large, *outs, *scratch]
    results = pl.pallas_call(
        functools.partial(layer_kernel, names, parts, inside),
        out_shape=[jax.ShapeDtypeStruct(shape, dtype) for shape, dtype, _ in outs.values()],
        in_specs=[vmem] * len(small) + [anywhere] * len(large),
        out_specs=[spec for _, _, spec in outs.values()],
        scratch_shapes=list(scratch.values()),
        compiler_params=pltpu.CompilerParams(
            collective_id=0, has_side_effects=True, vmem_limit_bytes=63 * 2**20
        ),
        name="layer",
    )(*small.values(), *large.values())
    outputs, input_grads, *shards = results
    if inside:
        return (outputs[None], input_grads[None], *shards)

    grads = shards[0].reshape(CHUNKS, 2, 2, 2, 4, PIECE, BLOCK)
    blocks = 8
    fc = grads[0:3].transpose(4, 1, 5, 0, 2, 3, 6).reshape(width, hidden_units)
    proj = grads[3:6].transpose(4, 1, 2, 3, 5, 0, 6).reshape(hidden_units, width)
    o = grads[6].transpose(3, 0, 4, 1, 2, 5).reshape(width, 4, BLOCK)[:, :, :192].reshape(width, width)
    qkv = grads[7].transpose(3, 0, 4, 1, 2, 5).reshape(width, 4 * BLOCK)
    lines = qkv[:, merged:].reshape(blocks, 96, LANES)
    vectors = [lines[:, 0, : merged // blocks], lines[:, 1:4]] + [lines[:, i, : width // blocks] for i in range(4, 9)]
    vectors = [vector.reshape(-1) for vector in vectors]
    every = [qkv[:, :merged], vectors[0], o, fc, vectors[1], proj, *vectors[2:]]
    shards = [lax.psum_scatter(item, "batch", scatter_dimension=0, tiled=True) for item in every]
    shards = [lax.psum(item, "seq").astype(F32) for item in shards]
    return (outputs[None], input_grads[None], *shards)


def solution(mesh):
    whole, part = P(), P("batch", "seq", None)
    in_specs = (part, P("batch", None), *[whole] * 11, part)
    matrix, vector = P("batch", None), P("batch")
    out_specs = (part, part, matrix, vector, matrix, matrix, vector, matrix, *[vector] * 5)
    return jax.shard_map(per_device, mesh=mesh, in_specs=in_specs, out_specs=out_specs, check_vma=False)
```

```python
import functools
import math
import types

import jax
import jax.numpy as jnp
import numpy as np
from jax import lax
from jax.experimental import pallas as pl
from jax.experimental.pallas import tpu as pltpu
from jax.sharding import PartitionSpec as P

HEAD = 64
ROT = 16
EPSILON = 1e-05
LANES = 128
BLOCK = 256
FAR = -1e30
LOG2E = math.log2(math.e)
MESH = pl.DeviceIdType.MESH
F32 = jnp.float32
BF16 = jnp.bfloat16

PIECE = 96
SLOTS = 4


class Chunk:
    def __init__(self, name, kind, height, count, base, lane):
        self.name, self.kind = name, kind
        self.height, self.count, self.base, self.lane = height, count, base, lane

    @property
    def rows(self):
        return self.height * self.count * (2 if self.kind == "whole" else 8)

    def place(self, core, p, s, i):
        if self.kind == "whole":
            at = core * 4 + i
        elif self.kind == "line":
            at = ((core * 4 + i) * 2 + p) * 2 + s
        else:
            at = ((core * 2 + p) * 2 + s) * self.count + i
        return self.base + at * self.height

    def ref(self, r):
        if self.lane is None:
            return r.grads
        return r.wp.at[:, self.lane * BLOCK : (self.lane + 1) * BLOCK]

    @staticmethod
    def split(core, y, x):
        return (y, x) if core else (x, y)

    def unfold(self, array):
        array = array[self.base : self.base + self.rows]
        if self.kind == "whole":
            return array.reshape(2, 4, self.height, BLOCK)
        if self.kind == "line":
            array = array.reshape(2, 4, 2, 2, self.height, BLOCK).transpose(0, 2, 3, 1, 4, 5)
        else:
            array = array.reshape(2, 2, 2, self.count, self.height, BLOCK)
        return jnp.stack([array[0].swapaxes(0, 1), array[1]])


def make_chunks():
    plans = [
        ("p0", "plane", PIECE, 3, None),
        ("p1", "plane", PIECE, 3, None),
        ("f0", "line", PIECE, 4, None),
        ("p2", "plane", PIECE, 3, None),
        ("f1", "block", PIECE, 4, None),
        ("p3", "plane", PIECE, 3, None),
        ("f2", "block", PIECE, 4, None),
        ("uc", "block", PIECE // 2, 4, 1),
        ("ua", "block", PIECE // 2, 4, 0),
        ("ub", "block", PIECE // 2, 4, 0),
        ("k", "whole", PIECE // 2, 4, 1),
        ("v", "whole", 16, 4, 1),
    ]
    chunks, filled = {}, {}
    for name, kind, height, count, lane in plans:
        chunk = Chunk(name, kind, height, count, filled.get(lane, 0), lane)
        chunks[name] = chunk
        filled[lane] = chunk.base + chunk.rows
    return chunks, filled[None]


CHUNKS, GRAD_ROWS = make_chunks()


def mm(a, b, ca=1, cb=0):
    return lax.dot_general(a, b, (((ca,), (cb,)), ((), ())), preferred_element_type=F32)


def flip(value):
    return value.astype(F32).T


def lanes_of(shape):
    return lax.broadcasted_iota(jnp.int32, shape, 1)


def rows_of(shape):
    return lax.broadcasted_iota(jnp.int32, shape, 0)


EARLY_DONE = 64

FEED_SCHEDULE = [
    ([], ["send:p0"], []),
    (["a:p0"], [], ["send:p1", "send:f0"]),
    (["a:f0", "a:p1"], ["send:p2"], ["send:f1"]),
    (["b:p0"], ["a:f1", "send:p3"], []),
    [],
]

SCHEDULE = {
    4: ["a:p2", "send:f2"],
    12: ["c:p0", "a:f2"],
    16: ["b:f1"],
    20: ["a:p3"],
    28: ["b:f2"],
    32: ["c:f1"],
    36: ["b:f0", "b:p2"],
    44: ["c:f2", "b:p1"],
    48: ["c:f0"],
    60: ["b:p3", "d:f1"],
    EARLY_DONE: ["make:uc", "d:f2", "send:uc", "c:p1"],
    68: ["c:p2", "a:uc"],
    72: ["g:f2", "c:p3", "g:f1"],
    76: ["b:uc", "d:f0"],
}

LATE_SCHEDULE = [
    [],
    ["send:ua", "c:uc", "e:f1", "a:ua", "e:f2", "send:ub", "a:ub"],
    ["send:k", "b:ua", "g:f0", "a:k"],
    ["b:ub", "send:v", "d_planes:p0", "c:ua", "d:uc", "a:v", "c:ub", "d:k", "e:f0", "g:p0", "d:ua", "d:v", "d:ub"],
    ["e:uc", "e:v", "e:ua", "e:p0", "e:ub", "e:k"],
]

LENT = 5


def gelu_parts(hidden):
    size = jnp.abs(hidden)
    t = pl.reciprocal(1.0 + (0.3275911 / math.sqrt(2.0)) * size)
    bell = jnp.exp2(hidden * hidden * (-0.5 * LOG2E))
    poly = 0.5 * 1.061405429
    for term in (-1.453152027, 1.421413741, -0.284496736, 0.254829592):
        poly = poly * t + 0.5 * term
    tail = poly * t * bell
    below = jnp.where(hidden >= 0, 1.0 - tail, tail)
    return below, hidden * bell * (1.0 / math.sqrt(2.0 * math.pi))


def layer_kernel(names, parts, inside, *refs):
    r = types.SimpleNamespace(**dict(zip(names, refs, strict=True)))
    span, width = r.x.shape
    hidden_units = r.wfc.shape[1]
    heads = width // HEAD
    mine = lax.axis_index("seq")
    batch = lax.axis_index("batch")
    partner = parts - 1 - mine
    high = jnp.maximum(mine, partner)

    loads = [
        pltpu.make_async_copy(src, dst, r.load_sem.at[i])
        for i, (src, dst) in enumerate(
            [(r.x_h, r.x), (r.wq_h, r.wq), (r.cot_h, r.cot), (r.wo_h, r.wo), (r.wfc_h, r.wfc), (r.wp_h, r.wp)]
        )
    ]
    for load in loads:
        load.start()

    barrier = pltpu.get_barrier_semaphore()
    peers = [(lax.rem(mine + distance, parts), batch) for distance in range(1, parts)]
    summing = Summing(r, mine, batch, parts) if inside else None
    if inside:
        peers += [summing.core_peer, *summing.z_peers]
    for peer in peers:
        pl.semaphore_signal(barrier, inc=1, device_id=peer, device_id_type=MESH)
    pl.semaphore_wait(barrier, len(peers))

    def keep(name, core, y, x, i, value):
        chunk = CHUNKS[name]
        row = chunk.place(core, *chunk.split(core, y, x), i)
        chunk.ref(r)[row : row + chunk.height, :] = value.astype(BF16)

    def step(steps):
        for item in steps if inside else ():
            kind, name = item.split(":")
            if kind == "make":
                make_early()
            else:
                getattr(summing, kind)(CHUNKS[name])

    loads[0].wait()

    def norm_tile(i):
        tokens = r.x[pl.ds(i * LANES, LANES), :].astype(F32)
        average = jnp.mean(tokens, axis=-1, keepdims=True)
        centered = tokens - average
        variance = jnp.mean(centered * centered, axis=-1, keepdims=True)
        inverse_std = lax.rsqrt(variance + EPSILON)
        return centered * inverse_std, inverse_std

    for i in range(span // LANES):
        normed, _ = norm_tile(i)
        rows = pl.ds(i * LANES, LANES)
        first = normed * r.g1[...][None] + r.s1[...][None]
        second = normed * r.g2[...][None] + r.s2[...][None]
        r.fi[rows, :] = first.astype(BF16)
        r.si[rows, :] = second.astype(BF16)
        r.fit[:, rows] = first.T.astype(BF16)
        r.sit[:, rows] = second.T.astype(BF16)

    half = ROT // 2
    index = rows_of((half, span))
    frequency = jnp.zeros((half, span), F32)
    for i in range(half):
        frequency = jnp.where(index == i, np.float32(10000.0 ** (-2.0 * i / ROT)), frequency)
    for i, part in enumerate((mine, partner)):
        angle = (part * span + lanes_of((half, span))).astype(F32) * frequency
        r.cos[i] = jnp.cos(angle)
        r.sin[i] = jnp.sin(angle)
    cosine, sine = r.cos[0], r.sin[0]
    ones = jnp.ones((HEAD - ROT, span), F32)
    zeros = jnp.zeros((HEAD - ROT, span), F32)
    table_cos = jnp.concatenate([cosine, cosine, ones] * 2, axis=0).T
    table_sin = jnp.concatenate([-sine, sine, zeros] * 2, axis=0).T
    lane = lanes_of((span, LANES))

    def rotate(tile, cos_of, sin_of):
        partner = jnp.where(
            lax.rem(lane, HEAD) < half, pltpu.roll(tile, LANES - half, 1), pltpu.roll(tile, half, 1)
        )
        return tile * cos_of + partner * sin_of

    def docs_row(part):
        return r.docs[0:1, pl.ds(pl.multiple_of(part * span, LANES), span)]

    loads[1].wait()
    key_value = mm(r.fi[...], r.wq[:, width:]) + r.bq[width:][None]
    low = lane < HEAD
    key_value = rotate(key_value, jnp.where(low, table_cos, 1.0), jnp.where(low, table_sin, 0.0))
    r.kv[mine] = key_value.astype(BF16)
    for distance in range(1, parts):
        kv_copy(r, mine, batch, parts, distance).start()

    feature_row = rows_of((LANES, span)) - HEAD

    def keep_queries(slot, tile, feature):
        for i, head in enumerate((tile, pltpu.roll(tile, HEAD, 1))):
            head = jnp.where(low, head, feature)
            r.q[slot + i] = head.astype(BF16)
            r.qt[slot + i] = head.T.astype(BF16)

    query_feature = jnp.where(feature_row == docs_row(mine), 1.0, 0.0).T
    for i in range(heads // 2):
        columns = slice(i * LANES, (i + 1) * LANES)
        tile = mm(r.fi[...], r.wq[:, columns]) + r.bq[columns][None]
        tile = rotate(tile, table_cos, table_sin) * (LOG2E / math.sqrt(HEAD))
        keep_queries(2 * i, tile, query_feature)
        if i == LENT:
            r.lent[...] = tile.astype(BF16)

    loads[2].wait()
    loads[3].wait()
    for i in range(width // BLOCK):
        rows = slice(i * BLOCK, (i + 1) * BLOCK)
        r.dot[rows, :] = mm(r.wo[rows, :], r.cot[...], 1, 1).astype(BF16)

    @pl.when(mine == parts - 1)
    def _():
        for copy in lent_copies(r, mine, batch, parts):
            copy.start()


    loads[4].wait()
    loads[5].wait()
    r.result[...] = jnp.zeros_like(r.result)
    r.second[...] = jnp.zeros_like(r.second)
    ones_rows = jnp.ones((8, span), BF16)
    group = 2 * 4 * 96

    for g in range(hidden_units // group):
        columns = slice(g * group, (g + 1) * group)
        hidden = mm(r.si[...], r.wfc[:, columns]) + r.bfc[columns][None]
        grad_act = mm(r.cot[...], r.wp[columns, :], 1, 1)
        below, slope = gelu_parts(hidden)
        r.act[...] = (hidden * below).astype(BF16)
        r.gh[...] = (grad_act * (below + slope)).astype(BF16)
        step(FEED_SCHEDULE[g][0])
        grad_w = mm(r.act[...], r.cot[...], 0, 0)
        for c in range(2):
            for q in range(4):
                row = (c * 4 + q) * PIECE
                for k in range(3):
                    piece = grad_w[row : row + PIECE, k * BLOCK : (k + 1) * BLOCK]
                    keep(f"p{g}", c, q // 2, q % 2, k, piece)
        step(FEED_SCHEDULE[g][1])
        grad_w = mm(r.sit[...], r.gh[...])
        for k in range(group // BLOCK):
            chunk, q = divmod(g * (group // BLOCK) + k, 4)
            for b in range(8):
                piece = grad_w[b * PIECE : (b + 1) * PIECE, k * BLOCK : (k + 1) * BLOCK]
                keep(f"f{chunk}", b % 2, q // 2, q % 2, b // 2, piece)
        step(FEED_SCHEDULE[g][2])
        r.sum_fc[:, columns] = mm(ones_rows, r.gh[...])
        r.result[...] += mm(r.act[...], r.wp[columns, :])
        r.second[...] += mm(r.gh[...], r.wfc[:, columns], 1, 1)
    step(FEED_SCHEDULE[4])

    for distance in range(1, parts):
        kv_copy(r, lax.rem(mine - distance + parts, parts), batch, parts, distance).wait_recv()
    for part in range(parts):
        apart = (feature_row >= 0) & (feature_row < 8) & (feature_row != docs_row(part))
        key_feature = jnp.where(apart, FAR, 0.0).T
        pair = r.kv[part].astype(F32)
        keys = jnp.where(low, pair, key_feature)
        values = jnp.where(low, pltpu.roll(pair, HEAD, 1), jnp.where(lane < HEAD + 2, 1.0, 0.0))
        r.kx[part] = keys.astype(BF16)
        r.kxt[part] = keys.T.astype(BF16)
        r.vx[part] = values.astype(BF16)
        r.vxt[part] = values.T.astype(BF16)

    @pl.when(mine == 0)
    def _():
        for copy in lent_copies(r, mine, batch, parts):
            copy.wait_recv()
        feature = jnp.where(feature_row == docs_row(partner), 1.0, 0.0).T
        keep_queries(heads, r.lent_in[...].astype(F32), feature)

    r.dk[...] = jnp.zeros_like(r.dk)
    r.dv[...] = jnp.zeros_like(r.dv)

    def make_early():
        @pl.when(mine == parts - 1)
        def _():
            for copy in back_copies(r, mine, batch, parts):
                copy.wait_recv()

        grad_q = mm(r.fit[...], r.gqt[BLOCK:width, :], 1, 1)
        for b in range(8):
            for y in range(2):
                rows = slice(b * PIECE + y * PIECE // 2, b * PIECE + (y + 1) * PIECE // 2)
                for x in range(2):
                    keep("uc", b % 2, y, x, b // 2, grad_q[rows, x * BLOCK : (x + 1) * BLOCK])

    mid = span // 2

    def tiles_of(last):
        return [(part, 0, span, 0) for part in range(last)] + [(last, 0, mid, 0), (last, mid, mid, mid)]

    def spread(value, start):
        return jnp.concatenate([jnp.zeros((value.shape[0], start), F32), value], axis=1) if start else value

    def attend(slot, last):
        rows = pl.ds(pl.multiple_of(slot * HEAD, HEAD), HEAD)
        tiles = tiles_of(last)
        tops = []
        for part, k0, count, q0 in tiles:
            raw = mm(r.kx[part, k0 : k0 + count], r.qt[slot, :, q0:])
            if part == last:
                raw = jnp.where(rows_of(raw.shape) <= lanes_of(raw.shape), raw, FAR)
            r.scores[k0 : k0 + count, part * span + q0 : (part + 1) * span] = raw
            top = jnp.max(raw, axis=0, keepdims=True)
            tops.append(jnp.concatenate([jnp.full((1, q0), FAR, F32), top], axis=1) if q0 else top)
        top = functools.reduce(jnp.maximum, tops)
        sums = []
        for part, k0, count, q0 in tiles:
            place = slice(k0, k0 + count), slice(part * span + q0, (part + 1) * span)
            raised = jnp.exp2(r.scores[place] - top[:, q0:]).astype(BF16)
            r.wfc[place] = raised
            sums.append(spread(mm(r.vxt[part, :, k0 : k0 + count], raised), q0))
        att = functools.reduce(jnp.add, sums)
        inverse = 1.0 / att[HEAD : HEAD + 1, :]
        attended = att[:HEAD, :] * inverse
        r.attt[rows, :] = attended.astype(BF16)
        grad_att = r.dot[rows, :].astype(F32)
        delta = jnp.sum(grad_att * attended, axis=0, keepdims=True) * -inverse
        delta_high = delta.astype(BF16).astype(F32)
        row = rows_of((HEAD, span))
        extra = jnp.where(row == 0, delta_high, jnp.where(row == 1, delta - delta_high, 0.0))
        grad_att = jnp.concatenate([grad_att * inverse, extra], axis=0)
        r.ga[...] = grad_att.astype(BF16)
        r.gat[...] = grad_att.T.astype(BF16)

    def attend_back(slot, borrowed, last):
        rows = pl.ds(pl.multiple_of(slot * HEAD, HEAD), HEAD)
        tiles = tiles_of(last)
        sums = []
        for part, k0, count, q0 in tiles:
            keys = slice(k0, k0 + count)
            grad_probs = mm(r.vx[part, keys], r.ga[:, q0:])
            raised = r.wfc[keys, part * span + q0 : (part + 1) * span]
            grad_scores = (raised.astype(F32) * grad_probs).astype(BF16)
            r.dv[part, keys] += mm(raised, r.gat[q0:])
            r.dk[part, keys] += mm(grad_scores, r.q[slot, q0:])
            sums.append(spread(mm(r.kxt[part, :, keys], grad_scores), q0))
        grad_query = functools.reduce(jnp.add, sums)[:HEAD] * (1.0 / math.sqrt(HEAD))
        r.gqt[rows, :] = rotate_back(r, grad_query, borrowed).astype(BF16)

    n_borrowed = jnp.where(mine == 0, 2, 0)
    n_own = jnp.where(mine == parts - 1, heads - 2, heads)
    whole = 2 * (n_borrowed * (partner + 1) + n_own * (mine + 1))

    def half_task(i, done):
        t, backward = i // 2, lax.rem(i, 2) == 1
        borrowed = t < n_borrowed
        own = t - n_borrowed + 4
        own = jnp.where(own >= n_own, own - n_own, own)
        slot = jnp.where(borrowed, heads + t, own)
        last = jnp.where(borrowed, partner, mine)
        for part in range(parts):

            @pl.when((last == part) & ~backward)
            def _():
                attend(slot, part)

            @pl.when((last == part) & backward)
            def _():
                attend_back(slot, jnp.where(borrowed, 1, 0), part)


        @pl.when((mine == 0) & backward & (slot == heads + 1))
        def _():
            for copy in back_copies(r, mine, batch, parts):
                copy.start()

        after = done + last + 1
        before_80, after_80 = done * 80 // whole, after * 80 // whole
        for when, steps in SCHEDULE.items():

            @pl.when((before_80 < when) & (when <= after_80))
            def _():
                step(steps)

        return after

    lax.fori_loop(0, 2 * (n_borrowed + n_own), half_task, 0)
    step(LATE_SCHEDULE[0])

    def packed(part):
        return jnp.where(low, r.dk[part] * (1.0 / LOG2E), pltpu.roll(r.dv[part], HEAD, 1))

    for distance in range(1, parts):
        target = lax.rem(mine - distance + parts, parts)

        @pl.when(target <= high)
        def _():
            r.dkv_out[distance] = packed(target).astype(BF16)
            dkv_copy(r, mine, batch, parts, distance).start()

    if not inside:
        make_early()
    grad_w = mm(r.attt[:width, :], r.cot[...])
    grad_q = mm(r.fit[...], r.gqt[:BLOCK, :], 1, 1)
    for b in range(8):
        core, z = b % 2, b // 2
        for i, name in enumerate(("ua", "ub")):
            rows = slice(b * PIECE + i * PIECE // 2, b * PIECE + (i + 1) * PIECE // 2)
            for q in range(4):
                piece = grad_w[rows, q * BLOCK : (q + 1) * BLOCK] if q < 3 else grad_q[rows]
                keep(name, core, q // 2, q % 2, z, piece)
    step(LATE_SCHEDULE[1])

    r.total[...] = packed(mine)
    for distance in range(1, parts):
        source = lax.rem(mine + distance, parts)

        @pl.when(mine <= jnp.maximum(source, parts - 1 - source))
        def _():
            dkv_copy(r, mine, batch, parts, distance).wait_recv()
            r.total[...] += r.dkv_in[distance].astype(F32)

    pair = r.total[...].T
    r.gkvt[:HEAD, :] = rotate_back(r, pair[:HEAD], 0).astype(BF16)
    r.gkvt[HEAD:, :] = pair[HEAD:].astype(BF16)

    grad_kv = mm(r.fit[...], r.gkvt[...], 1, 1)
    for b in range(8):
        halves = [grad_kv[b * PIECE + i * PIECE // 2 : b * PIECE + (i + 1) * PIECE // 2] for i in range(2)]
        keep("k", b % 2, 0, 0, b // 2, jnp.concatenate(halves, axis=1))
    step(LATE_SCHEDULE[2])
    for i in range(width // LANES):
        columns = slice(i * LANES, (i + 1) * LANES)
        r.act[:, columns] = flip(r.gqt[columns, :]).astype(BF16)
    r.gh[:, :LANES] = flip(r.gkvt[...]).astype(BF16)

    first = mm(r.act[...], r.wq[:, :width], 1, 1) + mm(r.gh[:, :LANES], r.wq[:, width:], 1, 1)
    for i in range(width // LANES):
        (r.dk if i < parts else r.dv)[i % parts] = first[:, i * LANES : (i + 1) * LANES]
    sums = [jnp.zeros((1, width), F32) for _ in range(4)]
    for i in range(span // LANES):
        rows = pl.ds(i * LANES, LANES)
        normed, inverse_std = norm_tile(i)
        first = [(r.dk if j < parts else r.dv)[j % parts, rows, :] for j in range(width // LANES)]
        first, second = jnp.concatenate(first, axis=1), r.second[rows, :]
        for j, term in enumerate((normed * first, first, normed * second, second)):
            sums[j] = sums[j] + jnp.sum(term, axis=0, keepdims=True)
        scaled = first * r.g1[...][None] + second * r.g2[...][None]
        mean_one = jnp.mean(scaled, axis=-1, keepdims=True)
        mean_two = jnp.mean(scaled * normed, axis=-1, keepdims=True)
        back = inverse_std * (scaled - mean_one - normed * mean_two)
        r.si[rows, :] = (r.cot[rows, :].astype(F32) + back).astype(BF16)

    sum_qkv = jnp.concatenate([mm(ones_rows, r.gqt[:width, :], 1, 1), mm(ones_rows, r.gkvt[...], 1, 1)], axis=1)[0:1]
    sum_proj = mm(ones_rows, r.cot[...])[0:1]
    for b in range(8):
        lines = [cut(sum_qkv, b * 112, 112)]
        lines += [r.sum_fc[0:1, b * 384 + i * LANES : b * 384 + (i + 1) * LANES] for i in range(3)]
        lines += [cut(line, b * 96, 96) for line in (sum_proj, *sums)]
        lines.append(jnp.zeros((16 - len(lines), LANES), F32))
        lines = jnp.concatenate(lines, axis=0)
        keep("v", b % 2, 0, 0, b // 2, jnp.concatenate([lines, jnp.zeros_like(lines)], axis=1))
    step(LATE_SCHEDULE[3])
    copies = [pltpu.make_async_copy(r.si, r.input_grads, r.load_sem.at[0])]
    copies[0].start()

    for i in range(width // LANES):
        columns = slice(i * LANES, (i + 1) * LANES)
        r.fi[:, columns] = flip(r.attt[columns, :]).astype(BF16)
    r.x[...] = (r.result[...] + r.x[...].astype(F32) + r.bp[...][None] + mm(r.fi[...], r.wo[...])).astype(BF16)
    copies.append(pltpu.make_async_copy(r.x, r.outputs, r.load_sem.at[1]))
    copies[1].start()

    if inside:
        step(LATE_SCHEDULE[4])
        summing.close()
    else:
        copies.append(pltpu.make_async_copy(r.grads, r.grads_out, r.load_sem.at[2]))
        copies.append(pltpu.make_async_copy(r.wp.at[:, : 2 * BLOCK], r.late_out, r.load_sem.at[3]))
        for copy in copies[2:]:
            copy.start()
    for copy in copies:
        copy.wait()
    for distance in range(1, parts):
        kv_copy(r, mine, batch, parts, distance).wait_send()
        target = lax.rem(mine - distance + parts, parts)

        @pl.when(target <= high)
        def _():
            dkv_copy(r, mine, batch, parts, distance).wait_send()


    @pl.when(mine == parts - 1)
    def _():
        for copy in lent_copies(r, mine, batch, parts):
            copy.wait_send()

    @pl.when(mine == 0)
    def _():
        for copy in back_copies(r, mine, batch, parts):
            copy.wait_send()


def cut(line, start, size):
    line = jnp.concatenate([line, jnp.zeros((1, LANES), F32)], axis=1)
    base = start // LANES * LANES
    line = line[:, base : base + 2 * LANES]
    shift = start - base
    if shift:
        line = pltpu.roll(line, 2 * LANES - shift, 1)
    return jnp.where(lanes_of((1, LANES)) < size, line[:, :LANES], 0.0)


def rotate_back(r, grads, which):
    half = ROT // 2
    one, two = grads[:half], grads[half:ROT]
    cosine, sine = r.cos[which], r.sin[which]
    return jnp.concatenate([one * cosine + two * sine, two * cosine - one * sine, grads[ROT:]], axis=0)


def remote(src, dst, send_sem, recv_sem, peer):
    return pltpu.make_async_remote_copy(
        src_ref=src, dst_ref=dst, send_sem=send_sem, recv_sem=recv_sem, device_id=peer, device_id_type=MESH
    )


def lent_copies(r, mine, batch, parts):
    peer, rows, there = (parts - 1 - mine, batch), LENT * LANES, r.dot.shape[0] - LANES
    return [
        remote(r.lent, r.lent_in, r.lent_sem.at[0, 0], r.lent_sem.at[1, 0], peer),
        remote(
            r.dot.at[rows : rows + LANES],
            r.dot.at[there : there + LANES],
            r.lent_sem.at[0, 1],
            r.lent_sem.at[1, 1],
            peer,
        ),
    ]


def back_copies(r, mine, batch, parts):
    peer, rows, here = (parts - 1 - mine, batch), LENT * LANES, r.dot.shape[0] - LANES
    return [
        remote(ref.at[here : here + LANES], ref.at[rows : rows + LANES], r.back_sem.at[0, j], r.back_sem.at[1, j], peer)
        for j, ref in enumerate((r.attt, r.gqt))
    ]


class Summing:
    def __init__(self, r, mine, batch, parts):
        self.r, self.mine, self.batch, self.parts = r, mine, batch, parts
        y, x = mine // 2, lax.rem(mine, 2)
        self.z, self.core = batch // 2, lax.rem(batch, 2)
        self.axes = {"x": (x, (y * 2 + 1 - x, batch)), "y": (y, ((1 - y) * 2 + x, batch))}
        self.core_peer = (mine, self.z * 2 + 1 - self.core)
        self.z_peers = [(mine, lax.rem(self.z + i, 4) * 2 + self.core) for i in (1, 2, 3)]
        self.seq_peers = [(lax.rem(mine + i, parts), batch) for i in range(1, parts)]
        self.out_copies, self.sent = [], []

    def of(self, _):
        (y, y_peer), (x, x_peer) = self.axes["y"], self.axes["x"]
        p, s = jnp.where(self.core == 0, x, y), jnp.where(self.core == 0, y, x)
        part_x, part_y = x_peer[0], y_peer[0]
        first, then = jnp.where(self.core == 0, part_x, part_y), jnp.where(self.core == 0, part_y, part_x)
        return p, (first, self.batch), s, (then, self.batch)

    def copy(self, name, src, peer, to=None, sem=None):
        start, rows, index = INBOX[name]
        to = start if to is None else to
        return remote(
            src,
            self.r.inbox.at[pl.ds(to, rows)],
            self.r.sum_sem.at[0, index],
            self.r.sum_sem.at[1, index if sem is None else sem],
            peer,
        )

    def start(self, make, *args):
        make(*args).start()
        self.sent.append((make, *args))

    def rows(self, chunk, start, pieces):
        return chunk.ref(self.r).at[pl.ds(pl.multiple_of(start, 16), pieces * chunk.height)]

    def add(self, chunk, start, name, offset, pieces):
        ref, height, from_row = chunk.ref(self.r), chunk.height, INBOX[name][0] + offset

        def one(i, _):
            to = pl.ds(pl.multiple_of(start + i * height, 16), height)
            ref[to, :] += self.r.inbox[pl.ds(pl.multiple_of(from_row + i * height, 16), height), :]
            return 0

        lax.fori_loop(0, pieces, one, 0)

    def pair(self, chunk):
        rows = chunk.rows // 2
        src = chunk.ref(self.r).at[pl.ds(pl.multiple_of(chunk.base + (1 - self.core) * rows, 16), rows)]
        return self.copy("pair " + chunk.name, src, self.core_peer)

    def half(self, chunk):
        p, peer, _, _ = self.of(chunk)
        if chunk.kind == "line":
            return self.copy("half " + chunk.name, self.rows(chunk, chunk.place(self.core, 1 - p, 0, self.z), 2), peer)
        src = self.rows(chunk, chunk.place(self.core, 1 - p, 0, 0), 2 * chunk.count)
        return self.copy("half " + chunk.name, src, peer)

    def quarter(self, chunk):
        p, _, s, peer = self.of(chunk)
        if chunk.kind == "line":
            src = self.rows(chunk, chunk.place(self.core, p, 1 - s, self.z), 1)
        else:
            src = self.rows(chunk, chunk.place(self.core, p, 1 - s, 0), chunk.count)
        return self.copy("quarter " + chunk.name, src, peer)

    def mine_of(self, chunk, z):
        p, _, s, _ = self.of(chunk)
        if chunk.kind in ("line", "whole"):
            return chunk.place(self.core, 0, 0, z)
        return chunk.place(self.core, p, s, 0 if chunk.kind == "plane" else z)

    def pieces(self, chunk):
        return {"plane": chunk.count, "line": 4}.get(chunk.kind, 1)

    def line(self, chunk, i):
        z = lax.rem(self.z + i, 4)
        src = self.rows(chunk, self.mine_of(chunk, z), self.pieces(chunk))
        return self.copy(f"line{i} " + chunk.name, src, self.z_peers[i - 1])

    def plane_line(self, chunk):
        z = int(chunk.name[1:])
        i = lax.rem(z - self.z + 4, 4)
        start, rows, index = INBOX["line1 p"]
        src = self.rows(chunk, self.mine_of(chunk, z), chunk.count)
        return remote(
            src,
            self.r.inbox.at[pl.ds(pl.multiple_of(start + (i - 1) * rows, 16), rows)],
            self.r.sum_sem.at[0, INBOX["line " + chunk.name][2]],
            self.r.sum_sem.at[1, index + i - 1],
            (self.mine, z * 2 + self.core),
        )

    def near(self, name):
        own, rows, _ = INBOX["share0 " + name]
        start, _, index = INBOX["share1 " + name]
        sem = self.r.sum_sem
        return remote(
            self.r.inbox.at[pl.ds(own, rows)],
            self.r.inbox.at[pl.ds(start, rows)],
            sem.at[0, index],
            sem.at[1, index],
            self.of(None)[1],
        )

    def far(self, name):
        own, rows, _ = INBOX["share0 " + name]
        start, _, index = INBOX["share2 " + name]
        sem = self.r.sum_sem
        return remote(
            self.r.inbox.at[pl.ds(own, 2 * rows)],
            self.r.inbox.at[pl.ds(start, 2 * rows)],
            sem.at[0, index],
            sem.at[1, index],
            self.of(None)[3],
        )

    def share(self, name, i):
        start, rows, index = INBOX[f"share{i} " + name]
        own = INBOX["share0 " + name][0]
        return remote(
            self.r.inbox.at[pl.ds(own, rows)],
            self.r.inbox.at[pl.ds(start, rows)],
            self.r.sum_sem.at[0, index],
            self.r.sum_sem.at[1, index],
            self.seq_peers[i - 1],
        )

    def send(self, chunk):
        order = list(CHUNKS).index(chunk.name)
        if order >= SLOTS:
            pl.semaphore_wait(self.r.free_sem.at[order % SLOTS], 1)
        self.start(self.pair, chunk)

    def a(self, chunk):
        self.pair(chunk).wait_recv()
        name, base, p = "pair " + chunk.name, self.core * (chunk.rows // 2), self.of(chunk)[0]
        if chunk.kind in ("line", "whole"):
            pieces = self.pieces(chunk)
            for i in (1, 2, 3, 0):
                start = self.mine_of(chunk, lax.rem(self.z + i, 4))
                self.add(chunk, start, name, start - chunk.base - base, pieces)
                if i:
                    self.start(self.line, chunk, i)
        else:
            for side in (1 - p, p):
                start = chunk.place(self.core, side, 0, 0)
                self.add(chunk, start, name, start - chunk.base - base, 2 * chunk.count)
                if side is not p:
                    self.start(self.half, chunk)
        order = list(CHUNKS).index(chunk.name)
        if order + SLOTS < len(CHUNKS):
            free = self.r.free_sem.at[order % SLOTS]
            pl.semaphore_signal(free, inc=1, device_id=self.core_peer, device_id_type=MESH)

    def total(self, chunk, name, start, pieces):
        rows = pieces * chunk.height
        total = chunk.ref(self.r)[pl.ds(pl.multiple_of(start, 16), rows), :].astype(F32)
        for i in (1, 2, 3):
            at = INBOX[f"line{i} " + name][0]
            total = total + self.r.inbox[at : at + rows, :].astype(F32)
        return total.astype(BF16)

    def give(self, name, value):
        own, rows, _ = INBOX["share0 " + name]
        self.r.inbox[own : own + rows, :] = value
        if name in TWO_STEPS:
            self.start(self.near, name)
            return
        for i in (1, 2, 3):
            self.start(self.share, name, i)

    def g(self, chunk):
        name = "p" if chunk.kind == "plane" else chunk.name
        self.near(name).wait_recv()
        self.start(self.far, name)

    def b(self, chunk):
        p, _, s, _ = self.of(chunk)
        if chunk.kind == "line":
            for i in (1, 2, 3):
                self.line(chunk, i).wait_recv()
            start = self.mine_of(chunk, self.z)
            self.rows(chunk, start, 4)[...] = self.total(chunk, chunk.name, start, 4)
            self.start(self.half, chunk)
            return
        self.half(chunk).wait_recv()
        for side in (1 - s, s):
            offset = side * chunk.count * chunk.height
            self.add(chunk, chunk.place(self.core, p, side, 0), "half " + chunk.name, offset, chunk.count)
            if side is not s:
                self.start(self.quarter, chunk)

    def c(self, chunk):
        p, _, s, _ = self.of(chunk)
        if chunk.kind == "line":
            self.half(chunk).wait_recv()
            for side in (1 - s, s):
                self.add(chunk, chunk.place(self.core, p, side, self.z), "half " + chunk.name, side * chunk.height, 1)
                if side is not s:
                    self.start(self.quarter, chunk)
            return
        self.quarter(chunk).wait_recv()
        name = "quarter " + chunk.name
        if chunk.kind == "plane":
            self.add(chunk, chunk.place(self.core, p, s, 0), name, 0, chunk.count)


            @pl.when(self.z != int(chunk.name[1:]))
            def _():
                self.plane_line(chunk).start()

            return
        for i in (1, 2, 3, 0):
            z = lax.rem(self.z + i, 4)
            self.add(chunk, chunk.place(self.core, p, s, z), name, z * chunk.height, 1)
            if i:
                self.start(self.line, chunk, i)

    def d(self, chunk):
        if chunk.kind == "line":
            p, _, s, _ = self.of(chunk)
            self.quarter(chunk).wait_recv()
            start = chunk.place(self.core, p, s, self.z)
            arrived = INBOX["quarter " + chunk.name][0]
            own = chunk.ref(self.r)[pl.ds(pl.multiple_of(start, 16), PIECE), :]
            self.give(chunk.name, own + self.r.inbox[arrived : arrived + PIECE, :])
            return
        for i in (1, 2, 3):
            self.line(chunk, i).wait_recv()
        self.give(chunk.name, self.total(chunk, chunk.name, self.mine_of(chunk, self.z), 1))

    def d_planes(self, _):
        r, (start, rows, index) = self.r, INBOX["line1 p"]
        p, _, s, _ = self.of(None)
        total = jnp.zeros((rows, BLOCK), F32)
        for z in range(4):
            here = pl.multiple_of(CHUNKS[f"p{z}"].place(self.core, p, s, 0), 16)
            total = jnp.where(self.z == z, r.grads[pl.ds(here, rows), :].astype(F32), total)
        for i in (1, 2, 3):
            at = start + (i - 1) * rows
            arrived = r.inbox.at[at : at + rows]
            remote(arrived, arrived, r.sum_sem.at[0, index], r.sum_sem.at[1, index + i - 1], self.z_peers[3 - i]).wait_recv()
            total = total + arrived[...].astype(F32)
        self.give("p", total.astype(BF16))

    def quarters(self, name):
        refs = [self.r.inbox.at[pl.ds(*INBOX[f"share{i} " + name][:2])] for i in range(4)]
        if name in TWO_STEPS:
            self.far(name).wait_recv()
            _, first, _, then = self.of(None)
            return zip((self.mine, first[0], then[0], 3 - self.mine), refs)
        for i in (1, 2, 3):
            self.share(name, i).wait_recv()
        return zip([lax.rem(self.mine + 4 - i, 4) for i in range(4)], refs)

    def e(self, chunk):
        r, name = self.r, chunk.name
        plane = chunk.kind == "plane"
        arrived = self.quarters("p" if plane else name)
        if chunk.kind == "whole":
            total = functools.reduce(jnp.add, [ref[...].astype(F32) for _, ref in arrived])
            if name == "k":
                for i in range(2):
                    rows = slice(384 + i * PIECE // 2, 384 + (i + 1) * PIECE // 2)
                    r.scores[rows, 768 : 768 + LANES] = total[:, i * LANES : (i + 1) * LANES]
                self.write(r.scores.at[384 : 384 + PIECE, : r.grad_qkv.shape[1]], r.grad_qkv)
                return
            r.grad_bq[...] = total[0, : r.grad_bq.shape[0]]
            for i in range(3):
                r.grad_bfc[i * LANES : (i + 1) * LANES] = total[1 + i, :LANES]
            for i, out in enumerate((r.grad_bp, r.grad_g1, r.grad_s1, r.grad_g2, r.grad_s2)):
                out[...] = total[4 + i, : out.shape[0]]
            return
        for part, ref in arrived:
            y, x = part // 2, lax.rem(part, 2)
            value = ref[...].astype(F32)
            if plane:
                for i in range(3):
                    to = pl.ds(pl.multiple_of(part * PIECE, PIECE), PIECE)
                    r.scores[to, i * BLOCK : (i + 1) * BLOCK] = value[i * PIECE : (i + 1) * PIECE]
            elif name in ("f0", "f1", "f2"):
                top = int(name[1]) * PIECE
                columns = pl.ds(pl.multiple_of(768 + part * BLOCK, BLOCK), BLOCK)
                r.scores[top : top + PIECE, columns] = value
            elif name == "uc":
                rows = pl.ds(pl.multiple_of(384 + y * PIECE // 2, 16), PIECE // 2)
                r.scores[rows, pl.ds(pl.multiple_of((1 + x) * BLOCK, BLOCK), BLOCK)] = value
            else:
                low = name == "ub"
                top = jnp.where(part == 3, 384, 288) + low * PIECE // 2
                left = jnp.where(part == 3, 0, 768 + part * BLOCK)
                rows = pl.ds(pl.multiple_of(top, 16), PIECE // 2)
                r.scores[rows, pl.ds(pl.multiple_of(left, BLOCK), BLOCK)] = value
        if plane:
            self.write(r.scores.at[:384, :768], r.grad_proj)
        elif name in ("f0", "f1", "f2"):
            k = int(name[1])
            src = r.scores.at[k * PIECE : (k + 1) * PIECE, 768 : 768 + 4 * BLOCK]
            self.write(src, r.grad_fc.at[:, 4 * k * BLOCK : 4 * (k + 1) * BLOCK])
        elif name == "ub":
            self.write(r.scores.at[288 : 288 + PIECE, 768 : 768 + 768], r.grad_o)

    def write(self, src, dst):
        copy = pltpu.make_async_copy(src, dst, self.r.out_sem.at[len(self.out_copies)])
        copy.start()
        self.out_copies.append(copy)

    def close(self):
        for copy in self.out_copies:
            copy.wait()
        for make, *args in self.sent:
            make(*args).wait_send()
        for z in range(4):

            @pl.when(self.z != z)
            def _():
                self.plane_line(CHUNKS[f"p{z}"]).wait_send()


TWO_STEPS = ("p", "f0", "f1", "f2")


def make_inbox():
    inbox, rows = {}, SLOTS * 16 * PIECE

    def add(name, count, start=None):
        nonlocal rows
        if start is None:
            start = rows
            rows += count
        inbox[name] = (start, count, len(inbox))

    for order, chunk in enumerate(CHUNKS.values()):
        name, piece = chunk.name, chunk.height
        add("pair " + name, chunk.rows // 2, order % SLOTS * 16 * PIECE)
        if chunk.kind == "plane":
            add("half " + name, 2 * chunk.count * piece)
            add("quarter " + name, chunk.count * piece)
            add("line " + name, chunk.count * piece, 0)
            continue
        if chunk.kind != "whole":
            count = 1 if chunk.kind == "line" else 4
            add("half " + name, 2 * count * piece)
            add("quarter " + name, count * piece)
        for i in (1, 2, 3):
            add(f"line{i} " + name, (4 if chunk.kind == "line" else 1) * piece)
        for i in range(4):
            add(f"share{i} " + name, piece)
    for i in (1, 2, 3):
        add(f"line{i} p", 3 * PIECE)
    for i in range(4):
        add(f"share{i} p", 3 * PIECE)
    return inbox, rows


INBOX, INBOX_ROWS = make_inbox()


def kv_copy(r, source, batch, parts, distance):
    peer = (lax.rem(source + distance, parts), batch)
    return remote(r.kv.at[source], r.kv.at[source], r.kv_sem.at[0, distance], r.kv_sem.at[1, distance], peer)


def dkv_copy(r, mine, batch, parts, distance):
    peer = (lax.rem(mine - distance + parts, parts), batch)
    return remote(
        r.dkv_out.at[distance], r.dkv_in.at[distance], r.dkv_sem.at[0, distance], r.dkv_sem.at[1, distance], peer
    )


def hand_out_kernel(count, *refs):
    sources, targets, held, sem = refs[:count], refs[count : 2 * count], refs[2 * count : -1], refs[-1]
    large = [i for i in range(count) if sources[i].ndim > 1]
    copies = [
        (
            pltpu.make_async_copy(sources[i], held[j], sem.at[0, j]),
            pltpu.make_async_copy(held[j], targets[i], sem.at[1, j]),
        )
        for j, i in enumerate(large)
    ]
    for here, _ in copies:
        here.start()
    for source, target in zip(sources, targets):
        if source.ndim == 1:
            target[...] = source[...]
    for here, there in copies:
        here.wait()
        there.start()
    for _, there in copies:
        there.wait()


def hand_out(results, specs):
    large = [pltpu.VMEM(item.shape, item.dtype) for item in results if item.ndim > 1]
    return pl.pallas_call(
        functools.partial(hand_out_kernel, len(results)),
        out_shape=[jax.ShapeDtypeStruct(item.shape, item.dtype) for item in results],
        in_specs=specs,
        out_specs=specs,
        scratch_shapes=[*large, pltpu.SemaphoreType.DMA((2, len(large)))],
        name="hand_out",
    )(*results)


def per_device(inputs, doc_ids, w_qkv, b_qkv, w_o, w_fc, b_fc, w_proj, b_proj, gain_one, shift_one, gain_two, shift_two, cotangent):
    rows_here, span, width = inputs.shape
    assert rows_here == 1
    parts = lax.axis_size("seq")
    heads = width // HEAD
    hidden_units = w_fc.shape[1]
    merged = width + 2 * HEAD
    inside = parts == 4 and lax.axis_size("batch") == 8
    vmem = pl.BlockSpec(memory_space=pltpu.VMEM)
    anywhere = pl.BlockSpec(memory_space=pl.ANY)

    small = dict(docs=doc_ids, bq=b_qkv, bfc=b_fc, bp=b_proj, g1=gain_one, s1=shift_one, g2=gain_two, s2=shift_two)
    large = dict(x_h=inputs[0], cot_h=cotangent[0], wq_h=w_qkv, wo_h=w_o, wfc_h=w_fc, wp_h=w_proj)
    outs = dict(outputs=((span, width), BF16, anywhere), input_grads=((span, width), BF16, anywhere))
    if inside:
        outs |= dict(
            grad_qkv=((width // 8, merged), F32, anywhere),
            grad_bq=((merged // 8,), F32, vmem),
            grad_o=((width // 8, width), F32, anywhere),
            grad_fc=((width // 8, hidden_units), F32, anywhere),
            grad_bfc=((hidden_units // 8,), F32, vmem),
            grad_proj=((hidden_units // 8, width), F32, anywhere),
            grad_bp=((width // 8,), F32, vmem),
            grad_g1=((width // 8,), F32, vmem),
            grad_s1=((width // 8,), F32, vmem),
            grad_g2=((width // 8,), F32, vmem),
            grad_s2=((width // 8,), F32, vmem),
        )
    else:
        outs |= dict(grads_out=((GRAD_ROWS, BLOCK), BF16, anywhere), late_out=((hidden_units, 2 * BLOCK), BF16, anywhere))
    scratch = dict(
        x=pltpu.VMEM((span, width), BF16),
        cot=pltpu.VMEM((span, width), BF16),
        wq=pltpu.VMEM((width, merged), BF16),
        wo=pltpu.VMEM((width, width), BF16),
        wfc=pltpu.VMEM((width, hidden_units), BF16),
        wp=pltpu.VMEM((hidden_units, width), BF16),
        fi=pltpu.VMEM((span, width), BF16),
        si=pltpu.VMEM((span, width), BF16),
        fit=pltpu.VMEM((width, span), BF16),
        sit=pltpu.VMEM((width, span), BF16),
        cos=pltpu.VMEM((2, ROT // 2, span), F32),
        sin=pltpu.VMEM((2, ROT // 2, span), F32),
        kv=pltpu.VMEM((parts, span, LANES), BF16),
        q=pltpu.VMEM((heads + 2, span, LANES), BF16),
        qt=pltpu.VMEM((heads + 2, LANES, span), BF16),
        lent=pltpu.VMEM((span, LANES), BF16),
        lent_in=pltpu.VMEM((span, LANES), BF16),
        dot=pltpu.VMEM((width + 2 * HEAD, span), BF16),
        act=pltpu.VMEM((span, width), BF16),
        gh=pltpu.VMEM((span, width), BF16),
        result=pltpu.VMEM((span, width), F32),
        second=pltpu.VMEM((span, width), F32),
        sum_fc=pltpu.VMEM((8, hidden_units), F32),
        kx=pltpu.VMEM((parts, span, LANES), BF16),
        kxt=pltpu.VMEM((parts, LANES, span), BF16),
        vx=pltpu.VMEM((parts, span, LANES), BF16),
        vxt=pltpu.VMEM((parts, LANES, span), BF16),
        dk=pltpu.VMEM((parts, span, LANES), F32),
        dv=pltpu.VMEM((parts, span, LANES), F32),
        scores=pltpu.VMEM((span, parts * span), F32),
        ga=pltpu.VMEM((LANES, span), BF16),
        gat=pltpu.VMEM((span, LANES), BF16),
        attt=pltpu.VMEM((width + 2 * HEAD, span), BF16),
        gqt=pltpu.VMEM((width + 2 * HEAD, span), BF16),
        gkvt=pltpu.VMEM((2 * HEAD, span), BF16),
        dkv_out=pltpu.VMEM((parts, span, LANES), BF16),
        dkv_in=pltpu.VMEM((parts, span, LANES), BF16),
        total=pltpu.VMEM((span, LANES), F32),
        grads=pltpu.VMEM((GRAD_ROWS, BLOCK), BF16),
        load_sem=pltpu.SemaphoreType.DMA((6,)),
        kv_sem=pltpu.SemaphoreType.DMA((2, parts)),
        dkv_sem=pltpu.SemaphoreType.DMA((2, parts)),
        lent_sem=pltpu.SemaphoreType.DMA((2, 2)),
        back_sem=pltpu.SemaphoreType.DMA((2, 2)),
    )
    if inside:
        scratch |= dict(
            inbox=pltpu.VMEM((INBOX_ROWS, BLOCK), BF16),
            sum_sem=pltpu.SemaphoreType.DMA((2, len(INBOX))),
            out_sem=pltpu.SemaphoreType.DMA((6,)),
            free_sem=pltpu.SemaphoreType.REGULAR((SLOTS,)),
        )
    names = [*small, *large, *outs, *scratch]
    results = pl.pallas_call(
        functools.partial(layer_kernel, names, parts, inside),
        out_shape=[jax.ShapeDtypeStruct(shape, dtype) for shape, dtype, _ in outs.values()],
        in_specs=[vmem] * len(small) + [anywhere] * len(large),
        out_specs=[spec for _, _, spec in outs.values()],
        scratch_shapes=list(scratch.values()),
        compiler_params=pltpu.CompilerParams(
            collective_id=0, has_side_effects=True, vmem_limit_bytes=63 * 2**20
        ),
        name="layer",
    )(*small.values(), *large.values())
    if inside:
        outputs, input_grads, *shards = hand_out(results, [spec for _, _, spec in outs.values()])
        return (outputs[None], input_grads[None], *shards)
    outputs, input_grads, *shards = results

    grads, late = shards
    planes = [CHUNKS[f"p{z}"].unfold(grads).transpose(0, 1, 2, 4, 3, 5).reshape(-1, width) for z in range(4)]
    proj = jnp.concatenate(planes)
    columns = [
        CHUNKS[name].unfold(grads).transpose(3, 0, 4, 1, 2, 5).reshape(width, 4 * BLOCK) for name in ("f0", "f1", "f2")
    ]
    fc = jnp.concatenate(columns, axis=1)
    halves = [CHUNKS[name].unfold(late[:, :BLOCK]).transpose(3, 0, 4, 1, 2, 5) for name in ("ua", "ub")]
    both = jnp.stack(halves, axis=2).reshape(width, 4 * BLOCK)
    o = both[:, :width]
    rest = CHUNKS["uc"].unfold(late[:, BLOCK:]).transpose(3, 0, 1, 4, 2, 5).reshape(width, 2 * BLOCK)
    last = CHUNKS["k"].unfold(late[:, BLOCK:]).reshape(2, 4, PIECE // 2, 2, LANES).transpose(1, 0, 3, 2, 4)
    qkv = jnp.concatenate([both[:, width:], rest, last.reshape(width, LANES)], axis=1)
    blocks = 8
    lines = CHUNKS["v"].unfold(late[:, BLOCK:]).transpose(1, 0, 2, 3).reshape(blocks, 16, BLOCK)[..., :LANES]
    vectors = [lines[:, 0, : merged // blocks], lines[:, 1:4]] + [lines[:, i, : width // blocks] for i in range(4, 9)]
    vectors = [vector.reshape(-1) for vector in vectors]
    every = [qkv, vectors[0], o, fc, vectors[1], proj, *vectors[2:]]
    shards = [lax.psum_scatter(item, "batch", scatter_dimension=0, tiled=True) for item in every]
    shards = [lax.psum(item, "seq").astype(F32) for item in shards]
    return (outputs[None], input_grads[None], *shards)


def solution(mesh):
    whole, part = P(), P("batch", "seq", None)
    in_specs = (part, P("batch", None), *[whole] * 11, part)
    matrix, vector = P("batch", None), P("batch")
    out_specs = (part, part, matrix, vector, matrix, matrix, vector, matrix, *[vector] * 5)
    return jax.shard_map(per_device, mesh=mesh, in_specs=in_specs, out_specs=out_specs, check_vma=False)
```

```python
import functools
import math
import types

import jax
import jax.numpy as jnp
import numpy as np
from jax import lax
from jax.experimental import pallas as pl
from jax.experimental.pallas import tpu as pltpu
from jax.sharding import PartitionSpec as P

HEAD = 64
ROT = 16
EPSILON = 1e-05
LANES = 128
BLOCK = 256
FAR = -1e30
LOG2E = math.log2(math.e)
MESH = pl.DeviceIdType.MESH
F32 = jnp.float32
BF16 = jnp.bfloat16

PIECE = 96
SLOTS = 4


class Chunk:
    def __init__(self, name, kind, height, count, base, lane):
        self.name, self.kind = name, kind
        self.height, self.count, self.base, self.lane = height, count, base, lane

    @property
    def rows(self):
        return self.height * self.count * (2 if self.kind == "whole" else 8)

    def place(self, core, p, s, i):
        if self.kind == "whole":
            at = core * 4 + i
        elif self.kind == "line":
            at = ((core * 4 + i) * 2 + p) * 2 + s
        else:
            at = ((core * 2 + p) * 2 + s) * self.count + i
        return self.base + at * self.height

    def ref(self, r):
        if self.lane is None:
            return r.grads
        return r.wp.at[:, self.lane * BLOCK : (self.lane + 1) * BLOCK]

    @staticmethod
    def split(core, y, x):
        return (y, x) if core else (x, y)

    def unfold(self, array):
        array = array[self.base : self.base + self.rows]
        if self.kind == "whole":
            return array.reshape(2, 4, self.height, BLOCK)
        if self.kind == "line":
            array = array.reshape(2, 4, 2, 2, self.height, BLOCK).transpose(0, 2, 3, 1, 4, 5)
        else:
            array = array.reshape(2, 2, 2, self.count, self.height, BLOCK)
        return jnp.stack([array[0].swapaxes(0, 1), array[1]])


def make_chunks():
    plans = [
        ("p0", "plane", PIECE, 3, None),
        ("p1", "plane", PIECE, 3, None),
        ("f0", "line", PIECE, 4, None),
        ("p2", "plane", PIECE, 3, None),
        ("f1", "block", PIECE, 4, None),
        ("p3", "plane", PIECE, 3, None),
        ("f2", "block", PIECE, 4, None),
        ("uc", "block", PIECE // 2, 4, 1),
        ("ua", "block", PIECE // 2, 4, 0),
        ("ub", "block", PIECE // 2, 4, 0),
        ("k", "whole", PIECE // 2, 4, 1),
        ("v", "whole", 16, 4, 1),
    ]
    chunks, filled = {}, {}
    for name, kind, height, count, lane in sorted(plans, key=lambda plan: plan[1] != "plane"):
        chunk = Chunk(name, kind, height, count, filled.get(lane, 0), lane)
        chunks[name] = chunk
        filled[lane] = chunk.base + chunk.rows
    return {plan[0]: chunks[plan[0]] for plan in plans}, filled[None]


CHUNKS, GRAD_ROWS = make_chunks()


def mm(a, b, ca=1, cb=0):
    return lax.dot_general(a, b, (((ca,), (cb,)), ((), ())), preferred_element_type=F32)


def flip(value):
    return value.astype(F32).T


def lanes_of(shape):
    return lax.broadcasted_iota(jnp.int32, shape, 1)


def rows_of(shape):
    return lax.broadcasted_iota(jnp.int32, shape, 0)


EARLY_DONE = 64

FEED_SCHEDULE = [
    ([], ["send:p0"], []),
    (["a:p0"], [], ["send:p1", "send:f0"]),
    (["a:f0", "a:p1"], ["send:p2"], ["send:f1"]),
    (["b:p0"], ["a:f1", "send:p3"], []),
    [],
]

SCHEDULE = {
    4: ["a:p2", "send:f2"],
    12: ["c:p0", "a:f2"],
    16: ["b:f1"],
    20: ["a:p3"],
    28: ["b:f2"],
    32: ["c:f1"],
    36: ["b:f0", "b:p2"],
    44: ["c:f2", "b:p1"],
    48: ["c:f0"],
    60: ["b:p3", "d:f1"],
    EARLY_DONE: ["make:uc", "d:f2", "send:uc", "c:p1"],
    68: ["c:p2", "a:uc"],
    72: ["g:f2", "c:p3", "g:f1"],
    76: ["b:uc", "d:f0"],
}

LATE_SCHEDULE = [
    [],
    ["send:ua", "c:uc", "e:f1", "a:ua", "e:f2", "send:ub", "a:ub"],
    ["send:k", "b:ua", "g:f0", "a:k"],
    ["b:ub", "send:v", "d_planes:p0", "c:ua", "d:uc", "a:v", "c:ub", "d:k", "e:f0", "g:p0", "d:ua", "d:v", "d:ub"],
    ["e:uc", "e:v", "e:ua", "e:p0", "e:ub", "e:k"],
]

LENT = 5


def gelu_parts(hidden):
    size = jnp.abs(hidden)
    t = pl.reciprocal(1.0 + (0.3275911 / math.sqrt(2.0)) * size)
    bell = jnp.exp2(hidden * hidden * (-0.5 * LOG2E))
    poly = 0.5 * 1.061405429
    for term in (-1.453152027, 1.421413741, -0.284496736, 0.254829592):
        poly = poly * t + 0.5 * term
    tail = poly * t * bell
    below = jnp.where(hidden >= 0, 1.0 - tail, tail)
    return below, hidden * bell * (1.0 / math.sqrt(2.0 * math.pi))


def layer_kernel(names, parts, inside, *refs):
    r = types.SimpleNamespace(**dict(zip(names, refs, strict=True)))
    span, width = r.x.shape
    hidden_units = r.wfc.shape[1]
    heads = width // HEAD
    mine = lax.axis_index("seq")
    batch = lax.axis_index("batch")
    partner = parts - 1 - mine
    high = jnp.maximum(mine, partner)

    loads = [
        pltpu.make_async_copy(src, dst, r.load_sem.at[i])
        for i, (src, dst) in enumerate(
            [(r.x_h, r.x), (r.wq_h, r.wq), (r.cot_h, r.cot), (r.wo_h, r.wo), (r.wfc_h, r.wfc), (r.wp_h, r.wp)]
        )
    ]
    for load in loads:
        load.start()

    barrier = pltpu.get_barrier_semaphore()
    peers = [(lax.rem(mine + distance, parts), batch) for distance in range(1, parts)]
    summing = Summing(r, mine, batch, parts) if inside else None
    if inside:
        peers += [summing.core_peer, *summing.z_peers]
    for peer in peers:
        pl.semaphore_signal(barrier, inc=1, device_id=peer, device_id_type=MESH)
    pl.semaphore_wait(barrier, len(peers))

    def keep(name, core, y, x, i, value):
        chunk = CHUNKS[name]
        row = chunk.place(core, *chunk.split(core, y, x), i)
        chunk.ref(r)[row : row + chunk.height, :] = value.astype(BF16)

    def step(steps):
        for item in steps if inside else ():
            kind, name = item.split(":")
            if kind == "make":
                make_early()
            else:
                getattr(summing, kind)(CHUNKS[name])

    loads[0].wait()

    def norm_tile(i):
        tokens = r.x[pl.ds(i * LANES, LANES), :].astype(F32)
        average = jnp.mean(tokens, axis=-1, keepdims=True)
        centered = tokens - average
        variance = jnp.mean(centered * centered, axis=-1, keepdims=True)
        inverse_std = lax.rsqrt(variance + EPSILON)
        return centered * inverse_std, inverse_std

    for i in range(span // LANES):
        normed, _ = norm_tile(i)
        rows = pl.ds(i * LANES, LANES)
        first = normed * r.g1[...][None] + r.s1[...][None]
        second = normed * r.g2[...][None] + r.s2[...][None]
        r.fi[rows, :] = first.astype(BF16)
        r.si[rows, :] = second.astype(BF16)
        r.fit[:, rows] = first.T.astype(BF16)
        r.sit[:, rows] = second.T.astype(BF16)

    half = ROT // 2
    index = rows_of((half, span))
    frequency = jnp.zeros((half, span), F32)
    for i in range(half):
        frequency = jnp.where(index == i, np.float32(10000.0 ** (-2.0 * i / ROT)), frequency)
    for i, part in enumerate((mine, partner)):
        angle = (part * span + lanes_of((half, span))).astype(F32) * frequency
        r.cos[i] = jnp.cos(angle)
        r.sin[i] = jnp.sin(angle)
    cosine, sine = r.cos[0], r.sin[0]
    ones = jnp.ones((HEAD - ROT, span), F32)
    zeros = jnp.zeros((HEAD - ROT, span), F32)
    table_cos = jnp.concatenate([cosine, cosine, ones] * 2, axis=0).T
    table_sin = jnp.concatenate([-sine, sine, zeros] * 2, axis=0).T
    lane = lanes_of((span, LANES))

    def rotate(tile, cos_of, sin_of):
        partner = jnp.where(
            lax.rem(lane, HEAD) < half, pltpu.roll(tile, LANES - half, 1), pltpu.roll(tile, half, 1)
        )
        return tile * cos_of + partner * sin_of

    def docs_row(part):
        return r.docs[0:1, pl.ds(pl.multiple_of(part * span, LANES), span)]

    loads[1].wait()
    key_value = mm(r.fi[...], r.wq[:, width:]) + r.bq[width:][None]
    low = lane < HEAD
    key_value = rotate(key_value, jnp.where(low, table_cos, 1.0), jnp.where(low, table_sin, 0.0))
    r.kv[mine] = key_value.astype(BF16)
    for distance in range(1, parts):
        kv_copy(r, mine, batch, parts, distance).start()

    feature_row = rows_of((LANES, span)) - HEAD

    def keep_queries(slot, tile, feature):
        for i, head in enumerate((tile, pltpu.roll(tile, HEAD, 1))):
            head = jnp.where(low, head, feature)
            r.q[slot + i] = head.astype(BF16)
            r.qt[slot + i] = head.T.astype(BF16)

    query_feature = jnp.where(feature_row == docs_row(mine), 1.0, 0.0).T
    for i in range(heads // 2):
        columns = slice(i * LANES, (i + 1) * LANES)
        tile = mm(r.fi[...], r.wq[:, columns]) + r.bq[columns][None]
        tile = rotate(tile, table_cos, table_sin) * (LOG2E / math.sqrt(HEAD))
        keep_queries(2 * i, tile, query_feature)
        if i == LENT:
            r.lent[...] = tile.astype(BF16)

    loads[2].wait()
    loads[3].wait()
    for i in range(width // BLOCK):
        rows = slice(i * BLOCK, (i + 1) * BLOCK)
        r.dot[rows, :] = mm(r.wo[rows, :], r.cot[...], 1, 1).astype(BF16)

    @pl.when(mine == parts - 1)
    def _():
        for copy in lent_copies(r, mine, batch, parts):
            copy.start()


    loads[4].wait()
    loads[5].wait()
    r.result[...] = jnp.zeros_like(r.result)
    r.second[...] = jnp.zeros_like(r.second)
    ones_rows = jnp.ones((8, span), BF16)
    group = 2 * 4 * 96

    def feed_steps(g, i):
        for group_of, steps in enumerate(FEED_SCHEDULE[:-1]):
            if steps[i]:

                @pl.when(g == group_of)
                def _():
                    step(steps[i])

    plane, line, block = CHUNKS["p0"], CHUNKS["f0"], CHUNKS["f1"]

    def feed_forward(g, _):
        columns = pl.ds(pl.multiple_of(g * group, LANES), group)
        hidden = mm(r.si[...], r.wfc[:, columns]) + r.bfc[columns][None]
        grad_act = mm(r.cot[...], r.wp[columns, :], 1, 1)
        below, slope = gelu_parts(hidden)
        r.act[...] = (hidden * below).astype(BF16)
        r.gh[...] = (grad_act * (below + slope)).astype(BF16)
        feed_steps(g, 0)
        grad_w = mm(r.act[...], r.cot[...], 0, 0)
        for c in range(2):
            for q in range(4):
                row = (c * 4 + q) * PIECE
                for k in range(3):
                    to = g * plane.rows + plane.place(c, *plane.split(c, q // 2, q % 2), k)
                    piece = grad_w[row : row + PIECE, k * BLOCK : (k + 1) * BLOCK]
                    r.grads[pl.ds(pl.multiple_of(to, 16), PIECE), :] = piece.astype(BF16)
        feed_steps(g, 1)
        grad_w = mm(r.sit[...], r.gh[...])
        for k in range(group // BLOCK):
            at = g * (group // BLOCK) + k
            chunk, y, x = at // 4, lax.rem(at, 4) // 2, lax.rem(at, 2)
            for b in range(8):
                c, z = b % 2, b // 2
                p, s = line.split(c, y, x)
                later = block.place(c, p, s, z) + (chunk - 1) * block.rows
                to = jnp.where(chunk == 0, line.place(c, p, s, z), later)
                piece = grad_w[b * PIECE : (b + 1) * PIECE, k * BLOCK : (k + 1) * BLOCK]
                r.grads[pl.ds(pl.multiple_of(to, 16), PIECE), :] = piece.astype(BF16)
        feed_steps(g, 2)
        r.sum_fc[:, columns] = mm(ones_rows, r.gh[...])
        r.result[...] += mm(r.act[...], r.wp[columns, :])
        r.second[...] += mm(r.gh[...], r.wfc[:, columns], 1, 1)
        return 0

    lax.fori_loop(0, hidden_units // group, feed_forward, 0)
    step(FEED_SCHEDULE[4])

    for distance in range(1, parts):
        kv_copy(r, lax.rem(mine - distance + parts, parts), batch, parts, distance).wait_recv()
    for part in range(parts):
        apart = (feature_row >= 0) & (feature_row < 8) & (feature_row != docs_row(part))
        key_feature = jnp.where(apart, FAR, 0.0).T
        pair = r.kv[part].astype(F32)
        keys = jnp.where(low, pair, key_feature)
        values = jnp.where(low, pltpu.roll(pair, HEAD, 1), jnp.where(lane < HEAD + 2, 1.0, 0.0))
        r.kx[part] = keys.astype(BF16)
        r.kxt[part] = keys.T.astype(BF16)
        r.vx[part] = values.astype(BF16)
        r.vxt[part] = values.T.astype(BF16)

    @pl.when(mine == 0)
    def _():
        for copy in lent_copies(r, mine, batch, parts):
            copy.wait_recv()
        feature = jnp.where(feature_row == docs_row(partner), 1.0, 0.0).T
        keep_queries(heads, r.lent_in[...].astype(F32), feature)

    r.dk[...] = jnp.zeros_like(r.dk)
    r.dv[...] = jnp.zeros_like(r.dv)

    def make_early():
        @pl.when(mine == parts - 1)
        def _():
            for copy in back_copies(r, mine, batch, parts):
                copy.wait_recv()

        grad_q = mm(r.fit[...], r.gqt[BLOCK:width, :], 1, 1)
        for b in range(8):
            for y in range(2):
                rows = slice(b * PIECE + y * PIECE // 2, b * PIECE + (y + 1) * PIECE // 2)
                for x in range(2):
                    keep("uc", b % 2, y, x, b // 2, grad_q[rows, x * BLOCK : (x + 1) * BLOCK])

    mid = span // 2

    def tiles_of(last):
        return [(part, 0, span, 0) for part in range(last)] + [(last, 0, mid, 0), (last, mid, mid, mid)]

    def spread(value, start):
        return jnp.concatenate([jnp.zeros((value.shape[0], start), F32), value], axis=1) if start else value

    def attend(slot, last):
        rows = pl.ds(pl.multiple_of(slot * HEAD, HEAD), HEAD)
        tiles = tiles_of(last)
        tops = []
        for part, k0, count, q0 in tiles:
            raw = mm(r.kx[part, k0 : k0 + count], r.qt[slot, :, q0:])
            if part == last:
                raw = jnp.where(rows_of(raw.shape) <= lanes_of(raw.shape), raw, FAR)
            r.scores[k0 : k0 + count, part * span + q0 : (part + 1) * span] = raw
            top = jnp.max(raw, axis=0, keepdims=True)
            tops.append(jnp.concatenate([jnp.full((1, q0), FAR, F32), top], axis=1) if q0 else top)
        top = functools.reduce(jnp.maximum, tops)
        sums = []
        for part, k0, count, q0 in tiles:
            place = slice(k0, k0 + count), slice(part * span + q0, (part + 1) * span)
            raised = jnp.exp2(r.scores[place] - top[:, q0:]).astype(BF16)
            r.wfc[place] = raised
            sums.append(spread(mm(r.vxt[part, :, k0 : k0 + count], raised), q0))
        att = functools.reduce(jnp.add, sums)
        inverse = 1.0 / att[HEAD : HEAD + 1, :]
        attended = att[:HEAD, :] * inverse
        r.attt[rows, :] = attended.astype(BF16)
        grad_att = r.dot[rows, :].astype(F32)
        delta = jnp.sum(grad_att * attended, axis=0, keepdims=True) * -inverse
        delta_high = delta.astype(BF16).astype(F32)
        row = rows_of((HEAD, span))
        extra = jnp.where(row == 0, delta_high, jnp.where(row == 1, delta - delta_high, 0.0))
        grad_att = jnp.concatenate([grad_att * inverse, extra], axis=0)
        r.ga[...] = grad_att.astype(BF16)
        r.gat[...] = grad_att.T.astype(BF16)

    def attend_back(slot, borrowed, last):
        rows = pl.ds(pl.multiple_of(slot * HEAD, HEAD), HEAD)
        tiles = tiles_of(last)
        sums = []
        for part, k0, count, q0 in tiles:
            keys = slice(k0, k0 + count)
            grad_probs = mm(r.vx[part, keys], r.ga[:, q0:])
            raised = r.wfc[keys, part * span + q0 : (part + 1) * span]
            grad_scores = (raised.astype(F32) * grad_probs).astype(BF16)
            r.dv[part, keys] += mm(raised, r.gat[q0:])
            r.dk[part, keys] += mm(grad_scores, r.q[slot, q0:])
            sums.append(spread(mm(r.kxt[part, :, keys], grad_scores), q0))
        grad_query = functools.reduce(jnp.add, sums)[:HEAD] * (1.0 / math.sqrt(HEAD))
        r.gqt[rows, :] = rotate_back(r, grad_query, borrowed).astype(BF16)

    n_borrowed = jnp.where(mine == 0, 2, 0)
    n_own = jnp.where(mine == parts - 1, heads - 2, heads)
    whole = 2 * (n_borrowed * (partner + 1) + n_own * (mine + 1))

    def half_task(i, done):
        t, backward = i // 2, lax.rem(i, 2) == 1
        borrowed = t < n_borrowed
        own = t - n_borrowed + 4
        own = jnp.where(own >= n_own, own - n_own, own)
        slot = jnp.where(borrowed, heads + t, own)
        last = jnp.where(borrowed, partner, mine)
        for part in range(parts):

            @pl.when((last == part) & ~backward)
            def _():
                attend(slot, part)

            @pl.when((last == part) & backward)
            def _():
                attend_back(slot, jnp.where(borrowed, 1, 0), part)


        @pl.when((mine == 0) & backward & (slot == heads + 1))
        def _():
            for copy in back_copies(r, mine, batch, parts):
                copy.start()

        after = done + last + 1
        before_80, after_80 = done * 80 // whole, after * 80 // whole
        for when, steps in SCHEDULE.items():

            @pl.when((before_80 < when) & (when <= after_80))
            def _():
                step(steps)

        return after

    lax.fori_loop(0, 2 * (n_borrowed + n_own), half_task, 0)
    step(LATE_SCHEDULE[0])

    def packed(part):
        return jnp.where(low, r.dk[part] * (1.0 / LOG2E), pltpu.roll(r.dv[part], HEAD, 1))

    for distance in range(1, parts):
        target = lax.rem(mine - distance + parts, parts)

        @pl.when(target <= high)
        def _():
            r.dkv_out[distance] = packed(target).astype(BF16)
            dkv_copy(r, mine, batch, parts, distance).start()

    if not inside:
        make_early()
    grad_w = mm(r.attt[:width, :], r.cot[...])
    grad_q = mm(r.fit[...], r.gqt[:BLOCK, :], 1, 1)
    for b in range(8):
        core, z = b % 2, b // 2
        for i, name in enumerate(("ua", "ub")):
            rows = slice(b * PIECE + i * PIECE // 2, b * PIECE + (i + 1) * PIECE // 2)
            for q in range(4):
                piece = grad_w[rows, q * BLOCK : (q + 1) * BLOCK] if q < 3 else grad_q[rows]
                keep(name, core, q // 2, q % 2, z, piece)
    step(LATE_SCHEDULE[1])

    r.total[...] = packed(mine)
    for distance in range(1, parts):
        source = lax.rem(mine + distance, parts)

        @pl.when(mine <= jnp.maximum(source, parts - 1 - source))
        def _():
            dkv_copy(r, mine, batch, parts, distance).wait_recv()
            r.total[...] += r.dkv_in[distance].astype(F32)

    pair = r.total[...].T
    r.gkvt[:HEAD, :] = rotate_back(r, pair[:HEAD], 0).astype(BF16)
    r.gkvt[HEAD:, :] = pair[HEAD:].astype(BF16)

    grad_kv = mm(r.fit[...], r.gkvt[...], 1, 1)
    for b in range(8):
        halves = [grad_kv[b * PIECE + i * PIECE // 2 : b * PIECE + (i + 1) * PIECE // 2] for i in range(2)]
        keep("k", b % 2, 0, 0, b // 2, jnp.concatenate(halves, axis=1))
    step(LATE_SCHEDULE[2])
    for i in range(width // LANES):
        columns = slice(i * LANES, (i + 1) * LANES)
        r.act[:, columns] = flip(r.gqt[columns, :]).astype(BF16)
    r.gh[:, :LANES] = flip(r.gkvt[...]).astype(BF16)

    first = mm(r.act[...], r.wq[:, :width], 1, 1) + mm(r.gh[:, :LANES], r.wq[:, width:], 1, 1)
    for i in range(width // LANES):
        (r.dk if i < parts else r.dv)[i % parts] = first[:, i * LANES : (i + 1) * LANES]
    sums = [jnp.zeros((1, width), F32) for _ in range(4)]
    for i in range(span // LANES):
        rows = pl.ds(i * LANES, LANES)
        normed, inverse_std = norm_tile(i)
        first = [(r.dk if j < parts else r.dv)[j % parts, rows, :] for j in range(width // LANES)]
        first, second = jnp.concatenate(first, axis=1), r.second[rows, :]
        for j, term in enumerate((normed * first, first, normed * second, second)):
            sums[j] = sums[j] + jnp.sum(term, axis=0, keepdims=True)
        scaled = first * r.g1[...][None] + second * r.g2[...][None]
        mean_one = jnp.mean(scaled, axis=-1, keepdims=True)
        mean_two = jnp.mean(scaled * normed, axis=-1, keepdims=True)
        back = inverse_std * (scaled - mean_one - normed * mean_two)
        r.si[rows, :] = (r.cot[rows, :].astype(F32) + back).astype(BF16)

    sum_qkv = jnp.concatenate([mm(ones_rows, r.gqt[:width, :], 1, 1), mm(ones_rows, r.gkvt[...], 1, 1)], axis=1)[0:1]
    sum_proj = mm(ones_rows, r.cot[...])[0:1]
    for b in range(8):
        lines = [cut(sum_qkv, b * 112, 112)]
        lines += [r.sum_fc[0:1, b * 384 + i * LANES : b * 384 + (i + 1) * LANES] for i in range(3)]
        lines += [cut(line, b * 96, 96) for line in (sum_proj, *sums)]
        lines.append(jnp.zeros((16 - len(lines), LANES), F32))
        lines = jnp.concatenate(lines, axis=0)
        keep("v", b % 2, 0, 0, b // 2, jnp.concatenate([lines, jnp.zeros_like(lines)], axis=1))
    step(LATE_SCHEDULE[3])
    copies = [pltpu.make_async_copy(r.si, r.input_grads, r.load_sem.at[0])]
    copies[0].start()

    for i in range(width // LANES):
        columns = slice(i * LANES, (i + 1) * LANES)
        r.fi[:, columns] = flip(r.attt[columns, :]).astype(BF16)
    r.x[...] = (r.result[...] + r.x[...].astype(F32) + r.bp[...][None] + mm(r.fi[...], r.wo[...])).astype(BF16)
    copies.append(pltpu.make_async_copy(r.x, r.outputs, r.load_sem.at[1]))
    copies[1].start()

    if inside:
        step(LATE_SCHEDULE[4])
        summing.close()
    else:
        copies.append(pltpu.make_async_copy(r.grads, r.grads_out, r.load_sem.at[2]))
        copies.append(pltpu.make_async_copy(r.wp.at[:, : 2 * BLOCK], r.late_out, r.load_sem.at[3]))
        for copy in copies[2:]:
            copy.start()
    for copy in copies:
        copy.wait()
    for distance in range(1, parts):
        kv_copy(r, mine, batch, parts, distance).wait_send()
        target = lax.rem(mine - distance + parts, parts)

        @pl.when(target <= high)
        def _():
            dkv_copy(r, mine, batch, parts, distance).wait_send()


    @pl.when(mine == parts - 1)
    def _():
        for copy in lent_copies(r, mine, batch, parts):
            copy.wait_send()

    @pl.when(mine == 0)
    def _():
        for copy in back_copies(r, mine, batch, parts):
            copy.wait_send()


def cut(line, start, size):
    line = jnp.concatenate([line, jnp.zeros((1, LANES), F32)], axis=1)
    base = start // LANES * LANES
    line = line[:, base : base + 2 * LANES]
    shift = start - base
    if shift:
        line = pltpu.roll(line, 2 * LANES - shift, 1)
    return jnp.where(lanes_of((1, LANES)) < size, line[:, :LANES], 0.0)


def rotate_back(r, grads, which):
    half = ROT // 2
    one, two = grads[:half], grads[half:ROT]
    cosine, sine = r.cos[which], r.sin[which]
    return jnp.concatenate([one * cosine + two * sine, two * cosine - one * sine, grads[ROT:]], axis=0)


def remote(src, dst, send_sem, recv_sem, peer):
    return pltpu.make_async_remote_copy(
        src_ref=src, dst_ref=dst, send_sem=send_sem, recv_sem=recv_sem, device_id=peer, device_id_type=MESH
    )


def lent_copies(r, mine, batch, parts):
    peer, rows, there = (parts - 1 - mine, batch), LENT * LANES, r.dot.shape[0] - LANES
    return [
        remote(r.lent, r.lent_in, r.lent_sem.at[0, 0], r.lent_sem.at[1, 0], peer),
        remote(
            r.dot.at[rows : rows + LANES],
            r.dot.at[there : there + LANES],
            r.lent_sem.at[0, 1],
            r.lent_sem.at[1, 1],
            peer,
        ),
    ]


def back_copies(r, mine, batch, parts):
    peer, rows, here = (parts - 1 - mine, batch), LENT * LANES, r.dot.shape[0] - LANES
    return [
        remote(ref.at[here : here + LANES], ref.at[rows : rows + LANES], r.back_sem.at[0, j], r.back_sem.at[1, j], peer)
        for j, ref in enumerate((r.attt, r.gqt))
    ]


class Summing:
    def __init__(self, r, mine, batch, parts):
        self.r, self.mine, self.batch, self.parts = r, mine, batch, parts
        y, x = mine // 2, lax.rem(mine, 2)
        self.z, self.core = batch // 2, lax.rem(batch, 2)
        self.axes = {"x": (x, (y * 2 + 1 - x, batch)), "y": (y, ((1 - y) * 2 + x, batch))}
        self.core_peer = (mine, self.z * 2 + 1 - self.core)
        self.z_peers = [(mine, lax.rem(self.z + i, 4) * 2 + self.core) for i in (1, 2, 3)]
        self.seq_peers = [(lax.rem(mine + i, parts), batch) for i in range(1, parts)]
        self.out_copies, self.sent = [], []

    def of(self, _):
        (y, y_peer), (x, x_peer) = self.axes["y"], self.axes["x"]
        p, s = jnp.where(self.core == 0, x, y), jnp.where(self.core == 0, y, x)
        part_x, part_y = x_peer[0], y_peer[0]
        first, then = jnp.where(self.core == 0, part_x, part_y), jnp.where(self.core == 0, part_y, part_x)
        return p, (first, self.batch), s, (then, self.batch)

    def copy(self, name, src, peer, to=None, sem=None):
        start, rows, index = INBOX[name]
        to = start if to is None else to
        return remote(
            src,
            self.r.inbox.at[pl.ds(to, rows)],
            self.r.sum_sem.at[0, index],
            self.r.sum_sem.at[1, index if sem is None else sem],
            peer,
        )

    def start(self, make, *args):
        make(*args).start()
        self.sent.append((make, *args))

    def rows(self, chunk, start, pieces):
        return chunk.ref(self.r).at[pl.ds(pl.multiple_of(start, 16), pieces * chunk.height)]

    def add(self, chunk, start, name, offset, pieces):
        ref, height, from_row = chunk.ref(self.r), chunk.height, INBOX[name][0] + offset

        def one(i, _):
            to = pl.ds(pl.multiple_of(start + i * height, 16), height)
            ref[to, :] += self.r.inbox[pl.ds(pl.multiple_of(from_row + i * height, 16), height), :]
            return 0

        lax.fori_loop(0, pieces, one, 0)

    def pair(self, chunk):
        rows = chunk.rows // 2
        src = chunk.ref(self.r).at[pl.ds(pl.multiple_of(chunk.base + (1 - self.core) * rows, 16), rows)]
        return self.copy("pair " + chunk.name, src, self.core_peer)

    def half(self, chunk):
        p, peer, _, _ = self.of(chunk)
        if chunk.kind == "line":
            return self.copy("half " + chunk.name, self.rows(chunk, chunk.place(self.core, 1 - p, 0, self.z), 2), peer)
        src = self.rows(chunk, chunk.place(self.core, 1 - p, 0, 0), 2 * chunk.count)
        return self.copy("half " + chunk.name, src, peer)

    def quarter(self, chunk):
        p, _, s, peer = self.of(chunk)
        if chunk.kind == "line":
            src = self.rows(chunk, chunk.place(self.core, p, 1 - s, self.z), 1)
        else:
            src = self.rows(chunk, chunk.place(self.core, p, 1 - s, 0), chunk.count)
        return self.copy("quarter " + chunk.name, src, peer)

    def mine_of(self, chunk, z):
        p, _, s, _ = self.of(chunk)
        if chunk.kind in ("line", "whole"):
            return chunk.place(self.core, 0, 0, z)
        return chunk.place(self.core, p, s, 0 if chunk.kind == "plane" else z)

    def pieces(self, chunk):
        return {"plane": chunk.count, "line": 4}.get(chunk.kind, 1)

    def line(self, chunk, i):
        z = lax.rem(self.z + i, 4)
        src = self.rows(chunk, self.mine_of(chunk, z), self.pieces(chunk))
        return self.copy(f"line{i} " + chunk.name, src, self.z_peers[i - 1])

    def plane_line(self, chunk):
        z = int(chunk.name[1:])
        i = lax.rem(z - self.z + 4, 4)
        start, rows, index = INBOX["line1 p"]
        src = self.rows(chunk, self.mine_of(chunk, z), chunk.count)
        return remote(
            src,
            self.r.inbox.at[pl.ds(pl.multiple_of(start + (i - 1) * rows, 16), rows)],
            self.r.sum_sem.at[0, INBOX["line " + chunk.name][2]],
            self.r.sum_sem.at[1, index + i - 1],
            (self.mine, z * 2 + self.core),
        )

    def near(self, name):
        own, rows, _ = INBOX["share0 " + name]
        start, _, index = INBOX["share1 " + name]
        sem = self.r.sum_sem
        return remote(
            self.r.inbox.at[pl.ds(own, rows)],
            self.r.inbox.at[pl.ds(start, rows)],
            sem.at[0, index],
            sem.at[1, index],
            self.of(None)[1],
        )

    def far(self, name):
        own, rows, _ = INBOX["share0 " + name]
        start, _, index = INBOX["share2 " + name]
        sem = self.r.sum_sem
        return remote(
            self.r.inbox.at[pl.ds(own, 2 * rows)],
            self.r.inbox.at[pl.ds(start, 2 * rows)],
            sem.at[0, index],
            sem.at[1, index],
            self.of(None)[3],
        )

    def share(self, name, i):
        start, rows, index = INBOX[f"share{i} " + name]
        own = INBOX["share0 " + name][0]
        return remote(
            self.r.inbox.at[pl.ds(own, rows)],
            self.r.inbox.at[pl.ds(start, rows)],
            self.r.sum_sem.at[0, index],
            self.r.sum_sem.at[1, index],
            self.seq_peers[i - 1],
        )

    def send(self, chunk):
        order = list(CHUNKS).index(chunk.name)
        if order >= SLOTS:
            pl.semaphore_wait(self.r.free_sem.at[order % SLOTS], 1)
        self.start(self.pair, chunk)

    def a(self, chunk):
        self.pair(chunk).wait_recv()
        name, base, p = "pair " + chunk.name, self.core * (chunk.rows // 2), self.of(chunk)[0]
        if chunk.kind in ("line", "whole"):
            pieces = self.pieces(chunk)
            for i in (1, 2, 3, 0):
                start = self.mine_of(chunk, lax.rem(self.z + i, 4))
                self.add(chunk, start, name, start - chunk.base - base, pieces)
                if i:
                    self.start(self.line, chunk, i)
        else:
            for side in (1 - p, p):
                start = chunk.place(self.core, side, 0, 0)
                self.add(chunk, start, name, start - chunk.base - base, 2 * chunk.count)
                if side is not p:
                    self.start(self.half, chunk)
        order = list(CHUNKS).index(chunk.name)
        if order + SLOTS < len(CHUNKS):
            free = self.r.free_sem.at[order % SLOTS]
            pl.semaphore_signal(free, inc=1, device_id=self.core_peer, device_id_type=MESH)

    def total(self, chunk, name, start, pieces):
        rows = pieces * chunk.height
        total = chunk.ref(self.r)[pl.ds(pl.multiple_of(start, 16), rows), :].astype(F32)
        for i in (1, 2, 3):
            at = INBOX[f"line{i} " + name][0]
            total = total + self.r.inbox[at : at + rows, :].astype(F32)
        return total.astype(BF16)

    def give(self, name, value):
        own, rows, _ = INBOX["share0 " + name]
        self.r.inbox[own : own + rows, :] = value
        if name in TWO_STEPS:
            self.start(self.near, name)
            return
        for i in (1, 2, 3):
            self.start(self.share, name, i)

    def g(self, chunk):
        name = "p" if chunk.kind == "plane" else chunk.name
        self.near(name).wait_recv()
        self.start(self.far, name)

    def b(self, chunk):
        p, _, s, _ = self.of(chunk)
        if chunk.kind == "line":
            for i in (1, 2, 3):
                self.line(chunk, i).wait_recv()
            start = self.mine_of(chunk, self.z)
            self.rows(chunk, start, 4)[...] = self.total(chunk, chunk.name, start, 4)
            self.start(self.half, chunk)
            return
        self.half(chunk).wait_recv()
        for side in (1 - s, s):
            offset = side * chunk.count * chunk.height
            self.add(chunk, chunk.place(self.core, p, side, 0), "half " + chunk.name, offset, chunk.count)
            if side is not s:
                self.start(self.quarter, chunk)

    def c(self, chunk):
        p, _, s, _ = self.of(chunk)
        if chunk.kind == "line":
            self.half(chunk).wait_recv()
            for side in (1 - s, s):
                self.add(chunk, chunk.place(self.core, p, side, self.z), "half " + chunk.name, side * chunk.height, 1)
                if side is not s:
                    self.start(self.quarter, chunk)
            return
        self.quarter(chunk).wait_recv()
        name = "quarter " + chunk.name
        if chunk.kind == "plane":
            self.add(chunk, chunk.place(self.core, p, s, 0), name, 0, chunk.count)


            @pl.when(self.z != int(chunk.name[1:]))
            def _():
                self.plane_line(chunk).start()

            return
        for i in (1, 2, 3, 0):
            z = lax.rem(self.z + i, 4)
            self.add(chunk, chunk.place(self.core, p, s, z), name, z * chunk.height, 1)
            if i:
                self.start(self.line, chunk, i)

    def d(self, chunk):
        if chunk.kind == "line":
            p, _, s, _ = self.of(chunk)
            self.quarter(chunk).wait_recv()
            start = chunk.place(self.core, p, s, self.z)
            arrived = INBOX["quarter " + chunk.name][0]
            own = chunk.ref(self.r)[pl.ds(pl.multiple_of(start, 16), PIECE), :]
            self.give(chunk.name, own + self.r.inbox[arrived : arrived + PIECE, :])
            return
        for i in (1, 2, 3):
            self.line(chunk, i).wait_recv()
        self.give(chunk.name, self.total(chunk, chunk.name, self.mine_of(chunk, self.z), 1))

    def d_planes(self, _):
        r, (start, rows, index) = self.r, INBOX["line1 p"]
        p, _, s, _ = self.of(None)
        total = jnp.zeros((rows, BLOCK), F32)
        for z in range(4):
            here = pl.multiple_of(CHUNKS[f"p{z}"].place(self.core, p, s, 0), 16)
            total = jnp.where(self.z == z, r.grads[pl.ds(here, rows), :].astype(F32), total)
        for i in (1, 2, 3):
            at = start + (i - 1) * rows
            arrived = r.inbox.at[at : at + rows]
            remote(arrived, arrived, r.sum_sem.at[0, index], r.sum_sem.at[1, index + i - 1], self.z_peers[3 - i]).wait_recv()
            total = total + arrived[...].astype(F32)
        self.give("p", total.astype(BF16))

    def quarters(self, name):
        refs = [self.r.inbox.at[pl.ds(*INBOX[f"share{i} " + name][:2])] for i in range(4)]
        if name in TWO_STEPS:
            self.far(name).wait_recv()
            _, first, _, then = self.of(None)
            return zip((self.mine, first[0], then[0], 3 - self.mine), refs)
        for i in (1, 2, 3):
            self.share(name, i).wait_recv()
        return zip([lax.rem(self.mine + 4 - i, 4) for i in range(4)], refs)

    def e(self, chunk):
        r, name = self.r, chunk.name
        plane = chunk.kind == "plane"
        arrived = self.quarters("p" if plane else name)
        if chunk.kind == "whole":
            total = functools.reduce(jnp.add, [ref[...].astype(F32) for _, ref in arrived])
            if name == "k":
                for i in range(2):
                    rows = slice(384 + i * PIECE // 2, 384 + (i + 1) * PIECE // 2)
                    r.scores[rows, 768 : 768 + LANES] = total[:, i * LANES : (i + 1) * LANES]
                self.write(r.scores.at[384 : 384 + PIECE, : r.grad_qkv.shape[1]], r.grad_qkv)
                return
            r.grad_bq[...] = total[0, : r.grad_bq.shape[0]]
            for i in range(3):
                r.grad_bfc[i * LANES : (i + 1) * LANES] = total[1 + i, :LANES]
            for i, out in enumerate((r.grad_bp, r.grad_g1, r.grad_s1, r.grad_g2, r.grad_s2)):
                out[...] = total[4 + i, : out.shape[0]]
            return
        for part, ref in arrived:
            y, x = part // 2, lax.rem(part, 2)
            value = ref[...].astype(F32)
            if plane:
                for i in range(3):
                    to = pl.ds(pl.multiple_of(part * PIECE, PIECE), PIECE)
                    r.scores[to, i * BLOCK : (i + 1) * BLOCK] = value[i * PIECE : (i + 1) * PIECE]
            elif name in ("f0", "f1", "f2"):
                top = int(name[1]) * PIECE
                columns = pl.ds(pl.multiple_of(768 + part * BLOCK, BLOCK), BLOCK)
                r.scores[top : top + PIECE, columns] = value
            elif name == "uc":
                rows = pl.ds(pl.multiple_of(384 + y * PIECE // 2, 16), PIECE // 2)
                r.scores[rows, pl.ds(pl.multiple_of((1 + x) * BLOCK, BLOCK), BLOCK)] = value
            else:
                low = name == "ub"
                top = jnp.where(part == 3, 384, 288) + low * PIECE // 2
                left = jnp.where(part == 3, 0, 768 + part * BLOCK)
                rows = pl.ds(pl.multiple_of(top, 16), PIECE // 2)
                r.scores[rows, pl.ds(pl.multiple_of(left, BLOCK), BLOCK)] = value
        if plane:
            self.write(r.scores.at[:384, :768], r.grad_proj)
        elif name in ("f0", "f1", "f2"):
            k = int(name[1])
            src = r.scores.at[k * PIECE : (k + 1) * PIECE, 768 : 768 + 4 * BLOCK]
            self.write(src, r.grad_fc.at[:, 4 * k * BLOCK : 4 * (k + 1) * BLOCK])
        elif name == "ub":
            self.write(r.scores.at[288 : 288 + PIECE, 768 : 768 + 768], r.grad_o)

    def write(self, src, dst):
        copy = pltpu.make_async_copy(src, dst, self.r.out_sem.at[len(self.out_copies)])
        copy.start()
        self.out_copies.append(copy)

    def close(self):
        for copy in self.out_copies:
            copy.wait()
        for make, *args in self.sent:
            make(*args).wait_send()
        for z in range(4):

            @pl.when(self.z != z)
            def _():
                self.plane_line(CHUNKS[f"p{z}"]).wait_send()


TWO_STEPS = ("p", "f0", "f1", "f2")


def make_inbox():
    inbox, rows = {}, SLOTS * 16 * PIECE

    def add(name, count, start=None):
        nonlocal rows
        if start is None:
            start = rows
            rows += count
        inbox[name] = (start, count, len(inbox))

    for order, chunk in enumerate(CHUNKS.values()):
        name, piece = chunk.name, chunk.height
        add("pair " + name, chunk.rows // 2, order % SLOTS * 16 * PIECE)
        if chunk.kind == "plane":
            add("half " + name, 2 * chunk.count * piece)
            add("quarter " + name, chunk.count * piece)
            add("line " + name, chunk.count * piece, 0)
            continue
        if chunk.kind != "whole":
            count = 1 if chunk.kind == "line" else 4
            add("half " + name, 2 * count * piece)
            add("quarter " + name, count * piece)
        for i in (1, 2, 3):
            add(f"line{i} " + name, (4 if chunk.kind == "line" else 1) * piece)
        for i in range(4):
            add(f"share{i} " + name, piece)
    for i in (1, 2, 3):
        add(f"line{i} p", 3 * PIECE)
    for i in range(4):
        add(f"share{i} p", 3 * PIECE)
    return inbox, rows


INBOX, INBOX_ROWS = make_inbox()


def kv_copy(r, source, batch, parts, distance):
    peer = (lax.rem(source + distance, parts), batch)
    return remote(r.kv.at[source], r.kv.at[source], r.kv_sem.at[0, distance], r.kv_sem.at[1, distance], peer)


def dkv_copy(r, mine, batch, parts, distance):
    peer = (lax.rem(mine - distance + parts, parts), batch)
    return remote(
        r.dkv_out.at[distance], r.dkv_in.at[distance], r.dkv_sem.at[0, distance], r.dkv_sem.at[1, distance], peer
    )


def hand_out_kernel(count, *refs):
    sources, targets, held, sem = refs[:count], refs[count : 2 * count], refs[2 * count : -1], refs[-1]
    large = [i for i in range(count) if sources[i].ndim > 1]
    copies = [
        (
            pltpu.make_async_copy(sources[i], held[j], sem.at[0, j]),
            pltpu.make_async_copy(held[j], targets[i], sem.at[1, j]),
        )
        for j, i in enumerate(large)
    ]
    for here, _ in copies:
        here.start()
    for source, target in zip(sources, targets):
        if source.ndim == 1:
            target[...] = source[...]
    for here, there in copies:
        here.wait()
        there.start()
    for _, there in copies:
        there.wait()


def hand_out(results, specs):
    large = [pltpu.VMEM(item.shape, item.dtype) for item in results if item.ndim > 1]
    return pl.pallas_call(
        functools.partial(hand_out_kernel, len(results)),
        out_shape=[jax.ShapeDtypeStruct(item.shape, item.dtype) for item in results],
        in_specs=specs,
        out_specs=specs,
        scratch_shapes=[*large, pltpu.SemaphoreType.DMA((2, len(large)))],
        name="hand_out",
    )(*results)


def per_device(inputs, doc_ids, w_qkv, b_qkv, w_o, w_fc, b_fc, w_proj, b_proj, gain_one, shift_one, gain_two, shift_two, cotangent):
    rows_here, span, width = inputs.shape
    assert rows_here == 1
    parts = lax.axis_size("seq")
    heads = width // HEAD
    hidden_units = w_fc.shape[1]
    merged = width + 2 * HEAD
    inside = parts == 4 and lax.axis_size("batch") == 8
    vmem = pl.BlockSpec(memory_space=pltpu.VMEM)
    anywhere = pl.BlockSpec(memory_space=pl.ANY)

    small = dict(docs=doc_ids, bq=b_qkv, bfc=b_fc, bp=b_proj, g1=gain_one, s1=shift_one, g2=gain_two, s2=shift_two)
    large = dict(x_h=inputs[0], cot_h=cotangent[0], wq_h=w_qkv, wo_h=w_o, wfc_h=w_fc, wp_h=w_proj)
    outs = dict(outputs=((span, width), BF16, anywhere), input_grads=((span, width), BF16, anywhere))
    if inside:
        outs |= dict(
            grad_qkv=((width // 8, merged), F32, anywhere),
            grad_bq=((merged // 8,), F32, vmem),
            grad_o=((width // 8, width), F32, anywhere),
            grad_fc=((width // 8, hidden_units), F32, anywhere),
            grad_bfc=((hidden_units // 8,), F32, vmem),
            grad_proj=((hidden_units // 8, width), F32, anywhere),
            grad_bp=((width // 8,), F32, vmem),
            grad_g1=((width // 8,), F32, vmem),
            grad_s1=((width // 8,), F32, vmem),
            grad_g2=((width // 8,), F32, vmem),
            grad_s2=((width // 8,), F32, vmem),
        )
    else:
        outs |= dict(grads_out=((GRAD_ROWS, BLOCK), BF16, anywhere), late_out=((hidden_units, 2 * BLOCK), BF16, anywhere))
    scratch = dict(
        x=pltpu.VMEM((span, width), BF16),
        cot=pltpu.VMEM((span, width), BF16),
        wq=pltpu.VMEM((width, merged), BF16),
        wo=pltpu.VMEM((width, width), BF16),
        wfc=pltpu.VMEM((width, hidden_units), BF16),
        wp=pltpu.VMEM((hidden_units, width), BF16),
        fi=pltpu.VMEM((span, width), BF16),
        si=pltpu.VMEM((span, width), BF16),
        fit=pltpu.VMEM((width, span), BF16),
        sit=pltpu.VMEM((width, span), BF16),
        cos=pltpu.VMEM((2, ROT // 2, span), F32),
        sin=pltpu.VMEM((2, ROT // 2, span), F32),
        kv=pltpu.VMEM((parts, span, LANES), BF16),
        q=pltpu.VMEM((heads + 2, span, LANES), BF16),
        qt=pltpu.VMEM((heads + 2, LANES, span), BF16),
        lent=pltpu.VMEM((span, LANES), BF16),
        lent_in=pltpu.VMEM((span, LANES), BF16),
        dot=pltpu.VMEM((width + 2 * HEAD, span), BF16),
        act=pltpu.VMEM((span, width), BF16),
        gh=pltpu.VMEM((span, width), BF16),
        result=pltpu.VMEM((span, width), F32),
        second=pltpu.VMEM((span, width), F32),
        sum_fc=pltpu.VMEM((8, hidden_units), F32),
        kx=pltpu.VMEM((parts, span, LANES), BF16),
        kxt=pltpu.VMEM((parts, LANES, span), BF16),
        vx=pltpu.VMEM((parts, span, LANES), BF16),
        vxt=pltpu.VMEM((parts, LANES, span), BF16),
        dk=pltpu.VMEM((parts, span, LANES), F32),
        dv=pltpu.VMEM((parts, span, LANES), F32),
        scores=pltpu.VMEM((span, parts * span), F32),
        ga=pltpu.VMEM((LANES, span), BF16),
        gat=pltpu.VMEM((span, LANES), BF16),
        attt=pltpu.VMEM((width + 2 * HEAD, span), BF16),
        gqt=pltpu.VMEM((width + 2 * HEAD, span), BF16),
        gkvt=pltpu.VMEM((2 * HEAD, span), BF16),
        dkv_out=pltpu.VMEM((parts, span, LANES), BF16),
        dkv_in=pltpu.VMEM((parts, span, LANES), BF16),
        total=pltpu.VMEM((span, LANES), F32),
        grads=pltpu.VMEM((GRAD_ROWS, BLOCK), BF16),
        load_sem=pltpu.SemaphoreType.DMA((6,)),
        kv_sem=pltpu.SemaphoreType.DMA((2, parts)),
        dkv_sem=pltpu.SemaphoreType.DMA((2, parts)),
        lent_sem=pltpu.SemaphoreType.DMA((2, 2)),
        back_sem=pltpu.SemaphoreType.DMA((2, 2)),
    )
    if inside:
        scratch |= dict(
            inbox=pltpu.VMEM((INBOX_ROWS, BLOCK), BF16),
            sum_sem=pltpu.SemaphoreType.DMA((2, len(INBOX))),
            out_sem=pltpu.SemaphoreType.DMA((6,)),
            free_sem=pltpu.SemaphoreType.REGULAR((SLOTS,)),
        )
    names = [*small, *large, *outs, *scratch]
    results = pl.pallas_call(
        functools.partial(layer_kernel, names, parts, inside),
        out_shape=[jax.ShapeDtypeStruct(shape, dtype) for shape, dtype, _ in outs.values()],
        in_specs=[vmem] * len(small) + [anywhere] * len(large),
        out_specs=[spec for _, _, spec in outs.values()],
        scratch_shapes=list(scratch.values()),
        compiler_params=pltpu.CompilerParams(
            collective_id=0, has_side_effects=True, vmem_limit_bytes=63 * 2**20
        ),
        name="layer",
    )(*small.values(), *large.values())
    if inside:
        outputs, input_grads, *shards = hand_out(results, [spec for _, _, spec in outs.values()])
        return (outputs[None], input_grads[None], *shards)
    outputs, input_grads, *shards = results

    grads, late = shards
    planes = [CHUNKS[f"p{z}"].unfold(grads).transpose(0, 1, 2, 4, 3, 5).reshape(-1, width) for z in range(4)]
    proj = jnp.concatenate(planes)
    columns = [
        CHUNKS[name].unfold(grads).transpose(3, 0, 4, 1, 2, 5).reshape(width, 4 * BLOCK) for name in ("f0", "f1", "f2")
    ]
    fc = jnp.concatenate(columns, axis=1)
    halves = [CHUNKS[name].unfold(late[:, :BLOCK]).transpose(3, 0, 4, 1, 2, 5) for name in ("ua", "ub")]
    both = jnp.stack(halves, axis=2).reshape(width, 4 * BLOCK)
    o = both[:, :width]
    rest = CHUNKS["uc"].unfold(late[:, BLOCK:]).transpose(3, 0, 1, 4, 2, 5).reshape(width, 2 * BLOCK)
    last = CHUNKS["k"].unfold(late[:, BLOCK:]).reshape(2, 4, PIECE // 2, 2, LANES).transpose(1, 0, 3, 2, 4)
    qkv = jnp.concatenate([both[:, width:], rest, last.reshape(width, LANES)], axis=1)
    blocks = 8
    lines = CHUNKS["v"].unfold(late[:, BLOCK:]).transpose(1, 0, 2, 3).reshape(blocks, 16, BLOCK)[..., :LANES]
    vectors = [lines[:, 0, : merged // blocks], lines[:, 1:4]] + [lines[:, i, : width // blocks] for i in range(4, 9)]
    vectors = [vector.reshape(-1) for vector in vectors]
    every = [qkv, vectors[0], o, fc, vectors[1], proj, *vectors[2:]]
    shards = [lax.psum_scatter(item, "batch", scatter_dimension=0, tiled=True) for item in every]
    shards = [lax.psum(item, "seq").astype(F32) for item in shards]
    return (outputs[None], input_grads[None], *shards)


def solution(mesh):
    whole, part = P(), P("batch", "seq", None)
    in_specs = (part, P("batch", None), *[whole] * 11, part)
    matrix, vector = P("batch", None), P("batch")
    out_specs = (part, part, matrix, vector, matrix, matrix, vector, matrix, *[vector] * 5)
    return jax.shard_map(per_device, mesh=mesh, in_specs=in_specs, out_specs=out_specs, check_vma=False)
```

```python
import functools
import math
import types

import jax
import jax.numpy as jnp
import numpy as np
from jax import lax
from jax.experimental import pallas as pl
from jax.experimental.pallas import tpu as pltpu
from jax.sharding import PartitionSpec as P

HEAD = 64
ROT = 16
EPSILON = 1e-05
LANES = 128
BLOCK = 256
FAR = -1e30
LOG2E = math.log2(math.e)
MESH = pl.DeviceIdType.MESH
F32 = jnp.float32
BF16 = jnp.bfloat16

PIECE = 96
SLOTS = 4


class Chunk:
    def __init__(self, name, kind, height, count, base, lane):
        self.name, self.kind = name, kind
        self.height, self.count, self.base, self.lane = height, count, base, lane

    @property
    def rows(self):
        return self.height * self.count * (2 if self.kind == "whole" else 8)

    def place(self, core, p, s, i):
        if self.kind == "whole":
            at = core * 4 + i
        elif self.kind == "line":
            at = ((core * 4 + i) * 2 + p) * 2 + s
        else:
            at = ((core * 2 + p) * 2 + s) * self.count + i
        return self.base + at * self.height

    def ref(self, r):
        if self.lane is None:
            return r.grads
        return r.wp.at[:, self.lane * BLOCK : (self.lane + 1) * BLOCK]

    @staticmethod
    def split(core, y, x):
        return (y, x) if core else (x, y)

    def unfold(self, array):
        array = array[self.base : self.base + self.rows]
        if self.kind == "whole":
            return array.reshape(2, 4, self.height, BLOCK)
        if self.kind == "line":
            array = array.reshape(2, 4, 2, 2, self.height, BLOCK).transpose(0, 2, 3, 1, 4, 5)
        else:
            array = array.reshape(2, 2, 2, self.count, self.height, BLOCK)
        return jnp.stack([array[0].swapaxes(0, 1), array[1]])


def make_chunks():
    plans = [
        ("p0", "plane", PIECE, 3, None),
        ("p1", "plane", PIECE, 3, None),
        ("f0", "line", PIECE, 4, None),
        ("p2", "plane", PIECE, 3, None),
        ("f1", "line", PIECE, 4, None),
        ("p3", "plane", PIECE, 3, None),
        ("f2", "block", PIECE, 4, None),
        ("uc", "block", PIECE // 2, 4, 1),
        ("ua", "block", PIECE // 2, 4, 0),
        ("ub", "block", PIECE // 2, 4, 0),
        ("k", "whole", PIECE // 2, 4, 1),
        ("v", "whole", 16, 4, 1),
    ]
    chunks, filled = {}, {}
    for name, kind, height, count, lane in sorted(plans, key=lambda plan: plan[1] != "plane"):
        chunk = Chunk(name, kind, height, count, filled.get(lane, 0), lane)
        chunks[name] = chunk
        filled[lane] = chunk.base + chunk.rows
    return {plan[0]: chunks[plan[0]] for plan in plans}, filled[None]


CHUNKS, GRAD_ROWS = make_chunks()


def mm(a, b, ca=1, cb=0):
    return lax.dot_general(a, b, (((ca,), (cb,)), ((), ())), preferred_element_type=F32)


def flip(value):
    return value.astype(F32).T


def lanes_of(shape):
    return lax.broadcasted_iota(jnp.int32, shape, 1)


def rows_of(shape):
    return lax.broadcasted_iota(jnp.int32, shape, 0)


EARLY_DONE = 64

FEED_SCHEDULE = [
    ([], [], []),
    ([], ["send:p0", "send:p1"], ["send:f0"]),
    (["a:f0", "a:p1"], ["a:p0"], ["send:p2"]),
    ([], [], ["a:p2"]),
    ["send:f1", "b:p1", "send:p3", "send:f2"],
]

SCHEDULE = {
    4: ["a:p3"],
    8: ["a:f2"],
    12: ["a:f1", "b:p2"],
    28: ["c:p1"],
    32: ["b:f0"],
    36: ["b:f2", "b:p0"],
    44: ["c:f0"],
    48: ["c:f2"],
    52: ["c:p0"],
    60: ["b:p3"],
    EARLY_DONE: ["make:uc", "send:uc", "d:f0"],
    68: ["a:uc", "c:p3"],
    72: ["b:f1", "g:f0"],
    76: ["b:uc"],
}

LATE_SCHEDULE = [
    ["c:f1"],
    ["c:p2", "c:uc", "send:ua", "a:ua", "send:ub", "d:f2", "a:ub"],
    ["send:k", "b:ua", "a:k", "b:ub", "d:f1", "c:ua", "d_planes:p0", "g:f2"],
    ["g:f1", "c:ub", "send:v", "d:uc", "g:p0", "a:v", "d:k"],
    ["d:ua", "e:f0", "e:f1", "e:f2", "d:ub", "d:v", "e:p0", "e:ua", "e:uc", "e:ub", "e:k", "e:v"],
]

LENT = 5


def gelu_parts(hidden):
    size = jnp.abs(hidden)
    t = pl.reciprocal(1.0 + (0.3275911 / math.sqrt(2.0)) * size)
    bell = jnp.exp2(hidden * hidden * (-0.5 * LOG2E))
    poly = 0.5 * 1.061405429
    for term in (-1.453152027, 1.421413741, -0.284496736, 0.254829592):
        poly = poly * t + 0.5 * term
    tail = poly * t * bell
    below = jnp.where(hidden >= 0, 1.0 - tail, tail)
    return below, hidden * bell * (1.0 / math.sqrt(2.0 * math.pi))


def layer_kernel(names, parts, inside, *refs):
    r = types.SimpleNamespace(**dict(zip(names, refs, strict=True)))
    span, width = r.x.shape
    hidden_units = r.wfc.shape[1]
    heads = width // HEAD
    mine = lax.axis_index("seq")
    batch = lax.axis_index("batch")
    partner = parts - 1 - mine
    high = jnp.maximum(mine, partner)

    loads = [
        pltpu.make_async_copy(src, dst, r.load_sem.at[i])
        for i, (src, dst) in enumerate(
            [(r.x_h, r.x), (r.wq_h, r.wq), (r.cot_h, r.cot), (r.wo_h, r.wo), (r.wfc_h, r.wfc), (r.wp_h, r.wp)]
        )
    ]
    for load in loads:
        load.start()

    barrier = pltpu.get_barrier_semaphore()
    peers = [(lax.rem(mine + distance, parts), batch) for distance in range(1, parts)]
    summing = Summing(r, mine, batch, parts) if inside else None
    if inside:
        peers += [summing.core_peer, *summing.z_peers]
    for peer in peers:
        pl.semaphore_signal(barrier, inc=1, device_id=peer, device_id_type=MESH)
    pl.semaphore_wait(barrier, len(peers))

    def keep(name, core, y, x, i, value):
        chunk = CHUNKS[name]
        row = chunk.place(core, *chunk.split(core, y, x), i)
        chunk.ref(r)[row : row + chunk.height, :] = value.astype(BF16)

    def step(steps):
        for item in steps if inside else ():
            kind, name = item.split(":")
            if kind == "make":
                make_early()
            else:
                getattr(summing, kind)(CHUNKS[name])

    loads[0].wait()

    def norm_tile(i):
        tokens = r.x[pl.ds(i * LANES, LANES), :].astype(F32)
        average = jnp.mean(tokens, axis=-1, keepdims=True)
        centered = tokens - average
        variance = jnp.mean(centered * centered, axis=-1, keepdims=True)
        inverse_std = lax.rsqrt(variance + EPSILON)
        return centered * inverse_std, inverse_std

    for i in range(span // LANES):
        normed, _ = norm_tile(i)
        rows = pl.ds(i * LANES, LANES)
        first = normed * r.g1[...][None] + r.s1[...][None]
        second = normed * r.g2[...][None] + r.s2[...][None]
        r.fi[rows, :] = first.astype(BF16)
        r.si[rows, :] = second.astype(BF16)
        r.fit[:, rows] = first.T.astype(BF16)
        r.sit[:, rows] = second.T.astype(BF16)

    half = ROT // 2
    index = rows_of((half, span))
    frequency = jnp.zeros((half, span), F32)
    for i in range(half):
        frequency = jnp.where(index == i, np.float32(10000.0 ** (-2.0 * i / ROT)), frequency)
    for i, part in enumerate((mine, partner)):
        angle = (part * span + lanes_of((half, span))).astype(F32) * frequency
        r.cos[i] = jnp.cos(angle)
        r.sin[i] = jnp.sin(angle)
    cosine, sine = r.cos[0], r.sin[0]
    ones = jnp.ones((HEAD - ROT, span), F32)
    zeros = jnp.zeros((HEAD - ROT, span), F32)
    table_cos = jnp.concatenate([cosine, cosine, ones] * 2, axis=0).T
    table_sin = jnp.concatenate([-sine, sine, zeros] * 2, axis=0).T
    lane = lanes_of((span, LANES))

    def rotate(tile, cos_of, sin_of):
        partner = jnp.where(
            lax.rem(lane, HEAD) < half, pltpu.roll(tile, LANES - half, 1), pltpu.roll(tile, half, 1)
        )
        return tile * cos_of + partner * sin_of

    def docs_row(part):
        return r.docs[0:1, pl.ds(pl.multiple_of(part * span, LANES), span)]

    loads[1].wait()
    key_value = mm(r.fi[...], r.wq[:, width:]) + r.bq[width:][None]
    low = lane < HEAD
    key_value = rotate(key_value, jnp.where(low, table_cos, 1.0), jnp.where(low, table_sin, 0.0))
    r.kv[mine] = key_value.astype(BF16)

    def needs(part, source):
        return (part > source) | (part == 0)

    for distance in range(1, parts):

        @pl.when(needs(lax.rem(mine + distance, parts), mine))
        def _():
            kv_copy(r, mine, batch, parts, distance).start()

    feature_row = rows_of((LANES, span)) - HEAD

    def keep_queries(slot, tile, feature):
        for i, head in enumerate((tile, pltpu.roll(tile, HEAD, 1))):
            head = jnp.where(low, head, feature)
            r.q[slot + i] = head.astype(BF16)
            r.qt[slot + i] = head.T.astype(BF16)

    query_feature = jnp.where(feature_row == docs_row(mine), 1.0, 0.0).T
    for i in range(heads // 2):
        columns = slice(i * LANES, (i + 1) * LANES)
        tile = mm(r.fi[...], r.wq[:, columns]) + r.bq[columns][None]
        tile = rotate(tile, table_cos, table_sin) * (LOG2E / math.sqrt(HEAD))
        keep_queries(2 * i, tile, query_feature)
        if i == LENT:
            r.dkv_out[0] = tile.astype(BF16)

    loads[2].wait()
    loads[3].wait()
    for i in range(width // BLOCK):
        rows = slice(i * BLOCK, (i + 1) * BLOCK)
        r.dot[rows, :] = mm(r.wo[rows, :], r.cot[...], 1, 1).astype(BF16)

    @pl.when(mine == parts - 1)
    def _():
        for copy in lent_copies(r, mine, batch, parts):
            copy.start()


    loads[4].wait()
    loads[5].wait()
    r.result[...] = jnp.zeros_like(r.result)
    r.second[...] = jnp.zeros_like(r.second)
    ones_rows = jnp.ones((8, span), BF16)
    group = 2 * 4 * 96

    def feed_steps(g, i):
        for group_of, steps in enumerate(FEED_SCHEDULE[:-1]):
            if steps[i]:

                @pl.when(g == group_of)
                def _():
                    step(steps[i])

    plane, line, block = CHUNKS["p0"], CHUNKS["f0"], CHUNKS["f2"]
    lines = sum(chunk.kind == "line" for chunk in CHUNKS.values())

    def feed_forward(g, _):
        columns = pl.ds(pl.multiple_of(g * group, LANES), group)
        hidden = mm(r.si[...], r.wfc[:, columns]) + r.bfc[columns][None]
        grad_act = mm(r.cot[...], r.wp[columns, :], 1, 1)
        below, slope = gelu_parts(hidden)
        r.act[...] = (hidden * below).astype(BF16)
        r.gh[...] = (grad_act * (below + slope)).astype(BF16)
        feed_steps(g, 0)
        grad_w = mm(r.act[...], r.cot[...], 0, 0)
        for c in range(2):
            for q in range(4):
                row = (c * 4 + q) * PIECE
                for k in range(3):
                    to = g * plane.rows + plane.place(c, *plane.split(c, q // 2, q % 2), k)
                    piece = grad_w[row : row + PIECE, k * BLOCK : (k + 1) * BLOCK]
                    r.grads[pl.ds(pl.multiple_of(to, 16), PIECE), :] = piece.astype(BF16)
        feed_steps(g, 1)
        grad_w = mm(r.sit[...], r.gh[...])
        for k in range(group // BLOCK):
            at = g * (group // BLOCK) + k
            chunk, y, x = at // 4, lax.rem(at, 4) // 2, lax.rem(at, 2)
            for b in range(8):
                c, z = b % 2, b // 2
                p, s = line.split(c, y, x)
                later = block.place(c, p, s, z) + (chunk - 2) * block.rows
                to = jnp.where(chunk < lines, line.place(c, p, s, z) + chunk * line.rows, later)
                piece = grad_w[b * PIECE : (b + 1) * PIECE, k * BLOCK : (k + 1) * BLOCK]
                r.grads[pl.ds(pl.multiple_of(to, 16), PIECE), :] = piece.astype(BF16)
        feed_steps(g, 2)
        r.sum_fc[:, columns] = mm(ones_rows, r.gh[...])
        r.result[...] += mm(r.act[...], r.wp[columns, :])
        r.second[...] += mm(r.gh[...], r.wfc[:, columns], 1, 1)
        return 0

    lax.fori_loop(0, hidden_units // group, feed_forward, 0)
    step(FEED_SCHEDULE[4])

    for distance in range(1, parts):
        source = lax.rem(mine - distance + parts, parts)

        @pl.when(needs(mine, source))
        def _():
            kv_copy(r, source, batch, parts, distance).wait_recv()

    def prepare(part):
        apart = (feature_row >= 0) & (feature_row < 8) & (feature_row != docs_row(part))
        key_feature = jnp.where(apart, FAR, 0.0).T
        pair = r.kv[part].astype(F32)
        keys = jnp.where(low, pair, key_feature)
        values = jnp.where(low, pltpu.roll(pair, HEAD, 1), jnp.where(lane < HEAD + 2, 1.0, 0.0))
        r.kx[part] = keys.astype(BF16)
        r.kxt[part] = keys.T.astype(BF16)
        r.vx[part] = values.astype(BF16)
        r.vxt[part] = values.T.astype(BF16)

    for part in range(parts):
        pl.when((mine >= part) | (mine == 0))(functools.partial(prepare, part))

    @pl.when(mine == 0)
    def _():
        for copy in lent_copies(r, mine, batch, parts):
            copy.wait_recv()
        feature = jnp.where(feature_row == docs_row(partner), 1.0, 0.0).T
        keep_queries(heads, r.dkv_in[0].astype(F32), feature)

    r.dk[...] = jnp.zeros_like(r.dk)
    r.dv[...] = jnp.zeros_like(r.dv)

    def make_early():
        @pl.when(mine == parts - 1)
        def _():
            for copy in back_copies(r, mine, batch, parts):
                copy.wait_recv()

        grad_q = mm(r.fit[...], r.gqt[BLOCK:width, :], 1, 1)
        for b in range(8):
            for y in range(2):
                rows = slice(b * PIECE + y * PIECE // 2, b * PIECE + (y + 1) * PIECE // 2)
                for x in range(2):
                    keep("uc", b % 2, y, x, b // 2, grad_q[rows, x * BLOCK : (x + 1) * BLOCK])

    def packed(part):
        return jnp.where(low, r.dk[part] * (1.0 / LOG2E), pltpu.roll(r.dv[part], HEAD, 1))

    def send_key_grads(distance):
        r.dkv_out[distance] = packed(lax.rem(mine - distance + parts, parts)).astype(BF16)
        dkv_copy(r, mine, batch, parts, distance).start()

    mid = span // 2

    def tiles_of(last):
        return [(part, 0, span, 0) for part in range(last)] + [(last, 0, mid, 0), (last, mid, mid, mid)]

    def spread(value, start):
        return jnp.concatenate([jnp.zeros((value.shape[0], start), F32), value], axis=1) if start else value

    def attend(slot, last):
        rows = pl.ds(pl.multiple_of(slot * HEAD, HEAD), HEAD)
        tiles = tiles_of(last)
        tops = []
        for part, k0, count, q0 in tiles:
            raw = mm(r.kx[part, k0 : k0 + count], r.qt[slot, :, q0:])
            if part == last:
                raw = jnp.where(rows_of(raw.shape) <= lanes_of(raw.shape), raw, FAR)
            r.scores[k0 : k0 + count, part * span + q0 : (part + 1) * span] = raw
            top = jnp.max(raw, axis=0, keepdims=True)
            tops.append(jnp.concatenate([jnp.full((1, q0), FAR, F32), top], axis=1) if q0 else top)
        top = functools.reduce(jnp.maximum, tops)
        sums = []
        for part, k0, count, q0 in tiles:
            place = slice(k0, k0 + count), slice(part * span + q0, (part + 1) * span)
            raised = jnp.exp2(r.scores[place] - top[:, q0:]).astype(BF16)
            r.wfc[place] = raised
            sums.append(spread(mm(r.vxt[part, :, k0 : k0 + count], raised), q0))
        att = functools.reduce(jnp.add, sums)
        inverse = 1.0 / att[HEAD : HEAD + 1, :]
        attended = att[:HEAD, :] * inverse
        r.attt[rows, :] = attended.astype(BF16)
        grad_att = r.dot[rows, :].astype(F32)
        delta = jnp.sum(grad_att * attended, axis=0, keepdims=True) * -inverse
        delta_high = delta.astype(BF16).astype(F32)
        row = rows_of((HEAD, span))
        extra = jnp.where(row == 0, delta_high, jnp.where(row == 1, delta - delta_high, 0.0))
        grad_att = jnp.concatenate([grad_att * inverse, extra], axis=0)
        r.ga[...] = grad_att.astype(BF16)
        r.gat[...] = grad_att.T.astype(BF16)

    def attend_back(slot, borrowed, last):
        rows = pl.ds(pl.multiple_of(slot * HEAD, HEAD), HEAD)
        tiles = tiles_of(last)
        sums = []
        for part, k0, count, q0 in tiles:
            keys = slice(k0, k0 + count)
            grad_probs = mm(r.vx[part, keys], r.ga[:, q0:])
            raised = r.wfc[keys, part * span + q0 : (part + 1) * span]
            grad_scores = (raised.astype(F32) * grad_probs).astype(BF16)
            r.dv[part, keys] += mm(raised, r.gat[q0:])
            r.dk[part, keys] += mm(grad_scores, r.q[slot, q0:])
            sums.append(spread(mm(r.kxt[part, :, keys], grad_scores), q0))
        grad_query = functools.reduce(jnp.add, sums)[:HEAD] * (1.0 / math.sqrt(HEAD))
        r.gqt[rows, :] = rotate_back(r, grad_query, borrowed).astype(BF16)

    n_borrowed = jnp.where(mine == 0, 2, 0)
    n_own = jnp.where(mine == parts - 1, heads - 2, heads)
    whole = 2 * (n_borrowed * (partner + 1) + n_own * (mine + 1))

    def half_task(i, done):
        t, backward = i // 2, lax.rem(i, 2) == 1
        borrowed = t < n_borrowed
        own = t - n_borrowed + 4
        own = jnp.where(own >= n_own, own - n_own, own)
        slot = jnp.where(borrowed, heads + t, own)
        last = jnp.where(borrowed, partner, mine)
        for part in range(parts):

            @pl.when((last == part) & ~backward)
            def _():
                attend(slot, part)

            @pl.when((last == part) & backward)
            def _():
                attend_back(slot, jnp.where(borrowed, 1, 0), part)


        @pl.when((mine == 0) & backward & (slot == heads + 1))
        def _():
            for copy in back_copies(r, mine, batch, parts):
                copy.start()

        after = done + last + 1
        before_80, after_80 = done * 80 // whole, after * 80 // whole
        for when, steps in SCHEDULE.items():

            @pl.when((before_80 < when) & (when <= after_80))
            def _():
                step(steps)

        return after

    lax.fori_loop(0, 2 * (n_borrowed + n_own), half_task, 0)
    step(LATE_SCHEDULE[0])

    for distance in reversed(range(1, parts)):

        @pl.when(lax.rem(mine - distance + parts, parts) <= high)
        def _():
            send_key_grads(distance)

    if not inside:
        make_early()
    grad_w = mm(r.attt[:width, :], r.cot[...])
    grad_q = mm(r.fit[...], r.gqt[:BLOCK, :], 1, 1)
    for b in range(8):
        core, z = b % 2, b // 2
        for i, name in enumerate(("ua", "ub")):
            rows = slice(b * PIECE + i * PIECE // 2, b * PIECE + (i + 1) * PIECE // 2)
            for q in range(4):
                piece = grad_w[rows, q * BLOCK : (q + 1) * BLOCK] if q < 3 else grad_q[rows]
                keep(name, core, q // 2, q % 2, z, piece)
    step(LATE_SCHEDULE[1])

    r.dk[mine] = packed(mine)
    for distance in range(1, parts):
        source = lax.rem(mine + distance, parts)

        @pl.when(mine <= jnp.maximum(source, parts - 1 - source))
        def _():
            dkv_copy(r, mine, batch, parts, distance).wait_recv()
            r.dk[mine] += r.dkv_in[distance].astype(F32)

    pair = r.dk[mine].T
    r.gkvt[:HEAD, :] = rotate_back(r, pair[:HEAD], 0).astype(BF16)
    r.gkvt[HEAD:, :] = pair[HEAD:].astype(BF16)

    grad_kv = mm(r.fit[...], r.gkvt[...], 1, 1)
    for b in range(8):
        halves = [grad_kv[b * PIECE + i * PIECE // 2 : b * PIECE + (i + 1) * PIECE // 2] for i in range(2)]
        keep("k", b % 2, 0, 0, b // 2, jnp.concatenate(halves, axis=1))
    step(LATE_SCHEDULE[2])
    for i in range(width // LANES):
        columns = slice(i * LANES, (i + 1) * LANES)
        r.act[:, columns] = flip(r.gqt[columns, :]).astype(BF16)
    r.gh[:, :LANES] = flip(r.gkvt[...]).astype(BF16)

    first = mm(r.act[...], r.wq[:, :width], 1, 1) + mm(r.gh[:, :LANES], r.wq[:, width:], 1, 1)
    for i in range(width // LANES):
        (r.dk if i < parts else r.dv)[i % parts] = first[:, i * LANES : (i + 1) * LANES]
    sums = [jnp.zeros((1, width), F32) for _ in range(4)]
    for i in range(span // LANES):
        rows = pl.ds(i * LANES, LANES)
        normed, inverse_std = norm_tile(i)
        first = [(r.dk if j < parts else r.dv)[j % parts, rows, :] for j in range(width // LANES)]
        first, second = jnp.concatenate(first, axis=1), r.second[rows, :]
        for j, term in enumerate((normed * first, first, normed * second, second)):
            sums[j] = sums[j] + jnp.sum(term, axis=0, keepdims=True)
        scaled = first * r.g1[...][None] + second * r.g2[...][None]
        mean_one = jnp.mean(scaled, axis=-1, keepdims=True)
        mean_two = jnp.mean(scaled * normed, axis=-1, keepdims=True)
        back = inverse_std * (scaled - mean_one - normed * mean_two)
        r.si[rows, :] = (r.cot[rows, :].astype(F32) + back).astype(BF16)

    sum_qkv = jnp.concatenate([mm(ones_rows, r.gqt[:width, :], 1, 1), mm(ones_rows, r.gkvt[...], 1, 1)], axis=1)[0:1]
    sum_proj = mm(ones_rows, r.cot[...])[0:1]
    for b in range(8):
        lines = [cut(sum_qkv, b * 112, 112)]
        lines += [r.sum_fc[0:1, b * 384 + i * LANES : b * 384 + (i + 1) * LANES] for i in range(3)]
        lines += [cut(line, b * 96, 96) for line in (sum_proj, *sums)]
        lines.append(jnp.zeros((16 - len(lines), LANES), F32))
        lines = jnp.concatenate(lines, axis=0)
        keep("v", b % 2, 0, 0, b // 2, jnp.concatenate([lines, jnp.zeros_like(lines)], axis=1))
    step(LATE_SCHEDULE[3])
    copies = [pltpu.make_async_copy(r.si, r.input_grads, r.load_sem.at[0])]
    copies[0].start()

    for i in range(width // LANES):
        columns = slice(i * LANES, (i + 1) * LANES)
        r.fi[:, columns] = flip(r.attt[columns, :]).astype(BF16)
    r.x[...] = (r.result[...] + r.x[...].astype(F32) + r.bp[...][None] + mm(r.fi[...], r.wo[...])).astype(BF16)
    copies.append(pltpu.make_async_copy(r.x, r.outputs, r.load_sem.at[1]))
    copies[1].start()

    if inside:
        step(LATE_SCHEDULE[4])
        summing.close()
    else:
        copies.append(pltpu.make_async_copy(r.grads, r.grads_out, r.load_sem.at[2]))
        copies.append(pltpu.make_async_copy(r.wp.at[:, : 2 * BLOCK], r.late_out, r.load_sem.at[3]))
        for copy in copies[2:]:
            copy.start()
    for copy in copies:
        copy.wait()
    for distance in range(1, parts):

        @pl.when(needs(lax.rem(mine + distance, parts), mine))
        def _():
            kv_copy(r, mine, batch, parts, distance).wait_send()

        target = lax.rem(mine - distance + parts, parts)

        @pl.when(target <= high)
        def _():
            dkv_copy(r, mine, batch, parts, distance).wait_send()


    @pl.when(mine == parts - 1)
    def _():
        for copy in lent_copies(r, mine, batch, parts):
            copy.wait_send()

    @pl.when(mine == 0)
    def _():
        for copy in back_copies(r, mine, batch, parts):
            copy.wait_send()


def cut(line, start, size):
    line = jnp.concatenate([line, jnp.zeros((1, LANES), F32)], axis=1)
    base = start // LANES * LANES
    line = line[:, base : base + 2 * LANES]
    shift = start - base
    if shift:
        line = pltpu.roll(line, 2 * LANES - shift, 1)
    return jnp.where(lanes_of((1, LANES)) < size, line[:, :LANES], 0.0)


def rotate_back(r, grads, which):
    half = ROT // 2
    one, two = grads[:half], grads[half:ROT]
    cosine, sine = r.cos[which], r.sin[which]
    return jnp.concatenate([one * cosine + two * sine, two * cosine - one * sine, grads[ROT:]], axis=0)


def remote(src, dst, send_sem, recv_sem, peer):
    return pltpu.make_async_remote_copy(
        src_ref=src, dst_ref=dst, send_sem=send_sem, recv_sem=recv_sem, device_id=peer, device_id_type=MESH
    )


def lent_copies(r, mine, batch, parts):
    peer, rows, there = (parts - 1 - mine, batch), LENT * LANES, r.dot.shape[0] - LANES
    return [
        remote(r.dkv_out.at[0], r.dkv_in.at[0], r.lent_sem.at[0, 0], r.lent_sem.at[1, 0], peer),
        remote(
            r.dot.at[rows : rows + LANES],
            r.dot.at[there : there + LANES],
            r.lent_sem.at[0, 1],
            r.lent_sem.at[1, 1],
            peer,
        ),
    ]


def back_copies(r, mine, batch, parts):
    peer, rows, here = (parts - 1 - mine, batch), LENT * LANES, r.dot.shape[0] - LANES
    return [
        remote(ref.at[here : here + LANES], ref.at[rows : rows + LANES], r.back_sem.at[0, j], r.back_sem.at[1, j], peer)
        for j, ref in enumerate((r.attt, r.gqt))
    ]


class Summing:
    def __init__(self, r, mine, batch, parts):
        self.r, self.mine, self.batch, self.parts = r, mine, batch, parts
        y, x = mine // 2, lax.rem(mine, 2)
        self.z, self.core = batch // 2, lax.rem(batch, 2)
        self.axes = {"x": (x, (y * 2 + 1 - x, batch)), "y": (y, ((1 - y) * 2 + x, batch))}
        self.core_peer = (mine, self.z * 2 + 1 - self.core)
        self.z_peers = [(mine, lax.rem(self.z + i, 4) * 2 + self.core) for i in (1, 2, 3)]
        self.seq_peers = [(lax.rem(mine + i, parts), batch) for i in range(1, parts)]
        self.out_copies, self.sent = [], []

    def of(self, _):
        (y, y_peer), (x, x_peer) = self.axes["y"], self.axes["x"]
        p, s = jnp.where(self.core == 0, x, y), jnp.where(self.core == 0, y, x)
        part_x, part_y = x_peer[0], y_peer[0]
        first, then = jnp.where(self.core == 0, part_x, part_y), jnp.where(self.core == 0, part_y, part_x)
        return p, (first, self.batch), s, (then, self.batch)

    def copy(self, name, src, peer, to=None, sem=None):
        start, rows, index = INBOX[name]
        to = start if to is None else to
        return remote(
            src,
            self.r.inbox.at[pl.ds(to, rows)],
            self.r.sum_sem.at[0, index],
            self.r.sum_sem.at[1, index if sem is None else sem],
            peer,
        )

    def start(self, make, *args):
        make(*args).start()
        self.sent.append((make, *args))

    def rows(self, chunk, start, pieces):
        return chunk.ref(self.r).at[pl.ds(pl.multiple_of(start, 16), pieces * chunk.height)]

    def add(self, chunk, start, name, offset, pieces):
        ref, height, from_row = chunk.ref(self.r), chunk.height, INBOX[name][0] + offset

        def one(i, _):
            to = pl.ds(pl.multiple_of(start + i * height, 16), height)
            ref[to, :] += self.r.inbox[pl.ds(pl.multiple_of(from_row + i * height, 16), height), :]
            return 0

        lax.fori_loop(0, pieces, one, 0)

    def pair(self, chunk):
        rows = chunk.rows // 2
        src = chunk.ref(self.r).at[pl.ds(pl.multiple_of(chunk.base + (1 - self.core) * rows, 16), rows)]
        return self.copy("pair " + chunk.name, src, self.core_peer)

    def half(self, chunk):
        p, peer, _, _ = self.of(chunk)
        if chunk.kind == "line":
            return self.copy("half " + chunk.name, self.rows(chunk, chunk.place(self.core, 1 - p, 0, self.z), 2), peer)
        src = self.rows(chunk, chunk.place(self.core, 1 - p, 0, 0), 2 * chunk.count)
        return self.copy("half " + chunk.name, src, peer)

    def quarter(self, chunk):
        p, _, s, peer = self.of(chunk)
        if chunk.kind == "line":
            src = self.rows(chunk, chunk.place(self.core, p, 1 - s, self.z), 1)
        else:
            src = self.rows(chunk, chunk.place(self.core, p, 1 - s, 0), chunk.count)
        return self.copy("quarter " + chunk.name, src, peer)

    def mine_of(self, chunk, z):
        p, _, s, _ = self.of(chunk)
        if chunk.kind in ("line", "whole"):
            return chunk.place(self.core, 0, 0, z)
        return chunk.place(self.core, p, s, 0 if chunk.kind == "plane" else z)

    def pieces(self, chunk):
        return {"plane": chunk.count, "line": 4}.get(chunk.kind, 1)

    def line(self, chunk, i):
        z = lax.rem(self.z + i, 4)
        src = self.rows(chunk, self.mine_of(chunk, z), self.pieces(chunk))
        return self.copy(f"line{i} " + chunk.name, src, self.z_peers[i - 1])

    def plane_line(self, chunk):
        z = int(chunk.name[1:])
        i = lax.rem(z - self.z + 4, 4)
        start, rows, index = INBOX["line1 p"]
        src = self.rows(chunk, self.mine_of(chunk, z), chunk.count)
        return remote(
            src,
            self.r.inbox.at[pl.ds(pl.multiple_of(start + (i - 1) * rows, 16), rows)],
            self.r.sum_sem.at[0, INBOX["line " + chunk.name][2]],
            self.r.sum_sem.at[1, index + i - 1],
            (self.mine, z * 2 + self.core),
        )

    def near(self, name):
        own, rows, _ = INBOX["share0 " + name]
        start, _, index = INBOX["share1 " + name]
        sem = self.r.sum_sem
        return remote(
            self.r.inbox.at[pl.ds(own, rows)],
            self.r.inbox.at[pl.ds(start, rows)],
            sem.at[0, index],
            sem.at[1, index],
            self.of(None)[1],
        )

    def far(self, name):
        own, rows, _ = INBOX["share0 " + name]
        start, _, index = INBOX["share2 " + name]
        sem = self.r.sum_sem
        return remote(
            self.r.inbox.at[pl.ds(own, 2 * rows)],
            self.r.inbox.at[pl.ds(start, 2 * rows)],
            sem.at[0, index],
            sem.at[1, index],
            self.of(None)[3],
        )

    def share(self, name, i):
        start, rows, index = INBOX[f"share{i} " + name]
        own = INBOX["share0 " + name][0]
        return remote(
            self.r.inbox.at[pl.ds(own, rows)],
            self.r.inbox.at[pl.ds(start, rows)],
            self.r.sum_sem.at[0, index],
            self.r.sum_sem.at[1, index],
            self.seq_peers[i - 1],
        )

    def send(self, chunk):
        order = list(CHUNKS).index(chunk.name)
        if order >= SLOTS:
            pl.semaphore_wait(self.r.free_sem.at[order % SLOTS], 1)
        self.start(self.pair, chunk)

    def a(self, chunk):
        self.pair(chunk).wait_recv()
        name, base, p = "pair " + chunk.name, self.core * (chunk.rows // 2), self.of(chunk)[0]
        if chunk.kind in ("line", "whole"):
            pieces = self.pieces(chunk)
            for i in (1, 2, 3, 0):
                start = self.mine_of(chunk, lax.rem(self.z + i, 4))
                self.add(chunk, start, name, start - chunk.base - base, pieces)
                if i:
                    self.start(self.line, chunk, i)
        else:
            for side in (1 - p, p):
                start = chunk.place(self.core, side, 0, 0)
                self.add(chunk, start, name, start - chunk.base - base, 2 * chunk.count)
                if side is not p:
                    self.start(self.half, chunk)
        order = list(CHUNKS).index(chunk.name)
        if order + SLOTS < len(CHUNKS):
            free = self.r.free_sem.at[order % SLOTS]
            pl.semaphore_signal(free, inc=1, device_id=self.core_peer, device_id_type=MESH)

    def total(self, chunk, name, start, pieces):
        rows = pieces * chunk.height
        total = chunk.ref(self.r)[pl.ds(pl.multiple_of(start, 16), rows), :].astype(F32)
        for i in (1, 2, 3):
            at = INBOX[f"line{i} " + name][0]
            total = total + self.r.inbox[at : at + rows, :].astype(F32)
        return total.astype(BF16)

    def give(self, name, value):
        own, rows, _ = INBOX["share0 " + name]
        self.r.inbox[own : own + rows, :] = value
        if name in TWO_STEPS:
            self.start(self.near, name)
            return
        for i in (1, 2, 3):
            self.start(self.share, name, i)

    def g(self, chunk):
        name = "p" if chunk.kind == "plane" else chunk.name
        self.near(name).wait_recv()
        self.start(self.far, name)

    def b(self, chunk):
        p, _, s, _ = self.of(chunk)
        if chunk.kind == "line":
            for i in (1, 2, 3):
                self.line(chunk, i).wait_recv()
            start = self.mine_of(chunk, self.z)
            self.rows(chunk, start, 4)[...] = self.total(chunk, chunk.name, start, 4)
            self.start(self.half, chunk)
            return
        self.half(chunk).wait_recv()
        for side in (1 - s, s):
            offset = side * chunk.count * chunk.height
            self.add(chunk, chunk.place(self.core, p, side, 0), "half " + chunk.name, offset, chunk.count)
            if side is not s:
                self.start(self.quarter, chunk)

    def c(self, chunk):
        p, _, s, _ = self.of(chunk)
        if chunk.kind == "line":
            self.half(chunk).wait_recv()
            for side in (1 - s, s):
                self.add(chunk, chunk.place(self.core, p, side, self.z), "half " + chunk.name, side * chunk.height, 1)
                if side is not s:
                    self.start(self.quarter, chunk)
            return
        self.quarter(chunk).wait_recv()
        name = "quarter " + chunk.name
        if chunk.kind == "plane":
            self.add(chunk, chunk.place(self.core, p, s, 0), name, 0, chunk.count)


            @pl.when(self.z != int(chunk.name[1:]))
            def _():
                self.plane_line(chunk).start()

            return
        for i in (1, 2, 3, 0):
            z = lax.rem(self.z + i, 4)
            self.add(chunk, chunk.place(self.core, p, s, z), name, z * chunk.height, 1)
            if i:
                self.start(self.line, chunk, i)

    def d(self, chunk):
        if chunk.kind == "line":
            p, _, s, _ = self.of(chunk)
            self.quarter(chunk).wait_recv()
            start = chunk.place(self.core, p, s, self.z)
            arrived = INBOX["quarter " + chunk.name][0]
            own = chunk.ref(self.r)[pl.ds(pl.multiple_of(start, 16), PIECE), :]
            self.give(chunk.name, own + self.r.inbox[arrived : arrived + PIECE, :])
            return
        for i in (1, 2, 3):
            self.line(chunk, i).wait_recv()
        self.give(chunk.name, self.total(chunk, chunk.name, self.mine_of(chunk, self.z), 1))

    def d_planes(self, _):
        r, (start, rows, index) = self.r, INBOX["line1 p"]
        p, _, s, _ = self.of(None)
        total = jnp.zeros((rows, BLOCK), F32)
        for z in range(4):
            here = pl.multiple_of(CHUNKS[f"p{z}"].place(self.core, p, s, 0), 16)
            total = jnp.where(self.z == z, r.grads[pl.ds(here, rows), :].astype(F32), total)
        for i in (1, 2, 3):
            at = start + (i - 1) * rows
            arrived = r.inbox.at[at : at + rows]
            remote(arrived, arrived, r.sum_sem.at[0, index], r.sum_sem.at[1, index + i - 1], self.z_peers[3 - i]).wait_recv()
            total = total + arrived[...].astype(F32)
        self.give("p", total.astype(BF16))

    def quarters(self, name):
        refs = [self.r.inbox.at[pl.ds(*INBOX[f"share{i} " + name][:2])] for i in range(4)]
        if name in TWO_STEPS:
            self.far(name).wait_recv()
            _, first, _, then = self.of(None)
            return zip((self.mine, first[0], then[0], 3 - self.mine), refs)
        for i in (1, 2, 3):
            self.share(name, i).wait_recv()
        return zip([lax.rem(self.mine + 4 - i, 4) for i in range(4)], refs)

    def e(self, chunk):
        r, name = self.r, chunk.name
        plane = chunk.kind == "plane"
        arrived = self.quarters("p" if plane else name)
        if chunk.kind == "whole":
            total = functools.reduce(jnp.add, [ref[...].astype(F32) for _, ref in arrived])
            if name == "k":
                for i in range(2):
                    rows = slice(384 + i * PIECE // 2, 384 + (i + 1) * PIECE // 2)
                    r.scores[rows, 768 : 768 + LANES] = total[:, i * LANES : (i + 1) * LANES]
                self.write(r.scores.at[384 : 384 + PIECE, : r.grad_qkv.shape[1]], r.grad_qkv)
                return
            r.grad_bq[...] = total[0, : r.grad_bq.shape[0]]
            for i in range(3):
                r.grad_bfc[i * LANES : (i + 1) * LANES] = total[1 + i, :LANES]
            for i, out in enumerate((r.grad_bp, r.grad_g1, r.grad_s1, r.grad_g2, r.grad_s2)):
                out[...] = total[4 + i, : out.shape[0]]
            return
        for part, ref in arrived:
            y, x = part // 2, lax.rem(part, 2)
            value = ref[...].astype(F32)
            if plane:
                for i in range(3):
                    to = pl.ds(pl.multiple_of(part * PIECE, PIECE), PIECE)
                    r.scores[to, i * BLOCK : (i + 1) * BLOCK] = value[i * PIECE : (i + 1) * PIECE]
            elif name in ("f0", "f1", "f2"):
                top = int(name[1]) * PIECE
                columns = pl.ds(pl.multiple_of(768 + part * BLOCK, BLOCK), BLOCK)
                r.scores[top : top + PIECE, columns] = value
            elif name == "uc":
                rows = pl.ds(pl.multiple_of(384 + y * PIECE // 2, 16), PIECE // 2)
                r.scores[rows, pl.ds(pl.multiple_of((1 + x) * BLOCK, BLOCK), BLOCK)] = value
            else:
                low = name == "ub"
                top = jnp.where(part == 3, 384, 288) + low * PIECE // 2
                left = jnp.where(part == 3, 0, 768 + part * BLOCK)
                rows = pl.ds(pl.multiple_of(top, 16), PIECE // 2)
                r.scores[rows, pl.ds(pl.multiple_of(left, BLOCK), BLOCK)] = value
        if plane:
            self.write(r.scores.at[:384, :768], r.grad_proj)
        elif name in ("f0", "f1", "f2"):
            k = int(name[1])
            src = r.scores.at[k * PIECE : (k + 1) * PIECE, 768 : 768 + 4 * BLOCK]
            self.write(src, r.grad_fc.at[:, 4 * k * BLOCK : 4 * (k + 1) * BLOCK])
        elif name == "ub":
            self.write(r.scores.at[288 : 288 + PIECE, 768 : 768 + 768], r.grad_o)

    def write(self, src, dst):
        copy = pltpu.make_async_copy(src, dst, self.r.out_sem.at[len(self.out_copies)])
        copy.start()
        self.out_copies.append(copy)

    def close(self):
        for copy in self.out_copies:
            copy.wait()
        for make, *args in self.sent:
            make(*args).wait_send()
        for z in range(4):

            @pl.when(self.z != z)
            def _():
                self.plane_line(CHUNKS[f"p{z}"]).wait_send()


TWO_STEPS = ("p", "f0", "f1", "f2")


def make_inbox():
    inbox, rows = {}, SLOTS * 16 * PIECE

    def add(name, count, start=None):
        nonlocal rows
        if start is None:
            start = rows
            rows += count
        inbox[name] = (start, count, len(inbox))

    for order, chunk in enumerate(CHUNKS.values()):
        name, piece = chunk.name, chunk.height
        add("pair " + name, chunk.rows // 2, order % SLOTS * 16 * PIECE)
        if chunk.kind == "plane":
            add("half " + name, 2 * chunk.count * piece)
            add("quarter " + name, chunk.count * piece)
            add("line " + name, chunk.count * piece, 0)
            continue
        if chunk.kind != "whole":
            count = 1 if chunk.kind == "line" else 4
            add("half " + name, 2 * count * piece)
            add("quarter " + name, count * piece)
        for i in (1, 2, 3):
            add(f"line{i} " + name, (4 if chunk.kind == "line" else 1) * piece)
        for i in range(4):
            add(f"share{i} " + name, piece)
    for i in (1, 2, 3):
        add(f"line{i} p", 3 * PIECE)
    for i in range(4):
        add(f"share{i} p", 3 * PIECE)
    return inbox, rows


INBOX, INBOX_ROWS = make_inbox()


def kv_copy(r, source, batch, parts, distance):
    peer = (lax.rem(source + distance, parts), batch)
    return remote(r.kv.at[source], r.kv.at[source], r.kv_sem.at[0, distance], r.kv_sem.at[1, distance], peer)


def dkv_copy(r, mine, batch, parts, distance):
    peer = (lax.rem(mine - distance + parts, parts), batch)
    return remote(
        r.dkv_out.at[distance], r.dkv_in.at[distance], r.dkv_sem.at[0, distance], r.dkv_sem.at[1, distance], peer
    )


def hand_out_kernel(count, *refs):
    sources, targets, held, sem = refs[:count], refs[count : 2 * count], refs[2 * count : -1], refs[-1]
    large = [i for i in range(count) if sources[i].ndim > 1]
    copies = [
        (
            pltpu.make_async_copy(sources[i], held[j], sem.at[0, j]),
            pltpu.make_async_copy(held[j], targets[i], sem.at[1, j]),
        )
        for j, i in enumerate(large)
    ]
    for here, _ in copies:
        here.start()
    for source, target in zip(sources, targets):
        if source.ndim == 1:
            target[...] = source[...]
    for here, there in copies:
        here.wait()
        there.start()
    for _, there in copies:
        there.wait()


def hand_out(results, specs):
    large = [pltpu.VMEM(item.shape, item.dtype) for item in results if item.ndim > 1]
    return pl.pallas_call(
        functools.partial(hand_out_kernel, len(results)),
        out_shape=[jax.ShapeDtypeStruct(item.shape, item.dtype) for item in results],
        in_specs=specs,
        out_specs=specs,
        scratch_shapes=[*large, pltpu.SemaphoreType.DMA((2, len(large)))],
        name="hand_out",
    )(*results)


def per_device(inputs, doc_ids, w_qkv, b_qkv, w_o, w_fc, b_fc, w_proj, b_proj, gain_one, shift_one, gain_two, shift_two, cotangent):
    rows_here, span, width = inputs.shape
    assert rows_here == 1
    parts = lax.axis_size("seq")
    heads = width // HEAD
    hidden_units = w_fc.shape[1]
    merged = width + 2 * HEAD
    inside = parts == 4 and lax.axis_size("batch") == 8
    vmem = pl.BlockSpec(memory_space=pltpu.VMEM)
    anywhere = pl.BlockSpec(memory_space=pl.ANY)

    small = dict(docs=doc_ids, bq=b_qkv, bfc=b_fc, bp=b_proj, g1=gain_one, s1=shift_one, g2=gain_two, s2=shift_two)
    large = dict(x_h=inputs[0], cot_h=cotangent[0], wq_h=w_qkv, wo_h=w_o, wfc_h=w_fc, wp_h=w_proj)
    outs = dict(outputs=((span, width), BF16, anywhere), input_grads=((span, width), BF16, anywhere))
    if inside:
        outs |= dict(
            grad_qkv=((width // 8, merged), F32, anywhere),
            grad_bq=((merged // 8,), F32, vmem),
            grad_o=((width // 8, width), F32, anywhere),
            grad_fc=((width // 8, hidden_units), F32, anywhere),
            grad_bfc=((hidden_units // 8,), F32, vmem),
            grad_proj=((hidden_units // 8, width), F32, anywhere),
            grad_bp=((width // 8,), F32, vmem),
            grad_g1=((width // 8,), F32, vmem),
            grad_s1=((width // 8,), F32, vmem),
            grad_g2=((width // 8,), F32, vmem),
            grad_s2=((width // 8,), F32, vmem),
        )
    else:
        outs |= dict(grads_out=((GRAD_ROWS, BLOCK), BF16, anywhere), late_out=((hidden_units, 2 * BLOCK), BF16, anywhere))
    scratch = dict(
        x=pltpu.VMEM((span, width), BF16),
        cot=pltpu.VMEM((span, width), BF16),
        wq=pltpu.VMEM((width, merged), BF16),
        wo=pltpu.VMEM((width, width), BF16),
        wfc=pltpu.VMEM((width, hidden_units), BF16),
        wp=pltpu.VMEM((hidden_units, width), BF16),
        fi=pltpu.VMEM((span, width), BF16),
        si=pltpu.VMEM((span, width), BF16),
        fit=pltpu.VMEM((width, span), BF16),
        sit=pltpu.VMEM((width, span), BF16),
        cos=pltpu.VMEM((2, ROT // 2, span), F32),
        sin=pltpu.VMEM((2, ROT // 2, span), F32),
        kv=pltpu.VMEM((parts, span, LANES), BF16),
        q=pltpu.VMEM((heads + 2, span, LANES), BF16),
        qt=pltpu.VMEM((heads + 2, LANES, span), BF16),
        dot=pltpu.VMEM((width + 2 * HEAD, span), BF16),
        act=pltpu.VMEM((span, width), BF16),
        gh=pltpu.VMEM((span, width), BF16),
        result=pltpu.VMEM((span, width), F32),
        second=pltpu.VMEM((span, width), F32),
        sum_fc=pltpu.VMEM((8, hidden_units), F32),
        kx=pltpu.VMEM((parts, span, LANES), BF16),
        kxt=pltpu.VMEM((parts, LANES, span), BF16),
        vx=pltpu.VMEM((parts, span, LANES), BF16),
        vxt=pltpu.VMEM((parts, LANES, span), BF16),
        dk=pltpu.VMEM((parts, span, LANES), F32),
        dv=pltpu.VMEM((parts, span, LANES), F32),
        scores=pltpu.VMEM((span, parts * span), F32),
        ga=pltpu.VMEM((LANES, span), BF16),
        gat=pltpu.VMEM((span, LANES), BF16),
        attt=pltpu.VMEM((width + 2 * HEAD, span), BF16),
        gqt=pltpu.VMEM((width + 2 * HEAD, span), BF16),
        gkvt=pltpu.VMEM((2 * HEAD, span), BF16),
        dkv_out=pltpu.VMEM((parts, span, LANES), BF16),
        dkv_in=pltpu.VMEM((parts, span, LANES), BF16),
        grads=pltpu.VMEM((GRAD_ROWS, BLOCK), BF16),
        load_sem=pltpu.SemaphoreType.DMA((6,)),
        kv_sem=pltpu.SemaphoreType.DMA((2, parts)),
        dkv_sem=pltpu.SemaphoreType.DMA((2, parts)),
        lent_sem=pltpu.SemaphoreType.DMA((2, 2)),
        back_sem=pltpu.SemaphoreType.DMA((2, 2)),
    )
    if inside:
        scratch |= dict(
            inbox=pltpu.VMEM((INBOX_ROWS, BLOCK), BF16),
            sum_sem=pltpu.SemaphoreType.DMA((2, len(INBOX))),
            out_sem=pltpu.SemaphoreType.DMA((6,)),
            free_sem=pltpu.SemaphoreType.REGULAR((SLOTS,)),
        )
    names = [*small, *large, *outs, *scratch]
    results = pl.pallas_call(
        functools.partial(layer_kernel, names, parts, inside),
        out_shape=[jax.ShapeDtypeStruct(shape, dtype) for shape, dtype, _ in outs.values()],
        in_specs=[vmem] * len(small) + [anywhere] * len(large),
        out_specs=[spec for _, _, spec in outs.values()],
        scratch_shapes=list(scratch.values()),
        compiler_params=pltpu.CompilerParams(
            collective_id=0, has_side_effects=True, vmem_limit_bytes=63 * 2**20
        ),
        name="layer",
    )(*small.values(), *large.values())
    if inside:
        outputs, input_grads, *shards = hand_out(results, [spec for _, _, spec in outs.values()])
        return (outputs[None], input_grads[None], *shards)
    outputs, input_grads, *shards = results

    grads, late = shards
    planes = [CHUNKS[f"p{z}"].unfold(grads).transpose(0, 1, 2, 4, 3, 5).reshape(-1, width) for z in range(4)]
    proj = jnp.concatenate(planes)
    columns = [
        CHUNKS[name].unfold(grads).transpose(3, 0, 4, 1, 2, 5).reshape(width, 4 * BLOCK) for name in ("f0", "f1", "f2")
    ]
    fc = jnp.concatenate(columns, axis=1)
    halves = [CHUNKS[name].unfold(late[:, :BLOCK]).transpose(3, 0, 4, 1, 2, 5) for name in ("ua", "ub")]
    both = jnp.stack(halves, axis=2).reshape(width, 4 * BLOCK)
    o = both[:, :width]
    rest = CHUNKS["uc"].unfold(late[:, BLOCK:]).transpose(3, 0, 1, 4, 2, 5).reshape(width, 2 * BLOCK)
    last = CHUNKS["k"].unfold(late[:, BLOCK:]).reshape(2, 4, PIECE // 2, 2, LANES).transpose(1, 0, 3, 2, 4)
    qkv = jnp.concatenate([both[:, width:], rest, last.reshape(width, LANES)], axis=1)
    blocks = 8
    lines = CHUNKS["v"].unfold(late[:, BLOCK:]).transpose(1, 0, 2, 3).reshape(blocks, 16, BLOCK)[..., :LANES]
    vectors = [lines[:, 0, : merged // blocks], lines[:, 1:4]] + [lines[:, i, : width // blocks] for i in range(4, 9)]
    vectors = [vector.reshape(-1) for vector in vectors]
    every = [qkv, vectors[0], o, fc, vectors[1], proj, *vectors[2:]]
    shards = [lax.psum_scatter(item, "batch", scatter_dimension=0, tiled=True) for item in every]
    shards = [lax.psum(item, "seq").astype(F32) for item in shards]
    return (outputs[None], input_grads[None], *shards)


def solution(mesh):
    whole, part = P(), P("batch", "seq", None)
    in_specs = (part, P("batch", None), *[whole] * 11, part)
    matrix, vector = P("batch", None), P("batch")
    out_specs = (part, part, matrix, vector, matrix, matrix, vector, matrix, *[vector] * 5)
    return jax.shard_map(per_device, mesh=mesh, in_specs=in_specs, out_specs=out_specs, check_vma=False)
```

```python
import functools
import math
import types

import jax
import jax.numpy as jnp
import numpy as np
from jax import lax
from jax.experimental import pallas as pl
from jax.experimental.pallas import tpu as pltpu
from jax.sharding import PartitionSpec as P

HEAD = 64
ROT = 16
EPSILON = 1e-05
LANES = 128
BLOCK = 256
FAR = -1e30
LOG2E = math.log2(math.e)
MESH = pl.DeviceIdType.MESH
F32 = jnp.float32
BF16 = jnp.bfloat16

PIECE = 96
SLOTS = 4


class Chunk:
    def __init__(self, name, kind, height, count, base, lane):
        self.name, self.kind = name, kind
        self.height, self.count, self.base, self.lane = height, count, base, lane

    @property
    def rows(self):
        return self.height * self.count * (2 if self.kind == "whole" else 8)

    def place(self, core, p, s, i):
        if self.kind == "whole":
            at = core * 4 + i
        elif self.kind == "line":
            at = ((core * 4 + i) * 2 + p) * 2 + s
        else:
            at = ((core * 2 + p) * 2 + s) * self.count + i
        return self.base + at * self.height

    def ref(self, r):
        if self.lane is None:
            return r.grads
        return r.wp.at[:, self.lane * BLOCK : (self.lane + 1) * BLOCK]

    @staticmethod
    def split(core, y, x):
        return (y, x) if core else (x, y)

    def unfold(self, array):
        array = array[self.base : self.base + self.rows]
        if self.kind == "whole":
            return array.reshape(2, 4, self.height, BLOCK)
        if self.kind == "line":
            array = array.reshape(2, 4, 2, 2, self.height, BLOCK).transpose(0, 2, 3, 1, 4, 5)
        else:
            array = array.reshape(2, 2, 2, self.count, self.height, BLOCK)
        return jnp.stack([array[0].swapaxes(0, 1), array[1]])


def make_chunks():
    plans = [
        ("p0", "plane", PIECE, 3, None),
        ("p1", "plane", PIECE, 3, None),
        ("f0", "line", PIECE, 4, None),
        ("p2", "plane", PIECE, 3, None),
        ("f1", "line", PIECE, 4, None),
        ("p3", "plane", PIECE, 3, None),
        ("f2", "block", PIECE, 4, None),
        ("uc", "block", PIECE // 2, 4, 1),
        ("ua", "block", PIECE // 2, 4, 0),
        ("ub", "block", PIECE // 2, 4, 0),
        ("k", "whole", PIECE // 2, 4, 1),
        ("v", "whole", 16, 4, 1),
    ]
    chunks, filled = {}, {}
    for name, kind, height, count, lane in sorted(plans, key=lambda plan: plan[1] != "plane"):
        chunk = Chunk(name, kind, height, count, filled.get(lane, 0), lane)
        chunks[name] = chunk
        filled[lane] = chunk.base + chunk.rows
    return {plan[0]: chunks[plan[0]] for plan in plans}, filled[None]


CHUNKS, GRAD_ROWS = make_chunks()


def mm(a, b, ca=1, cb=0):
    return lax.dot_general(a, b, (((ca,), (cb,)), ((), ())), preferred_element_type=F32)


def flip(value):
    return value.astype(F32).T


def lanes_of(shape):
    return lax.broadcasted_iota(jnp.int32, shape, 1)


def rows_of(shape):
    return lax.broadcasted_iota(jnp.int32, shape, 0)


EARLY_DONE = 64

FEED_SCHEDULE = [
    ([], [], []),
    ([], ["send:p0", "send:p1"], ["send:f0"]),
    (["a:f0", "a:p1"], ["a:p0"], ["send:p2"]),
    ([], [], ["a:p2"]),
    ["send:f1", "b:p1", "send:p3", "send:f2"],
]

SCHEDULE = {
    4: ["a:p3"],
    8: ["a:f2"],
    12: ["a:f1", "b:p2"],
    28: ["c:p1"],
    32: ["b:f0"],
    36: ["b:f2", "b:p0"],
    44: ["c:f0"],
    48: ["c:f2"],
    52: ["c:p0"],
    60: ["b:p3"],
    EARLY_DONE: ["make:uc", "send:uc", "d:f0"],
    68: ["a:uc", "c:p3"],
    72: ["b:f1", "g:f0"],
    76: ["b:uc"],
}

LATE_SCHEDULE = [
    ["c:f1"],
    ["c:p2", "c:uc", "send:ua", "a:ua", "send:ub", "d:f2", "a:ub"],
    ["send:k", "b:ua", "a:k", "b:ub", "d:f1", "c:ua", "d_planes:p0", "g:f2"],
    ["g:f1", "c:ub", "send:v", "d:uc", "g:p0", "a:v", "d:k"],
    ["d:ua", "e:f0", "e:f1", "e:f2", "d:ub", "d:v", "e:p0", "e:ua", "e:uc", "e:ub", "e:k", "e:v"],
]

LENT = 5


def gelu_parts(hidden):
    size = jnp.abs(hidden)
    t = pl.reciprocal(1.0 + (0.3275911 / math.sqrt(2.0)) * size)
    bell = jnp.exp2(hidden * hidden * (-0.5 * LOG2E))
    poly = 0.5 * 1.061405429
    for term in (-1.453152027, 1.421413741, -0.284496736, 0.254829592):
        poly = poly * t + 0.5 * term
    tail = poly * t * bell
    below = jnp.where(hidden >= 0, 1.0 - tail, tail)
    return below, hidden * bell * (1.0 / math.sqrt(2.0 * math.pi))


def layer_kernel(names, parts, inside, *refs):
    r = types.SimpleNamespace(**dict(zip(names, refs, strict=True)))
    span, width = r.x.shape
    hidden_units = r.wfc.shape[1]
    heads = width // HEAD
    mine = lax.axis_index("seq")
    batch = lax.axis_index("batch")
    partner = parts - 1 - mine
    high = jnp.maximum(mine, partner)

    loads = [
        pltpu.make_async_copy(src, dst, r.load_sem.at[i])
        for i, (src, dst) in enumerate(
            [(r.x_h, r.x), (r.wq_h, r.wq), (r.cot_h, r.cot), (r.wo_h, r.wo), (r.wfc_h, r.wfc), (r.wp_h, r.wp)]
        )
    ]
    for load in loads:
        load.start()

    barrier = pltpu.get_barrier_semaphore()
    peers = [(lax.rem(mine + distance, parts), batch) for distance in range(1, parts)]
    summing = Summing(r, mine, batch, parts) if inside else None
    if inside:
        peers += [summing.core_peer, *summing.z_peers]
    for peer in peers:
        pl.semaphore_signal(barrier, inc=1, device_id=peer, device_id_type=MESH)
    pl.semaphore_wait(barrier, len(peers))

    def keep(name, core, y, x, i, value):
        chunk = CHUNKS[name]
        row = chunk.place(core, *chunk.split(core, y, x), i)
        chunk.ref(r)[row : row + chunk.height, :] = value.astype(BF16)

    def step(steps):
        for item in steps if inside else ():
            kind, name = item.split(":")
            if kind == "make":
                make_early()
            else:
                getattr(summing, kind)(CHUNKS[name])

    loads[0].wait()

    def norm_tile(i):
        tokens = r.x[pl.ds(i * LANES, LANES), :].astype(F32)
        average = jnp.mean(tokens, axis=-1, keepdims=True)
        centered = tokens - average
        variance = jnp.mean(centered * centered, axis=-1, keepdims=True)
        inverse_std = lax.rsqrt(variance + EPSILON)
        return centered * inverse_std, inverse_std

    for i in range(span // LANES):
        normed, _ = norm_tile(i)
        rows = pl.ds(i * LANES, LANES)
        first = normed * r.g1[...][None] + r.s1[...][None]
        second = normed * r.g2[...][None] + r.s2[...][None]
        r.fi[rows, :] = first.astype(BF16)
        r.si[rows, :] = second.astype(BF16)
        r.fit[:, rows] = first.T.astype(BF16)
        r.sit[:, rows] = second.T.astype(BF16)

    half = ROT // 2
    index = rows_of((half, span))
    frequency = jnp.zeros((half, span), F32)
    for i in range(half):
        frequency = jnp.where(index == i, np.float32(10000.0 ** (-2.0 * i / ROT)), frequency)
    for i, part in enumerate((mine, partner)):
        angle = (part * span + lanes_of((half, span))).astype(F32) * frequency
        r.cos[i] = jnp.cos(angle)
        r.sin[i] = jnp.sin(angle)
    cosine, sine = r.cos[0], r.sin[0]
    ones = jnp.ones((HEAD - ROT, span), F32)
    zeros = jnp.zeros((HEAD - ROT, span), F32)
    table_cos = jnp.concatenate([cosine, cosine, ones] * 2, axis=0).T
    table_sin = jnp.concatenate([-sine, sine, zeros] * 2, axis=0).T
    lane = lanes_of((span, LANES))

    def rotate(tile, cos_of, sin_of):
        partner = jnp.where(
            lax.rem(lane, HEAD) < half, pltpu.roll(tile, LANES - half, 1), pltpu.roll(tile, half, 1)
        )
        return tile * cos_of + partner * sin_of

    def docs_row(part):
        return r.docs[0:1, pl.ds(pl.multiple_of(part * span, LANES), span)]

    loads[1].wait()
    key_value = mm(r.fi[...], r.wq[:, width:]) + r.bq[width:][None]
    low = lane < HEAD
    key_value = rotate(key_value, jnp.where(low, table_cos, 1.0), jnp.where(low, table_sin, 0.0))
    r.kv[mine] = key_value.astype(BF16)

    def needs(part, source):
        return (part > source) | (part == 0)

    for distance in range(1, parts):

        @pl.when(needs(lax.rem(mine + distance, parts), mine))
        def _():
            kv_copy(r, mine, batch, parts, distance).start()

    feature_row = rows_of((LANES, span)) - HEAD

    def keep_queries(slot, tile, feature):
        for i, head in enumerate((tile, pltpu.roll(tile, HEAD, 1))):
            head = jnp.where(low, head, feature)
            r.q[slot + i] = head.astype(BF16)
            r.qt[slot + i] = head.T.astype(BF16)

    query_feature = jnp.where(feature_row == docs_row(mine), 1.0, 0.0).T
    for i in range(heads // 2):
        columns = slice(i * LANES, (i + 1) * LANES)
        tile = mm(r.fi[...], r.wq[:, columns]) + r.bq[columns][None]
        tile = rotate(tile, table_cos, table_sin) * (LOG2E / math.sqrt(HEAD))
        keep_queries(2 * i, tile, query_feature)
        if i == LENT:
            r.dkv_out[0] = tile.astype(BF16)

    loads[2].wait()
    loads[3].wait()
    for i in range(width // BLOCK):
        rows = slice(i * BLOCK, (i + 1) * BLOCK)
        r.dot[rows, :] = mm(r.wo[rows, :], r.cot[...], 1, 1).astype(BF16)

    @pl.when(mine == parts - 1)
    def _():
        for copy in lent_copies(r, mine, batch, parts):
            copy.start()


    loads[4].wait()
    loads[5].wait()
    r.result[...] = jnp.zeros_like(r.result)
    r.second[...] = jnp.zeros_like(r.second)
    ones_rows = jnp.ones((8, span), BF16)
    group = 2 * 4 * 96

    def feed_steps(g, i):
        for group_of, steps in enumerate(FEED_SCHEDULE[:-1]):
            if steps[i]:

                @pl.when(g == group_of)
                def _():
                    step(steps[i])

    plane, line, block = CHUNKS["p0"], CHUNKS["f0"], CHUNKS["f2"]
    lines = sum(chunk.kind == "line" for chunk in CHUNKS.values())

    def feed_forward(g, _):
        columns = pl.ds(pl.multiple_of(g * group, LANES), group)
        hidden = mm(r.si[...], r.wfc[:, columns]) + r.bfc[columns][None]
        grad_act = mm(r.cot[...], r.wp[columns, :], 1, 1)
        below, slope = gelu_parts(hidden)
        r.act[...] = (hidden * below).astype(BF16)
        r.gh[...] = (grad_act * (below + slope)).astype(BF16)
        feed_steps(g, 0)
        grad_w = mm(r.act[...], r.cot[...], 0, 0)
        for c in range(2):
            for q in range(4):
                row = (c * 4 + q) * PIECE
                for k in range(3):
                    to = g * plane.rows + plane.place(c, *plane.split(c, q // 2, q % 2), k)
                    piece = grad_w[row : row + PIECE, k * BLOCK : (k + 1) * BLOCK]
                    r.grads[pl.ds(pl.multiple_of(to, 16), PIECE), :] = piece.astype(BF16)
        feed_steps(g, 1)
        grad_w = mm(r.sit[...], r.gh[...])
        for k in range(group // BLOCK):
            at = g * (group // BLOCK) + k
            chunk, y, x = at // 4, lax.rem(at, 4) // 2, lax.rem(at, 2)
            for b in range(8):
                c, z = b % 2, b // 2
                p, s = line.split(c, y, x)
                later = block.place(c, p, s, z) + (chunk - 2) * block.rows
                to = jnp.where(chunk < lines, line.place(c, p, s, z) + chunk * line.rows, later)
                piece = grad_w[b * PIECE : (b + 1) * PIECE, k * BLOCK : (k + 1) * BLOCK]
                r.grads[pl.ds(pl.multiple_of(to, 16), PIECE), :] = piece.astype(BF16)
        feed_steps(g, 2)
        r.sum_fc[:, columns] = mm(ones_rows, r.gh[...])
        r.result[...] += mm(r.act[...], r.wp[columns, :])
        r.second[...] += mm(r.gh[...], r.wfc[:, columns], 1, 1)
        return 0

    lax.fori_loop(0, hidden_units // group, feed_forward, 0)
    step(FEED_SCHEDULE[4])

    for distance in range(1, parts):
        source = lax.rem(mine - distance + parts, parts)

        @pl.when(needs(mine, source))
        def _():
            kv_copy(r, source, batch, parts, distance).wait_recv()

    def prepare(part):
        apart = (feature_row >= 0) & (feature_row < 8) & (feature_row != docs_row(part))
        key_feature = jnp.where(apart, FAR, 0.0).T
        pair = r.kv[part].astype(F32)
        keys = jnp.where(low, pair, key_feature)
        values = jnp.where(low, pltpu.roll(pair, HEAD, 1), jnp.where(lane < HEAD + 2, 1.0, 0.0))
        r.kx[part] = keys.astype(BF16)
        r.kxt[part] = keys.T.astype(BF16)
        r.vx[part] = values.astype(BF16)
        r.vxt[part] = values.T.astype(BF16)

    for part in range(parts):
        pl.when((mine >= part) | (mine == 0))(functools.partial(prepare, part))

    @pl.when(mine == 0)
    def _():
        for copy in lent_copies(r, mine, batch, parts):
            copy.wait_recv()
        feature = jnp.where(feature_row == docs_row(partner), 1.0, 0.0).T
        keep_queries(heads, r.dkv_in[0].astype(F32), feature)

    r.dk[...] = jnp.zeros_like(r.dk)
    r.dv[...] = jnp.zeros_like(r.dv)

    def make_early():
        @pl.when(mine == parts - 1)
        def _():
            for copy in back_copies(r, mine, batch, parts):
                copy.wait_recv()

        grad_q = mm(r.fit[...], r.gqt[BLOCK:width, :], 1, 1)
        for b in range(8):
            for y in range(2):
                rows = slice(b * PIECE + y * PIECE // 2, b * PIECE + (y + 1) * PIECE // 2)
                for x in range(2):
                    keep("uc", b % 2, y, x, b // 2, grad_q[rows, x * BLOCK : (x + 1) * BLOCK])

    def packed(part):
        return jnp.where(low, r.dk[part] * (1.0 / LOG2E), pltpu.roll(r.dv[part], HEAD, 1))

    def send_key_grads(distance):
        r.dkv_out[distance] = packed(lax.rem(mine - distance + parts, parts)).astype(BF16)
        dkv_copy(r, mine, batch, parts, distance).start()

    mid = span // 2

    def tiles_of(last):
        return [(part, 0, span, 0) for part in range(last)] + [(last, 0, mid, 0), (last, mid, mid, mid)]

    def spread(value, start):
        return jnp.concatenate([jnp.zeros((value.shape[0], start), F32), value], axis=1) if start else value

    def attend(slot, last):
        rows = pl.ds(pl.multiple_of(slot * HEAD, HEAD), HEAD)
        tiles = tiles_of(last)
        tops = []
        for part, k0, count, q0 in tiles:
            raw = mm(r.kx[part, k0 : k0 + count], r.qt[slot, :, q0:])
            if part == last:
                raw = jnp.where(rows_of(raw.shape) <= lanes_of(raw.shape), raw, FAR)
            r.scores[k0 : k0 + count, part * span + q0 : (part + 1) * span] = raw
            top = jnp.max(raw, axis=0, keepdims=True)
            tops.append(jnp.concatenate([jnp.full((1, q0), FAR, F32), top], axis=1) if q0 else top)
        top = functools.reduce(jnp.maximum, tops)
        sums = []
        for part, k0, count, q0 in tiles:
            place = slice(k0, k0 + count), slice(part * span + q0, (part + 1) * span)
            raised = jnp.exp2(r.scores[place] - top[:, q0:]).astype(BF16)
            r.wfc[place] = raised
            sums.append(spread(mm(r.vxt[part, :, k0 : k0 + count], raised), q0))
        att = functools.reduce(jnp.add, sums)
        inverse = 1.0 / att[HEAD : HEAD + 1, :]
        attended = att[:HEAD, :] * inverse
        r.attt[rows, :] = attended.astype(BF16)
        grad_att = r.dot[rows, :].astype(F32)
        delta = jnp.sum(grad_att * attended, axis=0, keepdims=True) * -inverse
        delta_high = delta.astype(BF16).astype(F32)
        row = rows_of((HEAD, span))
        extra = jnp.where(row == 0, delta_high, jnp.where(row == 1, delta - delta_high, 0.0))
        grad_att = jnp.concatenate([grad_att * inverse, extra], axis=0)
        r.ga[...] = grad_att.astype(BF16)
        r.gat[...] = grad_att.T.astype(BF16)

    def attend_back(slot, borrowed, last):
        rows = pl.ds(pl.multiple_of(slot * HEAD, HEAD), HEAD)
        tiles = tiles_of(last)
        sums = []
        for part, k0, count, q0 in tiles:
            keys = slice(k0, k0 + count)
            grad_probs = mm(r.vx[part, keys], r.ga[:, q0:])
            raised = r.wfc[keys, part * span + q0 : (part + 1) * span]
            grad_scores = (raised.astype(F32) * grad_probs).astype(BF16)
            r.dv[part, keys] += mm(raised, r.gat[q0:])
            r.dk[part, keys] += mm(grad_scores, r.q[slot, q0:])
            sums.append(spread(mm(r.kxt[part, :, keys], grad_scores), q0))
        grad_query = functools.reduce(jnp.add, sums)[:HEAD] * (1.0 / math.sqrt(HEAD))
        r.gqt[rows, :] = rotate_back(r, grad_query, borrowed).astype(BF16)

    n_borrowed = jnp.where(mine == 0, 2, 0)
    n_own = jnp.where(mine == parts - 1, heads - 2, heads)
    whole = 2 * (n_borrowed * (partner + 1) + n_own * (mine + 1))

    def half_task(i, done):
        t, backward = i // 2, lax.rem(i, 2) == 1
        borrowed = t < n_borrowed
        own = t - n_borrowed + 4
        own = jnp.where(own >= n_own, own - n_own, own)
        slot = jnp.where(borrowed, heads + t, own)
        last = jnp.where(borrowed, partner, mine)
        for part in range(parts):

            @pl.when((last == part) & ~backward)
            def _():
                attend(slot, part)

            @pl.when((last == part) & backward)
            def _():
                attend_back(slot, jnp.where(borrowed, 1, 0), part)


        @pl.when((mine == 0) & backward & (slot == heads + 1))
        def _():
            for copy in back_copies(r, mine, batch, parts):
                copy.start()

        after = done + last + 1
        before_80, after_80 = done * 80 // whole, after * 80 // whole
        for when, steps in SCHEDULE.items():

            @pl.when((before_80 < when) & (when <= after_80))
            def _():
                step(steps)

        return after

    lax.fori_loop(0, 2 * (n_borrowed + n_own), half_task, 0)
    step(LATE_SCHEDULE[0])

    for distance in reversed(range(1, parts)):

        @pl.when(lax.rem(mine - distance + parts, parts) <= high)
        def _():
            send_key_grads(distance)

    if not inside:
        make_early()
    grad_w = mm(r.attt[:width, :], r.cot[...])
    grad_q = mm(r.fit[...], r.gqt[:BLOCK, :], 1, 1)
    for b in range(8):
        core, z = b % 2, b // 2
        for i, name in enumerate(("ua", "ub")):
            rows = slice(b * PIECE + i * PIECE // 2, b * PIECE + (i + 1) * PIECE // 2)
            for q in range(4):
                piece = grad_w[rows, q * BLOCK : (q + 1) * BLOCK] if q < 3 else grad_q[rows]
                keep(name, core, q // 2, q % 2, z, piece)
    step(LATE_SCHEDULE[1])

    r.dk[mine] = packed(mine)
    for distance in range(1, parts):
        source = lax.rem(mine + distance, parts)

        @pl.when(mine <= jnp.maximum(source, parts - 1 - source))
        def _():
            dkv_copy(r, mine, batch, parts, distance).wait_recv()
            r.dk[mine] += r.dkv_in[distance].astype(F32)

    pair = r.dk[mine].T
    r.gkvt[:HEAD, :] = rotate_back(r, pair[:HEAD], 0).astype(BF16)
    r.gkvt[HEAD:, :] = pair[HEAD:].astype(BF16)

    grad_kv = mm(r.fit[...], r.gkvt[...], 1, 1)
    for b in range(8):
        halves = [grad_kv[b * PIECE + i * PIECE // 2 : b * PIECE + (i + 1) * PIECE // 2] for i in range(2)]
        keep("k", b % 2, 0, 0, b // 2, jnp.concatenate(halves, axis=1))
    step(LATE_SCHEDULE[2])
    for i in range(width // LANES):
        columns = slice(i * LANES, (i + 1) * LANES)
        r.act[:, columns] = flip(r.gqt[columns, :]).astype(BF16)
    r.gh[:, :LANES] = flip(r.gkvt[...]).astype(BF16)

    first = mm(r.act[...], r.wq[:, :width], 1, 1) + mm(r.gh[:, :LANES], r.wq[:, width:], 1, 1)
    for i in range(width // LANES):
        (r.dk if i < parts else r.dv)[i % parts] = first[:, i * LANES : (i + 1) * LANES]
    sums = [jnp.zeros((1, width), F32) for _ in range(4)]
    for i in range(span // LANES):
        rows = pl.ds(i * LANES, LANES)
        normed, inverse_std = norm_tile(i)
        first = [(r.dk if j < parts else r.dv)[j % parts, rows, :] for j in range(width // LANES)]
        first, second = jnp.concatenate(first, axis=1), r.second[rows, :]
        for j, term in enumerate((normed * first, first, normed * second, second)):
            sums[j] = sums[j] + jnp.sum(term, axis=0, keepdims=True)
        scaled = first * r.g1[...][None] + second * r.g2[...][None]
        mean_one = jnp.mean(scaled, axis=-1, keepdims=True)
        mean_two = jnp.mean(scaled * normed, axis=-1, keepdims=True)
        back = inverse_std * (scaled - mean_one - normed * mean_two)
        r.si[rows, :] = (r.cot[rows, :].astype(F32) + back).astype(BF16)

    sum_qkv = jnp.concatenate([mm(ones_rows, r.gqt[:width, :], 1, 1), mm(ones_rows, r.gkvt[...], 1, 1)], axis=1)[0:1]
    sum_proj = mm(ones_rows, r.cot[...])[0:1]
    for b in range(8):
        lines = [cut(sum_qkv, b * 112, 112)]
        lines += [r.sum_fc[0:1, b * 384 + i * LANES : b * 384 + (i + 1) * LANES] for i in range(3)]
        lines += [cut(line, b * 96, 96) for line in (sum_proj, *sums)]
        lines.append(jnp.zeros((16 - len(lines), LANES), F32))
        lines = jnp.concatenate(lines, axis=0)
        keep("v", b % 2, 0, 0, b // 2, jnp.concatenate([lines, jnp.zeros_like(lines)], axis=1))
    step(LATE_SCHEDULE[3])
    copies = [pltpu.make_async_copy(r.si, r.input_grads, r.load_sem.at[0])]
    copies[0].start()

    for i in range(width // LANES):
        columns = slice(i * LANES, (i + 1) * LANES)
        r.fi[:, columns] = flip(r.attt[columns, :]).astype(BF16)
    r.x[...] = (r.result[...] + r.x[...].astype(F32) + r.bp[...][None] + mm(r.fi[...], r.wo[...])).astype(BF16)
    copies.append(pltpu.make_async_copy(r.x, r.outputs, r.load_sem.at[1]))
    copies[1].start()

    if inside:
        step(LATE_SCHEDULE[4])
        summing.close()
    else:
        copies.append(pltpu.make_async_copy(r.grads, r.grads_out, r.load_sem.at[2]))
        copies.append(pltpu.make_async_copy(r.wp.at[:, : 2 * BLOCK], r.late_out, r.load_sem.at[3]))
        for copy in copies[2:]:
            copy.start()
    for copy in copies:
        copy.wait()
    for distance in range(1, parts):

        @pl.when(needs(lax.rem(mine + distance, parts), mine))
        def _():
            kv_copy(r, mine, batch, parts, distance).wait_send()

        target = lax.rem(mine - distance + parts, parts)

        @pl.when(target <= high)
        def _():
            dkv_copy(r, mine, batch, parts, distance).wait_send()


    @pl.when(mine == parts - 1)
    def _():
        for copy in lent_copies(r, mine, batch, parts):
            copy.wait_send()

    @pl.when(mine == 0)
    def _():
        for copy in back_copies(r, mine, batch, parts):
            copy.wait_send()


def cut(line, start, size):
    line = jnp.concatenate([line, jnp.zeros((1, LANES), F32)], axis=1)
    base = start // LANES * LANES
    line = line[:, base : base + 2 * LANES]
    shift = start - base
    if shift:
        line = pltpu.roll(line, 2 * LANES - shift, 1)
    return jnp.where(lanes_of((1, LANES)) < size, line[:, :LANES], 0.0)


def rotate_back(r, grads, which):
    half = ROT // 2
    one, two = grads[:half], grads[half:ROT]
    cosine, sine = r.cos[which], r.sin[which]
    return jnp.concatenate([one * cosine + two * sine, two * cosine - one * sine, grads[ROT:]], axis=0)


def remote(src, dst, send_sem, recv_sem, peer):
    return pltpu.make_async_remote_copy(
        src_ref=src, dst_ref=dst, send_sem=send_sem, recv_sem=recv_sem, device_id=peer, device_id_type=MESH
    )


def lent_copies(r, mine, batch, parts):
    peer, rows, there = (parts - 1 - mine, batch), LENT * LANES, r.dot.shape[0] - LANES
    return [
        remote(r.dkv_out.at[0], r.dkv_in.at[0], r.lent_sem.at[0, 0], r.lent_sem.at[1, 0], peer),
        remote(
            r.dot.at[rows : rows + LANES],
            r.dot.at[there : there + LANES],
            r.lent_sem.at[0, 1],
            r.lent_sem.at[1, 1],
            peer,
        ),
    ]


def back_copies(r, mine, batch, parts):
    peer, rows, here = (parts - 1 - mine, batch), LENT * LANES, r.dot.shape[0] - LANES
    return [
        remote(ref.at[here : here + LANES], ref.at[rows : rows + LANES], r.back_sem.at[0, j], r.back_sem.at[1, j], peer)
        for j, ref in enumerate((r.attt, r.gqt))
    ]


class Summing:
    def __init__(self, r, mine, batch, parts):
        self.r, self.mine, self.batch, self.parts = r, mine, batch, parts
        y, x = mine // 2, lax.rem(mine, 2)
        self.z, self.core = batch // 2, lax.rem(batch, 2)
        self.axes = {"x": (x, (y * 2 + 1 - x, batch)), "y": (y, ((1 - y) * 2 + x, batch))}
        self.core_peer = (mine, self.z * 2 + 1 - self.core)
        self.z_peers = [(mine, lax.rem(self.z + i, 4) * 2 + self.core) for i in (1, 2, 3)]
        self.seq_peers = [(lax.rem(mine + i, parts), batch) for i in range(1, parts)]
        self.out_copies, self.sent = [], []

    def of(self, _):
        (y, y_peer), (x, x_peer) = self.axes["y"], self.axes["x"]
        p, s = jnp.where(self.core == 0, x, y), jnp.where(self.core == 0, y, x)
        part_x, part_y = x_peer[0], y_peer[0]
        first, then = jnp.where(self.core == 0, part_x, part_y), jnp.where(self.core == 0, part_y, part_x)
        return p, (first, self.batch), s, (then, self.batch)

    def copy(self, name, src, peer, to=None, sem=None):
        start, rows, index = INBOX[name]
        to = start if to is None else to
        return remote(
            src,
            self.r.inbox.at[pl.ds(to, rows)],
            self.r.sum_sem.at[0, index],
            self.r.sum_sem.at[1, index if sem is None else sem],
            peer,
        )

    def start(self, make, *args):
        make(*args).start()
        self.sent.append((make, *args))

    def rows(self, chunk, start, pieces):
        return chunk.ref(self.r).at[pl.ds(pl.multiple_of(start, 16), pieces * chunk.height)]

    def add(self, chunk, start, name, offset, pieces):
        ref, height, from_row = chunk.ref(self.r), chunk.height, INBOX[name][0] + offset

        def one(i, _):
            to = pl.ds(pl.multiple_of(start + i * height, 16), height)
            ref[to, :] += self.r.inbox[pl.ds(pl.multiple_of(from_row + i * height, 16), height), :]
            return 0

        lax.fori_loop(0, pieces, one, 0)

    def pair(self, chunk):
        rows = chunk.rows // 2
        src = chunk.ref(self.r).at[pl.ds(pl.multiple_of(chunk.base + (1 - self.core) * rows, 16), rows)]
        return self.copy("pair " + chunk.name, src, self.core_peer)

    def half(self, chunk):
        p, peer, _, _ = self.of(chunk)
        if chunk.kind == "line":
            return self.copy("half " + chunk.name, self.rows(chunk, chunk.place(self.core, 1 - p, 0, self.z), 2), peer)
        src = self.rows(chunk, chunk.place(self.core, 1 - p, 0, 0), 2 * chunk.count)
        return self.copy("half " + chunk.name, src, peer)

    def quarter(self, chunk):
        p, _, s, peer = self.of(chunk)
        if chunk.kind == "line":
            src = self.rows(chunk, chunk.place(self.core, p, 1 - s, self.z), 1)
        else:
            src = self.rows(chunk, chunk.place(self.core, p, 1 - s, 0), chunk.count)
        return self.copy("quarter " + chunk.name, src, peer)

    def mine_of(self, chunk, z):
        p, _, s, _ = self.of(chunk)
        if chunk.kind in ("line", "whole"):
            return chunk.place(self.core, 0, 0, z)
        return chunk.place(self.core, p, s, 0 if chunk.kind == "plane" else z)

    def pieces(self, chunk):
        return {"plane": chunk.count, "line": 4}.get(chunk.kind, 1)

    def line(self, chunk, i):
        z = lax.rem(self.z + i, 4)
        src = self.rows(chunk, self.mine_of(chunk, z), self.pieces(chunk))
        return self.copy(f"line{i} " + chunk.name, src, self.z_peers[i - 1])

    def plane_line(self, chunk):
        z = int(chunk.name[1:])
        i = lax.rem(z - self.z + 4, 4)
        start, rows, index = INBOX["line1 p"]
        src = self.rows(chunk, self.mine_of(chunk, z), chunk.count)
        return remote(
            src,
            self.r.inbox.at[pl.ds(pl.multiple_of(start + (i - 1) * rows, 16), rows)],
            self.r.sum_sem.at[0, INBOX["line " + chunk.name][2]],
            self.r.sum_sem.at[1, index + i - 1],
            (self.mine, z * 2 + self.core),
        )

    def near(self, name):
        own, rows, _ = INBOX["share0 " + name]
        start, _, index = INBOX["share1 " + name]
        sem = self.r.sum_sem
        return remote(
            self.r.inbox.at[pl.ds(own, rows)],
            self.r.inbox.at[pl.ds(start, rows)],
            sem.at[0, index],
            sem.at[1, index],
            self.of(None)[1],
        )

    def far(self, name):
        own, rows, _ = INBOX["share0 " + name]
        start, _, index = INBOX["share2 " + name]
        sem = self.r.sum_sem
        return remote(
            self.r.inbox.at[pl.ds(own, 2 * rows)],
            self.r.inbox.at[pl.ds(start, 2 * rows)],
            sem.at[0, index],
            sem.at[1, index],
            self.of(None)[3],
        )

    def share(self, name, i):
        start, rows, index = INBOX[f"share{i} " + name]
        own = INBOX["share0 " + name][0]
        return remote(
            self.r.inbox.at[pl.ds(own, rows)],
            self.r.inbox.at[pl.ds(start, rows)],
            self.r.sum_sem.at[0, index],
            self.r.sum_sem.at[1, index],
            self.seq_peers[i - 1],
        )

    def send(self, chunk):
        order = list(CHUNKS).index(chunk.name)
        if order >= SLOTS:
            pl.semaphore_wait(self.r.free_sem.at[order % SLOTS], 1)
        self.start(self.pair, chunk)

    def a(self, chunk):
        self.pair(chunk).wait_recv()
        name, base, p = "pair " + chunk.name, self.core * (chunk.rows // 2), self.of(chunk)[0]
        if chunk.kind in ("line", "whole"):
            pieces = self.pieces(chunk)
            for i in (1, 2, 3, 0):
                start = self.mine_of(chunk, lax.rem(self.z + i, 4))
                self.add(chunk, start, name, start - chunk.base - base, pieces)
                if i:
                    self.start(self.line, chunk, i)
        else:
            for side in (1 - p, p):
                start = chunk.place(self.core, side, 0, 0)
                self.add(chunk, start, name, start - chunk.base - base, 2 * chunk.count)
                if side is not p:
                    self.start(self.half, chunk)
        order = list(CHUNKS).index(chunk.name)
        if order + SLOTS < len(CHUNKS):
            free = self.r.free_sem.at[order % SLOTS]
            pl.semaphore_signal(free, inc=1, device_id=self.core_peer, device_id_type=MESH)

    def total(self, chunk, name, start, pieces):
        rows = pieces * chunk.height
        total = chunk.ref(self.r)[pl.ds(pl.multiple_of(start, 16), rows), :].astype(F32)
        for i in (1, 2, 3):
            at = INBOX[f"line{i} " + name][0]
            total = total + self.r.inbox[at : at + rows, :].astype(F32)
        return total.astype(BF16)

    def give(self, name, value):
        own, rows, _ = INBOX["share0 " + name]
        self.r.inbox[own : own + rows, :] = value
        if name in TWO_STEPS:
            self.start(self.near, name)
            return
        for i in (1, 2, 3):
            self.start(self.share, name, i)

    def g(self, chunk):
        name = "p" if chunk.kind == "plane" else chunk.name
        self.near(name).wait_recv()
        self.start(self.far, name)

    def b(self, chunk):
        p, _, s, _ = self.of(chunk)
        if chunk.kind == "line":
            for i in (1, 2, 3):
                self.line(chunk, i).wait_recv()
            start = self.mine_of(chunk, self.z)
            self.rows(chunk, start, 4)[...] = self.total(chunk, chunk.name, start, 4)
            self.start(self.half, chunk)
            return
        self.half(chunk).wait_recv()
        for side in (1 - s, s):
            offset = side * chunk.count * chunk.height
            self.add(chunk, chunk.place(self.core, p, side, 0), "half " + chunk.name, offset, chunk.count)
            if side is not s:
                self.start(self.quarter, chunk)

    def c(self, chunk):
        p, _, s, _ = self.of(chunk)
        if chunk.kind == "line":
            self.half(chunk).wait_recv()
            for side in (1 - s, s):
                self.add(chunk, chunk.place(self.core, p, side, self.z), "half " + chunk.name, side * chunk.height, 1)
                if side is not s:
                    self.start(self.quarter, chunk)
            return
        self.quarter(chunk).wait_recv()
        name = "quarter " + chunk.name
        if chunk.kind == "plane":
            self.add(chunk, chunk.place(self.core, p, s, 0), name, 0, chunk.count)


            @pl.when(self.z != int(chunk.name[1:]))
            def _():
                self.plane_line(chunk).start()

            return
        for i in (1, 2, 3, 0):
            z = lax.rem(self.z + i, 4)
            self.add(chunk, chunk.place(self.core, p, s, z), name, z * chunk.height, 1)
            if i:
                self.start(self.line, chunk, i)

    def d(self, chunk):
        if chunk.kind == "line":
            p, _, s, _ = self.of(chunk)
            self.quarter(chunk).wait_recv()
            start = chunk.place(self.core, p, s, self.z)
            arrived = INBOX["quarter " + chunk.name][0]
            own = chunk.ref(self.r)[pl.ds(pl.multiple_of(start, 16), PIECE), :]
            self.give(chunk.name, own + self.r.inbox[arrived : arrived + PIECE, :])
            return
        for i in (1, 2, 3):
            self.line(chunk, i).wait_recv()
        self.give(chunk.name, self.total(chunk, chunk.name, self.mine_of(chunk, self.z), 1))

    def d_planes(self, _):
        r, (start, rows, index) = self.r, INBOX["line1 p"]
        p, _, s, _ = self.of(None)
        total = jnp.zeros((rows, BLOCK), F32)
        for z in range(4):
            here = pl.multiple_of(CHUNKS[f"p{z}"].place(self.core, p, s, 0), 16)
            total = jnp.where(self.z == z, r.grads[pl.ds(here, rows), :].astype(F32), total)
        for i in (1, 2, 3):
            at = start + (i - 1) * rows
            arrived = r.inbox.at[at : at + rows]
            remote(arrived, arrived, r.sum_sem.at[0, index], r.sum_sem.at[1, index + i - 1], self.z_peers[3 - i]).wait_recv()
            total = total + arrived[...].astype(F32)
        self.give("p", total.astype(BF16))

    def quarters(self, name):
        refs = [self.r.inbox.at[pl.ds(*INBOX[f"share{i} " + name][:2])] for i in range(4)]
        if name in TWO_STEPS:
            self.far(name).wait_recv()
            _, first, _, then = self.of(None)
            return zip((self.mine, first[0], then[0], 3 - self.mine), refs)
        for i in (1, 2, 3):
            self.share(name, i).wait_recv()
        return zip([lax.rem(self.mine + 4 - i, 4) for i in range(4)], refs)

    def e(self, chunk):
        r, name = self.r, chunk.name
        plane = chunk.kind == "plane"
        arrived = self.quarters("p" if plane else name)
        if chunk.kind == "whole":
            total = functools.reduce(jnp.add, [ref[...].astype(F32) for _, ref in arrived])
            if name == "k":
                for i in range(2):
                    rows = slice(384 + i * PIECE // 2, 384 + (i + 1) * PIECE // 2)
                    r.scores[rows, 768 : 768 + LANES] = total[:, i * LANES : (i + 1) * LANES]
                self.write(r.scores.at[384 : 384 + PIECE, : r.grad_qkv.shape[1]], r.grad_qkv)
                return
            r.grad_bq[...] = total[0, : r.grad_bq.shape[0]]
            for i in range(3):
                r.grad_bfc[i * LANES : (i + 1) * LANES] = total[1 + i, :LANES]
            for i, out in enumerate((r.grad_bp, r.grad_g1, r.grad_s1, r.grad_g2, r.grad_s2)):
                out[...] = total[4 + i, : out.shape[0]]
            return
        for part, ref in arrived:
            y, x = part // 2, lax.rem(part, 2)
            value = ref[...].astype(F32)
            if plane:
                for i in range(3):
                    to = pl.ds(pl.multiple_of(part * PIECE, PIECE), PIECE)
                    r.scores[to, i * BLOCK : (i + 1) * BLOCK] = value[i * PIECE : (i + 1) * PIECE]
            elif name in ("f0", "f1", "f2"):
                top = int(name[1]) * PIECE
                columns = pl.ds(pl.multiple_of(768 + part * BLOCK, BLOCK), BLOCK)
                r.scores[top : top + PIECE, columns] = value
            elif name == "uc":
                rows = pl.ds(pl.multiple_of(384 + y * PIECE // 2, 16), PIECE // 2)
                r.scores[rows, pl.ds(pl.multiple_of((1 + x) * BLOCK, BLOCK), BLOCK)] = value
            else:
                low = name == "ub"
                top = jnp.where(part == 3, 384, 288) + low * PIECE // 2
                left = jnp.where(part == 3, 0, 768 + part * BLOCK)
                rows = pl.ds(pl.multiple_of(top, 16), PIECE // 2)
                r.scores[rows, pl.ds(pl.multiple_of(left, BLOCK), BLOCK)] = value
        if plane:
            self.write(r.scores.at[:384, :768], r.grad_proj)
        elif name in ("f0", "f1", "f2"):
            k = int(name[1])
            src = r.scores.at[k * PIECE : (k + 1) * PIECE, 768 : 768 + 4 * BLOCK]
            self.write(src, r.grad_fc.at[:, 4 * k * BLOCK : 4 * (k + 1) * BLOCK])
        elif name == "ub":
            self.write(r.scores.at[288 : 288 + PIECE, 768 : 768 + 768], r.grad_o)

    def write(self, src, dst):
        copy = pltpu.make_async_copy(src, dst, self.r.out_sem.at[len(self.out_copies)])
        copy.start()
        self.out_copies.append(copy)

    def close(self):
        for copy in self.out_copies:
            copy.wait()
        for make, *args in self.sent:
            make(*args).wait_send()
        for z in range(4):

            @pl.when(self.z != z)
            def _():
                self.plane_line(CHUNKS[f"p{z}"]).wait_send()


TWO_STEPS = ("p", "f0", "f1", "f2")


def make_inbox():
    inbox, rows = {}, SLOTS * 16 * PIECE

    def add(name, count, start=None):
        nonlocal rows
        if start is None:
            start = rows
            rows += count
        inbox[name] = (start, count, len(inbox))

    for order, chunk in enumerate(CHUNKS.values()):
        name, piece = chunk.name, chunk.height
        add("pair " + name, chunk.rows // 2, order % SLOTS * 16 * PIECE)
        if chunk.kind == "plane":
            add("half " + name, 2 * chunk.count * piece)
            add("quarter " + name, chunk.count * piece)
            add("line " + name, chunk.count * piece, 0)
            continue
        if chunk.kind != "whole":
            count = 1 if chunk.kind == "line" else 4
            add("half " + name, 2 * count * piece)
            add("quarter " + name, count * piece)
        for i in (1, 2, 3):
            add(f"line{i} " + name, (4 if chunk.kind == "line" else 1) * piece)
        for i in range(4):
            add(f"share{i} " + name, piece)
    for i in (1, 2, 3):
        add(f"line{i} p", 3 * PIECE)
    for i in range(4):
        add(f"share{i} p", 3 * PIECE)
    return inbox, rows


INBOX, INBOX_ROWS = make_inbox()


def kv_copy(r, source, batch, parts, distance):
    peer = (lax.rem(source + distance, parts), batch)
    return remote(r.kv.at[source], r.kv.at[source], r.kv_sem.at[0, distance], r.kv_sem.at[1, distance], peer)


def dkv_copy(r, mine, batch, parts, distance):
    peer = (lax.rem(mine - distance + parts, parts), batch)
    return remote(
        r.dkv_out.at[distance], r.dkv_in.at[distance], r.dkv_sem.at[0, distance], r.dkv_sem.at[1, distance], peer
    )


def hand_out_kernel(count, *refs):
    sources, targets, held, sem = refs[:count], refs[count : 2 * count], refs[2 * count : -1], refs[-1]
    large = [i for i in range(count) if sources[i].ndim > 1]
    copies = []
    for j, i in enumerate(large):
        half = sources[i].shape[0] // 2
        for k in range(2):
            rows, at = pl.ds(k * half, half), 2 * j + k
            copies.append(
                (
                    pltpu.make_async_copy(sources[i].at[rows], held[j].at[rows], sem.at[0, at]),
                    pltpu.make_async_copy(held[j].at[rows], targets[i].at[rows], sem.at[1, at]),
                )
            )
    for here, _ in copies:
        here.start()
    for source, target in zip(sources, targets):
        if source.ndim == 1:
            target[...] = source[...]
    for here, there in copies:
        here.wait()
        there.start()
    for _, there in copies:
        there.wait()


def hand_out(results, specs):
    large = [pltpu.VMEM(item.shape, item.dtype) for item in results if item.ndim > 1]
    return pl.pallas_call(
        functools.partial(hand_out_kernel, len(results)),
        out_shape=[jax.ShapeDtypeStruct(item.shape, item.dtype) for item in results],
        in_specs=specs,
        out_specs=specs,
        scratch_shapes=[*large, pltpu.SemaphoreType.DMA((2, 2 * len(large)))],
        name="hand_out",
    )(*results)


def per_device(inputs, doc_ids, w_qkv, b_qkv, w_o, w_fc, b_fc, w_proj, b_proj, gain_one, shift_one, gain_two, shift_two, cotangent):
    rows_here, span, width = inputs.shape
    assert rows_here == 1
    parts = lax.axis_size("seq")
    heads = width // HEAD
    hidden_units = w_fc.shape[1]
    merged = width + 2 * HEAD
    inside = parts == 4 and lax.axis_size("batch") == 8
    vmem = pl.BlockSpec(memory_space=pltpu.VMEM)
    anywhere = pl.BlockSpec(memory_space=pl.ANY)

    small = dict(docs=doc_ids, bq=b_qkv, bfc=b_fc, bp=b_proj, g1=gain_one, s1=shift_one, g2=gain_two, s2=shift_two)
    large = dict(x_h=inputs[0], cot_h=cotangent[0], wq_h=w_qkv, wo_h=w_o, wfc_h=w_fc, wp_h=w_proj)
    outs = dict(outputs=((span, width), BF16, anywhere), input_grads=((span, width), BF16, anywhere))
    if inside:
        outs |= dict(
            grad_qkv=((width // 8, merged), F32, anywhere),
            grad_bq=((merged // 8,), F32, vmem),
            grad_o=((width // 8, width), F32, anywhere),
            grad_fc=((width // 8, hidden_units), F32, anywhere),
            grad_bfc=((hidden_units // 8,), F32, vmem),
            grad_proj=((hidden_units // 8, width), F32, anywhere),
            grad_bp=((width // 8,), F32, vmem),
            grad_g1=((width // 8,), F32, vmem),
            grad_s1=((width // 8,), F32, vmem),
            grad_g2=((width // 8,), F32, vmem),
            grad_s2=((width // 8,), F32, vmem),
        )
    else:
        outs |= dict(grads_out=((GRAD_ROWS, BLOCK), BF16, anywhere), late_out=((hidden_units, 2 * BLOCK), BF16, anywhere))
    scratch = dict(
        x=pltpu.VMEM((span, width), BF16),
        cot=pltpu.VMEM((span, width), BF16),
        wq=pltpu.VMEM((width, merged), BF16),
        wo=pltpu.VMEM((width, width), BF16),
        wfc=pltpu.VMEM((width, hidden_units), BF16),
        wp=pltpu.VMEM((hidden_units, width), BF16),
        fi=pltpu.VMEM((span, width), BF16),
        si=pltpu.VMEM((span, width), BF16),
        fit=pltpu.VMEM((width, span), BF16),
        sit=pltpu.VMEM((width, span), BF16),
        cos=pltpu.VMEM((2, ROT // 2, span), F32),
        sin=pltpu.VMEM((2, ROT // 2, span), F32),
        kv=pltpu.VMEM((parts, span, LANES), BF16),
        q=pltpu.VMEM((heads + 2, span, LANES), BF16),
        qt=pltpu.VMEM((heads + 2, LANES, span), BF16),
        dot=pltpu.VMEM((width + 2 * HEAD, span), BF16),
        act=pltpu.VMEM((span, width), BF16),
        gh=pltpu.VMEM((span, width), BF16),
        result=pltpu.VMEM((span, width), F32),
        second=pltpu.VMEM((span, width), F32),
        sum_fc=pltpu.VMEM((8, hidden_units), F32),
        kx=pltpu.VMEM((parts, span, LANES), BF16),
        kxt=pltpu.VMEM((parts, LANES, span), BF16),
        vx=pltpu.VMEM((parts, span, LANES), BF16),
        vxt=pltpu.VMEM((parts, LANES, span), BF16),
        dk=pltpu.VMEM((parts, span, LANES), F32),
        dv=pltpu.VMEM((parts, span, LANES), F32),
        scores=pltpu.VMEM((span, parts * span), F32),
        ga=pltpu.VMEM((LANES, span), BF16),
        gat=pltpu.VMEM((span, LANES), BF16),
        attt=pltpu.VMEM((width + 2 * HEAD, span), BF16),
        gqt=pltpu.VMEM((width + 2 * HEAD, span), BF16),
        gkvt=pltpu.VMEM((2 * HEAD, span), BF16),
        dkv_out=pltpu.VMEM((parts, span, LANES), BF16),
        dkv_in=pltpu.VMEM((parts, span, LANES), BF16),
        grads=pltpu.VMEM((GRAD_ROWS, BLOCK), BF16),
        load_sem=pltpu.SemaphoreType.DMA((6,)),
        kv_sem=pltpu.SemaphoreType.DMA((2, parts)),
        dkv_sem=pltpu.SemaphoreType.DMA((2, parts)),
        lent_sem=pltpu.SemaphoreType.DMA((2, 2)),
        back_sem=pltpu.SemaphoreType.DMA((2, 2)),
    )
    if inside:
        scratch |= dict(
            inbox=pltpu.VMEM((INBOX_ROWS, BLOCK), BF16),
            sum_sem=pltpu.SemaphoreType.DMA((2, len(INBOX))),
            out_sem=pltpu.SemaphoreType.DMA((6,)),
            free_sem=pltpu.SemaphoreType.REGULAR((SLOTS,)),
        )
    names = [*small, *large, *outs, *scratch]
    results = pl.pallas_call(
        functools.partial(layer_kernel, names, parts, inside),
        out_shape=[jax.ShapeDtypeStruct(shape, dtype) for shape, dtype, _ in outs.values()],
        in_specs=[vmem] * len(small) + [anywhere] * len(large),
        out_specs=[spec for _, _, spec in outs.values()],
        scratch_shapes=list(scratch.values()),
        compiler_params=pltpu.CompilerParams(
            collective_id=0, has_side_effects=True, vmem_limit_bytes=63 * 2**20
        ),
        name="layer",
    )(*small.values(), *large.values())
    if inside:
        outputs, input_grads, *shards = hand_out(results, [spec for _, _, spec in outs.values()])
        return (outputs[None], input_grads[None], *shards)
    outputs, input_grads, *shards = results

    grads, late = shards
    planes = [CHUNKS[f"p{z}"].unfold(grads).transpose(0, 1, 2, 4, 3, 5).reshape(-1, width) for z in range(4)]
    proj = jnp.concatenate(planes)
    columns = [
        CHUNKS[name].unfold(grads).transpose(3, 0, 4, 1, 2, 5).reshape(width, 4 * BLOCK) for name in ("f0", "f1", "f2")
    ]
    fc = jnp.concatenate(columns, axis=1)
    halves = [CHUNKS[name].unfold(late[:, :BLOCK]).transpose(3, 0, 4, 1, 2, 5) for name in ("ua", "ub")]
    both = jnp.stack(halves, axis=2).reshape(width, 4 * BLOCK)
    o = both[:, :width]
    rest = CHUNKS["uc"].unfold(late[:, BLOCK:]).transpose(3, 0, 1, 4, 2, 5).reshape(width, 2 * BLOCK)
    last = CHUNKS["k"].unfold(late[:, BLOCK:]).reshape(2, 4, PIECE // 2, 2, LANES).transpose(1, 0, 3, 2, 4)
    qkv = jnp.concatenate([both[:, width:], rest, last.reshape(width, LANES)], axis=1)
    blocks = 8
    lines = CHUNKS["v"].unfold(late[:, BLOCK:]).transpose(1, 0, 2, 3).reshape(blocks, 16, BLOCK)[..., :LANES]
    vectors = [lines[:, 0, : merged // blocks], lines[:, 1:4]] + [lines[:, i, : width // blocks] for i in range(4, 9)]
    vectors = [vector.reshape(-1) for vector in vectors]
    every = [qkv, vectors[0], o, fc, vectors[1], proj, *vectors[2:]]
    shards = [lax.psum_scatter(item, "batch", scatter_dimension=0, tiled=True) for item in every]
    shards = [lax.psum(item, "seq").astype(F32) for item in shards]
    return (outputs[None], input_grads[None], *shards)


def solution(mesh):
    whole, part = P(), P("batch", "seq", None)
    in_specs = (part, P("batch", None), *[whole] * 11, part)
    matrix, vector = P("batch", None), P("batch")
    out_specs = (part, part, matrix, vector, matrix, matrix, vector, matrix, *[vector] * 5)
    return jax.shard_map(per_device, mesh=mesh, in_specs=in_specs, out_specs=out_specs, check_vma=False)
```
